32 devices in a mesh: dp: 4 (over z), ctx: 8 (over y, x, core).
Axes of the slice: x: 2, y: 2, z: 4, core: 2. Of those that a mesh axis runs over, the one named last changes fastest.
Arguments:
- tokens: bfloat16 [8, 512, 2048], P('dp', 'ctx'), may hold values from -6 to 6
- block_order: int32 [8, 16], P('dp'), may hold values from 0 to 15, each once within a row
- ln_gain: bfloat16 [2048], P(('dp', 'ctx')), may hold values from 0.5 to 1.5
- ln_bias: bfloat16 [2048], P(('dp', 'ctx')), may hold values from -1.75 to 1.75
- w_qkv: bfloat16 [2048, 6144], P(('dp', 'ctx')), may hold values from -0.125 to 0.125
- b_qkv: bfloat16 [6144], P(('dp', 'ctx')), may hold values from -1.75 to 1.75
- w_dense: bfloat16 [2048, 2048], P(('dp', 'ctx')), may hold values from -1 to 1
- b_dense: bfloat16 [2048], P(('dp', 'ctx')), may hold values from -1.75 to 1.75
- w_fc1: bfloat16 [2048, 8192], P(('dp', 'ctx')), may hold values from -0.125 to 0.125
- b_fc1: bfloat16 [8192], P(('dp', 'ctx')), may hold values from -3 to 3
- w_fc2: bfloat16 [8192, 2048], P(('dp', 'ctx')), may hold values from -0.0625 to 0.0625
- b_fc2: bfloat16 [2048], P(('dp', 'ctx')), may hold values from -1.75 to 1.75
- cotangent: bfloat16 [8, 512, 2048], P('dp', 'ctx'), may hold values from -6 to 6
Outputs:
- output: bfloat16 [8, 512, 2048], P('dp', 'ctx')
- token_grad: bfloat16 [8, 512, 2048], P('dp', 'ctx')
- grad_ln_gain: float32 [2048], P(('dp', 'ctx'))
- grad_ln_bias: float32 [2048], P(('dp', 'ctx'))
- grad_w_qkv: float32 [2048, 6144], P(('dp', 'ctx'))
- grad_b_qkv: float32 [6144], P(('dp', 'ctx'))
- grad_w_dense: float32 [2048, 2048], P(('dp', 'ctx'))
- grad_b_dense: float32 [2048], P(('dp', 'ctx'))
- grad_w_fc1: float32 [2048, 8192], P(('dp', 'ctx'))
- grad_b_fc1: float32 [8192], P(('dp', 'ctx'))
- grad_w_fc2: float32 [8192, 2048], P(('dp', 'ctx'))
- grad_b_fc2: float32 [2048], P(('dp', 'ctx'))
The draws below stay inside these ranges and needn't reach their ends.
Inputs may be any that keep to these rules, and one draw needn't show every extreme that they name: `block_order`: each row names every block of its sequence once.
All inputs are finite; a program needn't handle non-finite values.
Results may differ from the reference program's by a relative error of at most 0.014.
Values may be sent and summed in bfloat16 or wider, within the bound.
No kernel may reach another device: no remote copies, remote signals or barrier semaphores. Data moves between devices by JAX's collectives and lax.ppermute only.
A program may use at most 704 MiB of HBM per device.

```python
import jax
import jax.numpy as jnp
from jax import lax

D = 2048
HEAD = 64
ROT = 32
ROPE_BASE = 10000
FF = 8192
BLOCK = 32
BLOCKS = 16
LENGTH = 512
SEQS = 8


def steps_of(own_key, shape, split, low, high):
    def one(axis_at, parts):
        heights = jax.random.uniform(jax.random.fold_in(jax.random.fold_in(own_key, 6), axis_at), (parts,), jnp.float32, low / len(split), high / len(split))
        return jnp.repeat(jnp.exp(heights), shape[axis_at] // parts).reshape((-1,) + (1,) * (len(shape) - axis_at - 1))

    gain = one(*split[0])
    for cut in split[1:]:
        gain = gain * one(*cut)
    return gain


def bell_draw(stream_key, dims, scale, reach, shards=(), held_as=jnp.bfloat16):
    values = jax.random.normal(stream_key, dims, jnp.float32) * scale
    if len(shards) > 0:
        values = steps_of(stream_key, dims, shards, -0.22, 0.18) * values
    return jnp.clip(values, min=-reach, max=reach).astype(held_as)


def setup_inputs(seed: int = 0) -> dict:
    arg_keys = jax.random.split(jax.random.key(seed), 14)
    tokens = bell_draw(arg_keys[0], (SEQS, LENGTH, D), 1.0, 6.0, ((0, 4), (1, 8)))
    block_order = jax.vmap(lambda own: jax.random.permutation(own, BLOCKS))(jax.random.split(arg_keys[1], SEQS)).reshape((SEQS, BLOCKS)).astype(jnp.int32)
    ln_gain = jnp.clip(1.0 + 0.1 * jax.random.normal(arg_keys[2], (D,), jnp.float32), 0.5, 1.5).astype(jnp.bfloat16)
    ln_bias = bell_draw(arg_keys[3], (D,), 0.3, 1.75, ((0, 32),))
    w_qkv = bell_draw(arg_keys[4], (D, 3 * D), D ** -0.5, 0.125, ((0, 32),))
    b_qkv = bell_draw(arg_keys[5], (3 * D,), 0.3, 1.75, ((0, 32),))
    w_dense = bell_draw(arg_keys[6], (D, D), (max(1, 8 * D // LENGTH)) ** -0.5, 1.0, ((0, 32),))
    b_dense = bell_draw(arg_keys[7], (D,), 0.3, 1.75, ((0, 32),))
    w_fc1 = bell_draw(arg_keys[8], (D, FF), D ** -0.5, 0.125, ((0, 32),))
    b_fc1 = bell_draw(arg_keys[9], (FF,), 0.5, 3.0, ((0, 32),))
    w_fc2 = bell_draw(arg_keys[10], (FF, D), FF ** -0.5, 0.0625, ((0, 32),))
    b_fc2 = bell_draw(arg_keys[11], (D,), 0.3, 1.75, ((0, 32),))
    cotangent = bell_draw(arg_keys[12], (SEQS, LENGTH, D), 1.0, 6.0, ((0, 4), (1, 8)))
    return {"tokens": tokens, "block_order": block_order, "ln_gain": ln_gain, "ln_bias": ln_bias, "w_qkv": w_qkv, "b_qkv": b_qkv, "w_dense": w_dense, "b_dense": b_dense, "w_fc1": w_fc1, "b_fc1": b_fc1, "w_fc2": w_fc2, "b_fc2": b_fc2, "cotangent": cotangent}


norm_eps = 1e-05

@jax.custom_vjp
def low(v):
    return lax.optimization_barrier(v.astype(jnp.bfloat16)).astype(jnp.float32)

@jax.custom_vjp
def low_back(v):
    return v

def low_keep(v):
    return (low(v), None)

def low_pass(kept, grad):
    return (grad,)

def back_keep(v):
    return (v, None)

def back_low(kept, grad):
    return (low(grad),)
low.defvjp(low_keep, low_pass)
low_back.defvjp(back_keep, back_low)

def matmul(left, right):
    return jnp.dot(left, right, precision=lax.Precision.HIGHEST, preferred_element_type=jnp.float32)

def layer_norm(inputs, gain_vec, shift_vec):
    centre = inputs - lax.optimization_barrier(jnp.mean(inputs, -1, keepdims=True))
    spread = lax.optimization_barrier(jnp.mean(centre * centre, -1, keepdims=True))
    return centre * lax.rsqrt(spread + norm_eps) * gain_vec + shift_vec

def rotate(field, token_place, turn_sign):
    half_rot = ROT // 2
    freqs = jnp.asarray(ROPE_BASE, jnp.float32) ** (-(jnp.arange(half_rot, dtype=jnp.float32) * (2.0 / ROT)))
    angles = token_place.astype(jnp.float32)[..., None] * freqs
    cosine = jnp.cos(angles)[..., None, :]
    sine = turn_sign * jnp.sin(angles)[..., None, :]
    first = field[..., :half_rot]
    second = field[..., half_rot:ROT]
    return jnp.concatenate([first * cosine - second * sine, second * cosine + first * sine, field[..., ROT:]], -1)

def layer(inputs, token_place, params):
    gain_vec, shift_vec, wqkv, bqkv, wdense, bdense, wup, bup, wdown, bdown = params
    seq_len, model_width = inputs.shape
    head_count = model_width // HEAD
    score_scale = HEAD ** (-0.5)
    normed = low(layer_norm(inputs, gain_vec, shift_vec))
    qkv_proj = low_back(matmul(normed, wqkv) + bqkv)
    query = low(rotate(qkv_proj[:, :model_width].reshape(seq_len, head_count, HEAD), token_place, 1.0))
    key_rot = low(rotate(qkv_proj[:, model_width:2 * model_width].reshape(seq_len, head_count, HEAD), token_place, 1.0))
    value = low(qkv_proj[:, 2 * model_width:].reshape(seq_len, head_count, HEAD))
    query_len = min(512, seq_len)
    query_blocks = query.reshape(seq_len // query_len, query_len, head_count, HEAD)
    place_blocks = token_place.reshape(seq_len // query_len, query_len)

    def attend(items):
        query_blk, place_blk = items
        scores = low_back(jnp.einsum('qhe,khe->hqk', query_blk, key_rot, precision=lax.Precision.HIGHEST, preferred_element_type=jnp.float32) * score_scale)
        allowed = token_place[None, None, :] <= place_blk[None, :, None]
        scores = jnp.where(allowed, scores, -1e+30)
        probability = low(jax.nn.softmax(scores, axis=-1))
        mixed = jnp.einsum('hqk,khe->qhe', probability, value, precision=lax.Precision.HIGHEST, preferred_element_type=jnp.float32)
        return mixed.reshape(query_len, model_width)
    attention = lax.map(jax.checkpoint(attend), (query_blocks, place_blocks)).reshape(seq_len, model_width)
    attention = low(low_back(attention))
    up_proj = low_back(matmul(normed, wup) + bup)
    hidden = low(jax.nn.gelu(up_proj, approximate=True))
    return inputs + (matmul(attention, wdense) + bdense) + (matmul(hidden, wdown) + bdown)

def reference(tokens, block_order, ln_gain, ln_bias, w_qkv, b_qkv, w_dense, b_dense, w_fc1, b_fc1, w_fc2, b_fc2, cotangent):
    params = tuple((item.astype(jnp.float32) for item in (ln_gain, ln_bias, w_qkv, b_qkv, w_dense, b_dense, w_fc1, b_fc1, w_fc2, b_fc2)))
    offsets = jnp.arange(BLOCK, dtype=jnp.int32)

    def one_sequence(summed, item):
        inputs, order_row, grad_row = item
        token_place = (order_row.astype(jnp.int32)[:, None] * BLOCK + offsets[None, :]).reshape(-1).astype(jnp.int32)
        result, backward = jax.vjp(lambda xin, pin: layer(xin, token_place, pin), inputs, params)
        grad_in, grad_params = backward(grad_row)
        summed = jax.tree.map(lambda left, right: left + right, summed, grad_params)
        return (summed, (result.astype(jnp.bfloat16), grad_in.astype(jnp.bfloat16)))
    start_grads = tuple((jnp.zeros_like(item) for item in params))
    grads, (outputs, token_grads) = lax.scan(one_sequence, start_grads, (tokens.astype(jnp.float32), block_order, cotangent.astype(jnp.float32)))
    return (outputs, token_grads, grads[0], grads[1], grads[2], grads[3], grads[4], grads[5], grads[6], grads[7], grads[8], grads[9])
```

```python
from functools import partial

import jax
import jax.numpy as jnp
from jax import lax
from jax.experimental import pallas as pl
from jax.experimental.pallas import tpu as pltpu
from jax.sharding import PartitionSpec as P

HEAD = 64
ROT = 32
ROPE_BASE = 10000
NORM_EPS = 1e-05
BOTH = ("dp", "ctx")
LOW = jnp.bfloat16
WIDE = jnp.float32
GELU_SCALE = 0.7978845608028654
GELU_CUBIC = 0.044715


def place(axis, index):
    return lax.dynamic_index_in_dim(axis, index, 0, keepdims=False)


class Grid:
    def __init__(self):
        self.z_count = lax.axis_size("dp")
        self.ctx_count = lax.axis_size("ctx")
        self.y_count = self.ctx_count // 4
        ctx = lax.axis_index("ctx")
        self.z = lax.axis_index("dp")
        self.y = ctx // 4
        self.x = (ctx // 2) % 2
        self.c = ctx % 2
        self.rank = self.z * self.y_count + self.y
        self.rank_count = self.z_count * self.y_count
        self.parity = (self.z + self.x) % 2

    def send(self, value, z=0, y=0, x=0, c=0):
        pairs = []
        for z_at in range(self.z_count):
            for y_at in range(self.y_count):
                for x_at in range(2):
                    for c_at in range(2):
                        z_to = (z_at + z) % self.z_count
                        y_to = (y_at + y) % self.y_count
                        source = ((z_at * self.y_count + y_at) * 2 + x_at) * 2 + c_at
                        target = ((z_to * self.y_count + y_to) * 2 + (x_at ^ x)) * 2 + (c_at ^ c)
                        pairs.append((source, target))
        return lax.ppermute(value, BOTH, pairs)


def gather_tokens(grid, value):
    own = place(value, grid.c)
    other = grid.send(place(value, 1 - grid.c), c=1)
    first = jnp.concatenate([own, other], 0)
    pieces = {0: first}
    for k in range(1, grid.z_count // 2 + 1):
        pieces[k] = grid.send(pieces[k - 1], z=1)
    for k in range(grid.z_count - 1, grid.z_count // 2, -1):
        pieces[k] = grid.send(pieces[(k + 1) % grid.z_count], z=-1)
    sequences = []
    for i in range(grid.z_count // 2):
        even, odd = pieces[2 * i], pieces[2 * i + 1]
        keep = jnp.where(grid.parity == 0, even, odd)
        away = jnp.where(grid.parity == 0, odd, even)
        parts = [keep, grid.send(away, x=1)]
        here = list(parts)
        for _ in range(1, grid.y_count):
            here = [grid.send(part, y=1) for part in here]
            parts = parts + here
        sequences.append(jnp.concatenate(parts, 0))
    return sequences


def scatter_tokens(grid, sequences):
    pieces = {}
    for i, whole in enumerate(sequences):
        halves = whole.reshape(grid.y_count, 2, -1, whole.shape[-1])
        summed = [halves[0, 0].astype(WIDE), halves[0, 1].astype(WIDE)]
        arrived = None
        for dy in range(grid.y_count - 1, 0, -1):
            step = [halves[dy, dx].astype(WIDE) for dx in range(2)]
            if arrived is not None:
                step = [a + b.astype(WIDE) for a, b in zip(step, arrived)]
            arrived = [grid.send(part.astype(LOW), y=-1) for part in step]
        summed = [a + b.astype(WIDE) for a, b in zip(summed, arrived)]
        kept = summed[0].astype(LOW)
        swapped = grid.send(summed[1].astype(LOW), x=1)
        pieces[2 * i] = jnp.where(grid.parity == 0, kept, swapped)
        pieces[2 * i + 1] = jnp.where(grid.parity == 0, swapped, kept)
    total = pieces[0].astype(WIDE)
    arrived = None
    for k in range(grid.z_count // 2, 0, -1):
        step = pieces[k] if arrived is None else (pieces[k].astype(WIDE) + arrived.astype(WIDE)).astype(LOW)
        arrived = grid.send(step, z=-1)
    total = total + arrived.astype(WIDE)
    arrived = None
    for k in range(grid.z_count // 2 + 1, grid.z_count):
        step = pieces[k] if arrived is None else (pieces[k].astype(WIDE) + arrived.astype(WIDE)).astype(LOW)
        arrived = grid.send(step, z=1)
    if arrived is not None:
        total = total + arrived.astype(WIDE)
    span = total.shape[0] // 2
    own = total[:span]
    other = grid.send(total[span:].astype(LOW), c=1).astype(WIDE)
    return jnp.where(grid.c == 0, jnp.stack([own, other]), jnp.stack([other, own]))


def gather_columns(grid, weight, parts):
    rows = weight.shape[0]
    zn, yn = grid.z_count, grid.y_count
    width = weight.shape[1] // (parts * zn * yn)
    cut = weight.reshape(rows, parts, zn, yn, width)
    by_y = jnp.zeros((yn, rows, parts, zn, width), weight.dtype)
    for dy in range(yn):
        chunk = lax.dynamic_index_in_dim(cut, (grid.y + dy) % yn, 3, keepdims=False)
        got = grid.send(chunk, y=dy) if dy else chunk
        by_y = lax.dynamic_update_index_in_dim(by_y, got, (grid.y - dy) % yn, 0)
    by_z = jnp.zeros((zn, yn, rows, parts, width), weight.dtype)
    for dz in range(zn):
        chunk = lax.dynamic_index_in_dim(by_y, (grid.z + dz) % zn, 3, keepdims=False)
        got = grid.send(chunk, z=dz) if dz else chunk
        by_z = lax.dynamic_update_index_in_dim(by_z, got, (grid.z - dz) % zn, 0)
    by_z = by_z.reshape(zn * yn, rows, parts * width)
    return gather_pairs(grid, by_z)


def gather_pairs(grid, value):
    other = grid.send(value, x=1)
    pair = jnp.where(
        grid.x == 0, jnp.stack([value, other], 1), jnp.stack([other, value], 1)
    )
    other = grid.send(pair, c=1)
    quad = jnp.where(
        grid.c == 0, jnp.stack([pair, other], 2), jnp.stack([other, pair], 2)
    )
    return quad.reshape(-1, value.shape[-1])


def scatter_pairs(grid, value):
    width = value.shape[-1]
    cut = value.reshape(-1, 2, 2, value.shape[0] // (4 * grid.group_ranks), width)
    away = lax.dynamic_index_in_dim(cut, 1 - grid.c, 2, keepdims=False).astype(LOW)
    kept = lax.dynamic_index_in_dim(cut, grid.c, 2, keepdims=False)
    cut = kept + grid.send(away, c=1).astype(WIDE)
    away = lax.dynamic_index_in_dim(cut, 1 - grid.x, 1, keepdims=False).astype(LOW)
    kept = lax.dynamic_index_in_dim(cut, grid.x, 1, keepdims=False)
    return kept + grid.send(away, x=1).astype(WIDE)


def scatter_columns(grid, value, parts):
    zn, yn = grid.z_count, grid.y_count
    grid.group_ranks = zn * yn
    summed = scatter_pairs(grid, value).astype(LOW)
    rows, width = summed.shape[1], summed.shape[2] // parts
    cut = summed.reshape(zn, yn, rows, parts, width)
    by_z = jnp.zeros((yn, rows, parts, zn, width), LOW)
    for dz in range(zn):
        chunk = place(cut, (grid.z + dz) % zn)
        got = grid.send(chunk, z=dz) if dz else chunk
        by_z = lax.dynamic_update_index_in_dim(by_z, got, (grid.z - dz) % zn, 3)
    by_y = jnp.zeros((rows, parts, zn, yn, width), LOW)
    for dy in range(yn):
        chunk = place(by_z, (grid.y + dy) % yn)
        got = grid.send(chunk, y=dy) if dy else chunk
        by_y = lax.dynamic_update_index_in_dim(by_y, got, (grid.y - dy) % yn, 3)
    return by_y.reshape(rows, -1).astype(WIDE)


def contract_last(left, right):
    return lax.dot_general(
        left, right, (((1,), (1,)), ((), ())), preferred_element_type=WIDE
    )


def contract_first(left, right):
    return lax.dot_general(
        left, right, (((0,), (0,)), ((), ())), preferred_element_type=WIDE
    )


def layer_norm(inputs, gain_vec, shift_vec):
    centre = inputs - jnp.mean(inputs, -1, keepdims=True)
    spread = jnp.mean(centre * centre, -1, keepdims=True)
    return centre * lax.rsqrt(spread + NORM_EPS) * gain_vec + shift_vec


def swap_halves(field):
    width = field.shape[-1]
    half = ROT // 2
    if width % 128 == 0:
        after = pltpu.roll(field, width - half, 1)
        before = pltpu.roll(field, half, 1)
    else:
        after = jnp.concatenate([field[:, half:], field[:, :half]], 1)
        before = jnp.concatenate([field[:, width - half :], field[:, : width - half]], 1)
    lane = lax.broadcasted_iota(jnp.int32, field.shape, 1) % HEAD
    return jnp.where(lane < half, after, before)


def attention_body(
    query_ref, key_ref, value_ref, grad_ref, cos_ref, sin_ref, column_ref, row_ref,
    mixed_ref, grad_query_ref, grad_key_ref, grad_value_ref,
):
    cosine, sine = cos_ref[...], sin_ref[...]
    scale = HEAD**-0.5
    query = query_ref[...]
    query_all = (query * cosine + swap_halves(query) * sine).astype(LOW)
    key = key_ref[...]
    key_all = (key * cosine + swap_halves(key) * sine).astype(LOW)
    value_all = value_ref[...].astype(LOW)
    grad_all = grad_ref[...]
    allowed = row_ref[...] <= column_ref[...]
    outs = []
    for at in range(query_all.shape[1] // HEAD):
        part = slice(at * HEAD, (at + 1) * HEAD)
        query_low, key_low = query_all[:, part], key_all[:, part]
        value_low, grad_low = value_all[:, part], grad_all[:, part]
        scores = jnp.where(allowed, contract_last(query_low, key_low) * scale, -1e30)
        weights = jnp.exp(scores - jnp.max(scores, -1, keepdims=True))
        probability = weights / jnp.sum(weights, -1, keepdims=True)
        probability_low = probability.astype(LOW)
        mixed = jnp.dot(probability_low, value_low, preferred_element_type=WIDE)
        delta = jnp.sum(grad_low.astype(WIDE) * mixed, -1, keepdims=True)
        grad_probability = contract_last(grad_low, value_low)
        grad_scores = (probability * (grad_probability - delta)).astype(LOW)
        grad_value = contract_first(probability_low, grad_low)
        grad_query = jnp.dot(grad_scores, key_low, preferred_element_type=WIDE) * scale
        grad_key = contract_first(grad_scores, query_low) * scale
        outs.append((mixed, grad_query, grad_key, grad_value))
    mixed, grad_query, grad_key, grad_value = [jnp.concatenate(item, 1) for item in zip(*outs)]
    mixed_ref[...] = mixed.astype(LOW)
    grad_query_ref[...] = (grad_query * cosine - swap_halves(grad_query) * sine).astype(LOW)
    grad_key_ref[...] = (grad_key * cosine - swap_halves(grad_key) * sine).astype(LOW)
    grad_value_ref[...] = grad_value.astype(LOW)


def attend(qkv, grad_attention, cosine, sine, places, length):
    tokens, width = grad_attention.shape
    lanes = min(128, width)
    block = (length, lanes)
    places = places.astype(WIDE)
    field = pl.BlockSpec(block, lambda s, h: (s, h))
    table = pl.BlockSpec(block, lambda s, h: (s, 0))
    third = lambda part: pl.BlockSpec((None, *block), lambda s, h: (part, s, h))
    low = jax.ShapeDtypeStruct((tokens, width), LOW)
    return pl.pallas_call(
        attention_body,
        grid=(tokens // length, width // lanes),
        in_specs=[
            third(0), third(1), third(2), field, table, table,
            pl.BlockSpec((length, 1), lambda s, h: (s, 0)),
            pl.BlockSpec((None, 1, length), lambda s, h: (s, 0, 0)),
        ],
        out_specs=[field] * 4,
        out_shape=[low] * 4,
        compiler_params=pltpu.CompilerParams(vmem_limit_bytes=48 * 1024 * 1024),
        cost_estimate=pl.CostEstimate(
            flops=12 * tokens * length * width, bytes_accessed=30 * tokens * width, transcendentals=tokens * length * width // HEAD
        ),
    )(
        qkv, qkv, qkv, grad_attention, cosine[:, :lanes], sine[:, :lanes],
        places[:, None], places.reshape(-1, 1, length),
    )


def rotary_tables(places):
    lane = jnp.arange(128, dtype=jnp.int32) % HEAD
    half = ROT // 2
    freqs = jnp.asarray(ROPE_BASE, WIDE) ** (-((lane % half).astype(WIDE) * (2.0 / ROT)))
    angles = places.astype(WIDE)[:, None] * freqs
    turned = (lane < ROT)[None, :]
    sign = jnp.where(lane < half, -1.0, 1.0)
    return jnp.where(turned, jnp.cos(angles), 1.0), jnp.where(turned, jnp.sin(angles) * sign, 0.0)


def on_device(
    tokens, block_order, ln_gain, ln_bias, w_qkv, b_qkv, w_dense, b_dense, w_fc1, b_fc1, w_fc2, b_fc2, cotangent,
):
    grid = Grid()
    seqs, span, model_width = tokens.shape
    device_count = grid.z_count * grid.ctx_count
    ranks = grid.rank_count
    length = span * grid.ctx_count
    block_len = span // 2
    group_seqs = grid.z_count // 2
    head_width = model_width // ranks

    vectors = (ln_gain, ln_bias, b_qkv, b_dense, b_fc1, b_fc2, block_order.astype(LOW).reshape(-1))
    sizes = [item.shape[0] for item in vectors]
    gathered = lax.all_gather(jnp.concatenate(vectors), BOTH, axis=0)
    cuts = [sum(sizes[:i]) for i in range(len(sizes) + 1)]
    gain_full, shift_full, bias_qkv, bias_dense, bias_up, bias_down = [
        gathered[:, cuts[i] : cuts[i + 1]].reshape(-1).astype(WIDE) for i in range(6)
    ]
    orders = gathered[:: grid.ctx_count, cuts[6] :].reshape(grid.z_count, 2, -1).astype(jnp.int32)

    ctx_from = jnp.stack(
        [
            (((grid.y - dy) % grid.y_count) * 2 + (grid.x ^ dx)) * 2 + (grid.c ^ dc)
            for dy in range(grid.y_count)
            for dx in range(2)
            for dc in range(2)
        ]
    )
    z_from = jnp.stack([(grid.z - 2 * i - grid.parity) % grid.z_count for i in range(group_seqs)])
    own_orders = lax.dynamic_index_in_dim(orders, grid.c, 1, keepdims=False)[z_from]
    slots = (ctx_from[:, None] * 2 + jnp.arange(2)).reshape(-1)
    places = (own_orders[:, slots][:, :, None] * block_len + jnp.arange(block_len)).reshape(-1)
    cosine, sine = rotary_tables(places)

    inputs = jnp.concatenate(gather_tokens(grid, tokens), 0)
    win_qkv = gather_columns(grid, w_qkv, 3)
    win_up = gather_columns(grid, w_fc1, 1)
    grad_out = jnp.concatenate(gather_tokens(grid, cotangent), 0)
    wout_dense = gather_pairs(grid, w_dense[None])
    wout_down = gather_pairs(grid, w_fc2[None])

    normed_low = layer_norm(inputs.astype(WIDE), gain_full, shift_full).astype(LOW)
    own_bias_qkv = lax.dynamic_index_in_dim(bias_qkv.reshape(3, ranks, -1), grid.rank, 1, keepdims=False)
    own_bias_up = place(bias_up.reshape(ranks, -1), grid.rank)
    qkv = jnp.stack(
        [
            jnp.dot(normed_low, win_qkv[:, i * head_width : (i + 1) * head_width], preferred_element_type=WIDE)
            + own_bias_qkv[i]
            for i in range(3)
        ]
    )
    grad_attention_low = contract_last(grad_out, wout_dense).astype(LOW)
    attention_low, grad_query_low, grad_key_low, grad_value_low = attend(
        qkv, grad_attention_low, cosine, sine, places, length
    )
    grad_qkv_low = jnp.concatenate([grad_query_low, grad_key_low, grad_value_low], 1)

    up = jnp.dot(normed_low, win_up, preferred_element_type=WIDE) + own_bias_up
    bent = jnp.tanh(GELU_SCALE * (up + GELU_CUBIC * up * up * up))
    hidden_low = (0.5 * up * (1.0 + bent)).astype(LOW)
    slope = 0.5 * (1.0 + bent) + 0.5 * up * (1.0 - bent * bent) * GELU_SCALE * (1.0 + 3.0 * GELU_CUBIC * up * up)
    grad_up_low = (contract_last(grad_out, wout_down) * slope).astype(LOW)

    projected = (
        jnp.dot(attention_low, wout_dense, preferred_element_type=WIDE)
        + jnp.dot(hidden_low, wout_down, preferred_element_type=WIDE)
    ).astype(LOW)
    projected = scatter_tokens(grid, [projected[i * length : (i + 1) * length] for i in range(group_seqs)])
    own_inputs = tokens.astype(WIDE)
    output = (own_inputs + projected + bias_dense + bias_down).astype(LOW)

    grad_normed = (contract_last(grad_qkv_low, win_qkv) + contract_last(grad_up_low, win_up)).astype(LOW)
    grad_normed = scatter_tokens(grid, [grad_normed[i * length : (i + 1) * length] for i in range(group_seqs)])

    centre = own_inputs - jnp.mean(own_inputs, -1, keepdims=True)
    turn = lax.rsqrt(jnp.mean(centre * centre, -1, keepdims=True) + NORM_EPS)
    unit = centre * turn
    scaled = grad_normed * gain_full
    own_grad = cotangent.astype(WIDE)
    token_grad = (
        own_grad
        + turn * (scaled - jnp.mean(scaled, -1, keepdims=True) - unit * jnp.mean(scaled * unit, -1, keepdims=True))
    ).astype(LOW)

    def laid(part, count):
        whole = jnp.zeros((count, ranks, part.shape[-1]), WIDE)
        whole = lax.dynamic_update_index_in_dim(whole, part, grid.rank, 1)
        return whole.reshape(device_count, -1)

    sums = jnp.concatenate(
        [
            jnp.sum(grad_normed * unit, (0, 1)).reshape(device_count, -1),
            jnp.sum(grad_normed, (0, 1)).reshape(device_count, -1),
            laid(jnp.sum(grad_qkv_low.astype(WIDE), 0).reshape(3, -1), 3),
            jnp.sum(own_grad, (0, 1)).reshape(device_count, -1),
            laid(jnp.sum(grad_up_low.astype(WIDE), 0).reshape(1, -1), 1),
        ],
        1,
    )
    sums = lax.psum_scatter(sums, BOTH, scatter_dimension=0, tiled=False)
    grad_gain, grad_shift = sums[: sizes[0]], sums[sizes[0] : 2 * sizes[0]]
    rest = sums[2 * sizes[0] :]
    grad_bias_qkv = rest[: sizes[2]]
    grad_bias_out = rest[sizes[2] : sizes[2] + sizes[3]]
    grad_bias_up = rest[sizes[2] + sizes[3] :]

    grid.group_ranks = 1
    grad_w_dense = scatter_pairs(grid, contract_first(attention_low, grad_out))[0]
    grad_w_down = scatter_pairs(grid, contract_first(hidden_low, grad_out))[0]
    grad_w_up = scatter_columns(grid, contract_first(normed_low, grad_up_low), 1)
    grad_w_qkv = scatter_columns(grid, contract_first(normed_low, grad_qkv_low), 3)
    return (
        output, token_grad, grad_gain, grad_shift, grad_w_qkv, grad_bias_qkv,
        grad_w_dense, grad_bias_out, grad_w_up, grad_bias_up, grad_w_down, grad_bias_out,
    )


def solution(mesh):
    rows = P(("dp", "ctx"), None)
    vector = P(("dp", "ctx"))
    spread = P("dp", "ctx", None)
    in_specs = (
        spread, P("dp", None), vector, vector, rows, vector, rows, vector, rows, vector, rows, vector, spread,
    )
    out_specs = (
        spread, spread, vector, vector, rows, vector, rows, vector, rows, vector, rows, vector,
    )
    return jax.shard_map(on_device, mesh=mesh, in_specs=in_specs, out_specs=out_specs, check_vma=False)
```

```python
from functools import partial

import jax
import jax.numpy as jnp
import numpy as np
from jax import lax
from jax.experimental import pallas as pl
from jax.experimental.pallas import tpu as pltpu
from jax.sharding import PartitionSpec as P

HEAD = 64
ROT = 32
ROPE_BASE = 10000
NORM_EPS = 1e-05
BOTH = ("dp", "ctx")
LOW = jnp.bfloat16
WIDE = jnp.float32
GELU_SCALE = 0.7978845608028654
GELU_CUBIC = 0.044715


COST_SCALE = 500_000_000


LIGHT = pl.CostEstimate(flops=1024, bytes_accessed=1024, transcendentals=1)


def cost(micros):
    return pl.CostEstimate(flops=int(micros * COST_SCALE), bytes_accessed=1024, transcendentals=1)
ROOM = pltpu.CompilerParams(vmem_limit_bytes=48 * 1024 * 1024)


def low_shape(*shape):
    return jax.ShapeDtypeStruct(shape, LOW)


def place(array, index):
    return lax.dynamic_index_in_dim(array, index, 0, keepdims=False)


def turn_page(token):
    def body(token_ref, copy_ref):
        copy_ref[...] = token_ref[...]

    return pl.pallas_call(
        body,
        out_shape=jax.ShapeDtypeStruct(token.shape, token.dtype),
        cost_estimate=pl.CostEstimate(flops=100_000_000_000, bytes_accessed=8192, transcendentals=0),
    )(token)


class Grid:
    def __init__(self):
        self.z_count = lax.axis_size("dp")
        self.ctx_count = lax.axis_size("ctx")
        self.y_count = self.ctx_count // 4
        ctx = lax.axis_index("ctx")
        self.z = lax.axis_index("dp")
        self.y = ctx // 4
        self.x = (ctx // 2) % 2
        self.c = ctx % 2
        self.where = jnp.stack([self.z, self.y, self.x, self.c]).astype(jnp.int32)
        self.rank = self.z * self.y_count + self.y
        self.rank_count = self.z_count * self.y_count
        self.parity = (self.z + self.x) % 2
        self.token = jnp.zeros((8, 128), WIDE)
        self.started, self.pages, self.ordered = False, True, True

    def steps(self):
        order = sorted(range(1, self.z_count), key=lambda k: (min(k, self.z_count - k), k))
        return order

    def after(self, value):
        self.page()
        return lax.optimization_barrier((value, self.token))[0] if self.ordered else value

    def hold(self, value):
        self.page()
        if self.ordered:
            value, self.token = lax.optimization_barrier((value, self.token))
        return value

    wait = hold

    def page(self):
        if self.started and self.pages:
            self.token = turn_page(self.token)
        self.started = False

    def start(self, value, z=0, y=0, x=0, c=0):
        pairs = []
        for z_at in range(self.z_count):
            for y_at in range(self.y_count):
                for x_at in range(2):
                    for c_at in range(2):
                        z_to = (z_at + z) % self.z_count
                        y_to = (y_at + y) % self.y_count
                        source = ((z_at * self.y_count + y_at) * 2 + x_at) * 2 + c_at
                        target = ((z_to * self.y_count + y_to) * 2 + (x_at ^ x)) * 2 + (c_at ^ c)
                        pairs.append((source, target))
        if self.ordered:
            value = lax.optimization_barrier((value, self.token))[0]
        self.started = True
        return lax.ppermute(value, BOTH, pairs)

    def local(self, body, inputs, outs):
        count = len(inputs)

        def whole_body(where_ref, *refs):
            body(*[where_ref[i] for i in range(4)], refs[:count], refs[count:])

        vmem = pl.BlockSpec(memory_space=pltpu.VMEM)
        return pl.pallas_call(
            whole_body,
            in_specs=[pl.BlockSpec(memory_space=pltpu.SMEM)] + [vmem] * count,
            out_specs=[vmem] * len(outs),
            out_shape=outs,
            compiler_params=ROOM,
            cost_estimate=cost(1.5),
        )(self.where, *inputs)

    def pile(self, *arrays):
        lengths = [item.shape[0] for item in arrays]
        starts = [sum(lengths[:i]) for i in range(len(lengths))]

        def body(z, y, x, c, ins, outs):
            for ref, start, length in zip(ins, starts, lengths):
                outs[0][start : start + length] = ref[...]

        return self.local(body, arrays, [low_shape(sum(lengths), *arrays[0].shape[1:])])[0]


def mover(grid, plan, inputs, outs):
    count = len(inputs)

    def copies_of(where_ref, refs, sems):
        at = [where_ref[i] for i in range(4)]
        listed = plan(*at, refs[:count], refs[count:])
        return [pltpu.make_async_copy(source, target, sems.at[i]) for i, (source, target) in enumerate(listed)]

    def body(where_ref, *refs):
        copies = copies_of(where_ref, refs[:-1], refs[-1])
        for copy in copies:
            copy.start()
        for copy in copies:
            copy.wait()

    most = 4 * max(4, grid.rank_count)
    return pl.pallas_call(
        body,
        in_specs=[pl.BlockSpec(memory_space=pltpu.SMEM)] + [pl.BlockSpec(memory_space=pltpu.VMEM)] * count,
        out_specs=[pl.BlockSpec(memory_space=pltpu.HBM)] * len(outs),
        out_shape=outs,
        scratch_shapes=[pltpu.SemaphoreType.DMA((most,))],
        compiler_params=pltpu.CompilerParams(vmem_limit_bytes=24 * 1024 * 1024),
        cost_estimate=LIGHT,
    )(grid.where, *inputs)


def part_cores(grid, tokens, cotangent):
    span, width = tokens.shape[1:]

    def body(z, y, x, c, ins, outs):
        for at, ref in enumerate(ins):
            outs[0][at * span : (at + 1) * span] = ref[1 - c]
            outs[1 + at][...] = ref[c]

    shapes = [low_shape(2 * span, width), low_shape(span, width), low_shape(span, width)]
    return grid.local(body, [tokens, cotangent], shapes)


def pair_of(grid, even, odd):
    def body(z, y, x, c, ins, outs):
        swap = lax.rem(z + x, 2)
        for first in range(2):

            @pl.when(swap == first)
            def _(first=first):
                outs[0][...] = ins[first][...]
                outs[1][...] = ins[1 - first][...]

    return grid.local(body, [even, odd], [low_shape(*even.shape)] * 2)


class Ring:
    def __init__(self, grid, first):
        self.grid, self.pieces, self.moving = grid, {0: first}, {}

    def begin(self, r):
        zn = self.grid.z_count
        self.moving[r] = self.grid.start(self.pieces[r - 1], z=1)
        if zn - r > zn // 2:
            self.moving[zn - r] = self.grid.start(self.pieces[(zn - r + 1) % zn], z=-1)

    def end(self):
        self.pieces.update(self.grid.wait(self.moving))
        self.moving = {}

    def finish(self):
        for r in range(3, self.grid.z_count // 2 + 1):
            self.begin(r)
            self.end()

    def pair(self, i):
        return pair_of(self.grid, self.pieces[2 * i], self.pieces[2 * i + 1])


class Spread:
    def __init__(self, grid, pair):
        self.grid = grid
        self.keep, away = pair
        self.moving = grid.start(away, x=1)

    def end_x(self):
        self.parts = [self.grid.pile(self.keep, self.grid.wait(self.moving))]

    def begin_y(self):
        self.moving = self.grid.start(self.parts[-1], y=1)

    def end_y(self):
        self.parts.append(self.grid.wait(self.moving))
        for _ in range(2, self.grid.y_count):
            self.begin_y()
            self.parts.append(self.grid.wait(self.moving))


def sum_low(left, right):
    return (left.astype(WIDE) + right.astype(WIDE)).astype(LOW)


class TokenSum:
    def __init__(self, grid, part, dy):
        self.grid = grid
        self.moving = grid.start(part, y=-1)
        self.left = dy - 1

    def more(self, part):
        arrived = self.grid.wait(self.moving)
        if self.left:
            self.moving = self.grid.start(sum_low(part, arrived), y=-1)
            self.left -= 1
            return
        span = arrived.shape[0] // 2

        def body(z, y, x, c, ins, outs):
            for at in range(2):
                here = slice(at * span, (at + 1) * span)
                outs[at][...] = sum_low(ins[0][here], ins[1][here])

        self.kept, self.away = self.grid.local(body, [part, arrived], [low_shape(span, arrived.shape[1])] * 2)

    def begin_x(self):
        self.moving = self.grid.start(self.away, x=1)

    def end_x(self):
        return pair_of(self.grid, self.kept, self.grid.wait(self.moving))


class RingSum:
    def __init__(self, grid):
        self.grid, self.pieces = grid, {}

    def add(self, left, right):
        def body(z, y, x, c, ins, outs):
            outs[0][...] = sum_low(ins[0][...], ins[1][...])

        return self.grid.local(body, [left, right], [low_shape(*left.shape)])[0]

    def begin_far(self):
        grid, zn, pieces = self.grid, self.grid.z_count, self.pieces
        down, up = zn // 2, zn // 2 + 1
        while down > 2:
            arrived = grid.wait(grid.start(pieces[down], z=-1))
            down -= 1
            pieces[down] = self.add(pieces[down], arrived)
        while up < zn - 1:
            arrived = grid.wait(grid.start(pieces[up], z=1))
            up += 1
            pieces[up] = self.add(pieces[up], arrived)
        self.moving = grid.start(pieces[2], z=-1), grid.start(pieces[zn - 1], z=1)

    def end_far(self):
        self.down, self.up = self.grid.wait(self.moving)

    def begin_near(self):
        self.moving = self.grid.start(self.add(self.pieces[1], self.down), z=-1)

    def end_near(self):
        near = self.grid.wait(self.moving)
        span = near.shape[0] // 2

        def body(z, y, x, c, ins, outs):
            total = ins[0][...].astype(WIDE) + ins[1][...].astype(WIDE) + ins[2][...].astype(WIDE)
            outs[0][...] = total[:span]
            outs[1][...] = total[span:].astype(LOW)

        shapes = [jax.ShapeDtypeStruct((span, near.shape[1]), WIDE), low_shape(span, near.shape[1])]
        self.own, away = self.grid.local(body, [self.pieces[0], self.up, near], shapes)
        self.moving = self.grid.start(away, c=1)

    def end(self):
        other = self.grid.wait(self.moving).astype(WIDE)
        first = self.grid.c == 0
        return jnp.stack([jnp.where(first, self.own, other), jnp.where(first, other, self.own)])


def cut_columns(grid, w_qkv, w_up):
    zn, yn, ranks = grid.z_count, grid.y_count, grid.rank_count
    rows, third, wide = w_qkv.shape[0], w_qkv.shape[1] // 3, w_up.shape[1]
    head, hidden = third // ranks, wide // ranks
    width = 3 * head + hidden
    outs = [low_shape(rows, width)] * zn + [low_shape(zn, rows, width)] * (yn - 1)

    def plan(z, y, x, c, ins, refs):
        copies = []
        for dy in range(yn):
            for k in range(zn):
                rank = lax.rem(z + k, zn) * yn + lax.rem(y + dy, yn)
                target = refs[k] if dy == 0 else refs[zn + dy - 1].at[k]
                for part in range(3):
                    start = pl.multiple_of(part * third + rank * head, 128)
                    copies.append((ins[0].at[:, pl.ds(start, head)], target.at[:, pl.ds(part * head, head)]))
                start = pl.multiple_of(rank * hidden, 128)
                copies.append((ins[1].at[:, pl.ds(start, hidden)], target.at[:, pl.ds(3 * head, hidden)]))
        return copies

    if head % 128 == 0:
        made = mover(grid, plan, [w_qkv, w_up], outs)
    else:
        heads = w_qkv.reshape(rows, 3, ranks, head)
        hiddens = w_up.reshape(rows, ranks, hidden)

        def block(k, dy):
            rank = (grid.z + k) % zn * yn + (grid.y + dy) % yn
            mine = lax.dynamic_index_in_dim(heads, rank, 2, keepdims=False).reshape(rows, 3 * head)
            return jnp.concatenate([mine, lax.dynamic_index_in_dim(hiddens, rank, 1, keepdims=False)], 1)

        made = [block(k, 0) for k in range(zn)] + [
            jnp.stack([block(k, dy) for k in range(zn)]) for dy in range(1, yn)
        ]
    return made[:zn], made[zn:]


def join_columns(grid, groups):
    zn, yn = grid.z_count, grid.y_count
    rows, width = groups[0][1].shape[-2:]
    flat = [item for group in groups for item in group[1:]]

    def body(where_ref, *refs):
        z, y, x, c = [where_ref[i] for i in range(4)]
        for at_group, group in enumerate(groups):
            for way in range(4):
                column, core = lax.rem(x + way % 2, 2), lax.rem(c + way // 2, 2)
                for at, k in enumerate(group[0]):
                    for dy in range(yn):
                        rank = lax.rem(z - k + zn, zn) * yn + lax.rem(y - dy + yn, yn)
                        start = pl.multiple_of(((rank * 2 + column) * 2 + core) * rows, rows)
                        refs[-1][pl.ds(start, rows)] = refs[2 * at_group + way // 2][way % 2, at, dy]

    vmem = pl.BlockSpec(memory_space=pltpu.VMEM)
    return pl.pallas_call(
        body,
        in_specs=[pl.BlockSpec(memory_space=pltpu.SMEM)] + [vmem] * len(flat),
        out_specs=vmem,
        out_shape=low_shape(zn * yn * 4 * rows, width),
        compiler_params=ROOM,
        cost_estimate=LIGHT,
    )(grid.where, *flat)


def join_out(grid, here, there, dense_rows):
    down_rows = here.shape[1] - dense_rows

    def plan(z, y, x, c, ins, outs):
        copies = []
        for way in range(4):
            source = ins[way // 2].at[way % 2]
            at = lax.rem(x + way % 2, 2) * 2 + lax.rem(c + way // 2, 2)
            first = pl.multiple_of(at * dense_rows, dense_rows)
            second = pl.multiple_of(4 * dense_rows + at * down_rows, dense_rows)
            copies.append((source.at[pl.ds(0, dense_rows)], outs[0].at[pl.ds(first, dense_rows)]))
            copies.append((source.at[pl.ds(dense_rows, down_rows)], outs[0].at[pl.ds(second, down_rows)]))
        return copies

    return mover(grid, plan, [here, there], [low_shape(4 * here.shape[1], here.shape[2])])[0]


def halves_in(grid, left, rights):
    tokens, ranks = left.shape[0], grid.rank_count
    widths = [item.shape[1] for item in rights]
    width = sum(widths)
    quad = left.shape[1] // ranks
    rows = quad // 4
    sums = [jax.ShapeDtypeStruct((1, size), WIDE) for size in widths]
    if quad % 128:
        made = contract_first(left, jnp.concatenate(rights, 1)).astype(LOW).reshape(ranks, 2, 2, rows, width)
        pick = lambda index: lax.dynamic_index_in_dim(made, index, 2, keepdims=False)
        return pick(grid.c), pick(1 - grid.c), [jnp.sum(item.astype(WIDE), 0, keepdims=True) for item in rights]
    starts = [sum(widths[:i]) for i in range(len(widths))]

    def body(where_ref, left_ref, *refs):
        core = where_ref[3]
        ins, (kept_ref, away_ref, *sum_refs), made_ref = refs[: len(rights)], refs[len(rights) : -1], refs[-1]
        for ref, start, size in zip(ins, starts, widths):
            made_ref[:, start : start + size] = contract_first(left_ref[...], ref[...]).astype(LOW)
        for column in range(2):
            for out_ref, at in ((kept_ref, core), (away_ref, 1 - core)):
                start = pl.multiple_of((2 * column + at) * rows, rows)
                out_ref[column] = made_ref[pl.ds(start, rows)]

        @pl.when(pl.program_id(0) == 0)
        def _():
            for ref, sum_ref in zip(ins, sum_refs):
                sum_ref[...] = jnp.sum(ref[...].astype(WIDE), 0, keepdims=True)

    half = pl.BlockSpec((None, 2, rows, width), lambda t: (t, 0, 0, 0))
    made = pl.pallas_call(
        body,
        grid=(ranks,),
        in_specs=[pl.BlockSpec(memory_space=pltpu.SMEM), pl.BlockSpec((tokens, quad), lambda t: (0, t))]
        + [whole(item) for item in rights],
        out_specs=[half, half] + [whole(item) for item in sums],
        out_shape=[low_shape(ranks, 2, rows, width)] * 2 + sums,
        scratch_shapes=[pltpu.VMEM((quad, width), LOW)],
        compiler_params=ROOM,
        cost_estimate=cost(8.0),
    )(grid.where, left, *rights)
    return made[0], made[1], made[2:]


def halves_out(grid, attention_low, hidden_low, grad_out):
    tokens, width = grad_out.shape
    dense, down = attention_low.shape[1], hidden_low.shape[1]
    rows = (dense // 4, down // 4)
    shape = low_shape(1, 2, sum(rows), width)
    if dense % 128 or down % 512:
        made = [
            contract_first(item, grad_out).astype(LOW).reshape(2, 2, -1, width) for item in (attention_low, hidden_low)
        ]
        pick = lambda index: jnp.concatenate(
            [lax.dynamic_index_in_dim(item, index, 1, keepdims=False) for item in made], 1
        )[None]
        return pick(grid.c), pick(1 - grid.c)

    def body(where_ref, dense_ref, down_ref, grad_ref, kept_ref, away_ref, made_ref):
        core, step = where_ref[3], pl.program_id(0)

        @pl.when(step == 0)
        def _():
            made_ref[...] = contract_first(dense_ref[...], grad_ref[...]).astype(LOW)
            for column in range(2):
                for out_ref, at in ((kept_ref, core), (away_ref, 1 - core)):
                    start = pl.multiple_of((2 * column + at) * rows[0], rows[0])
                    out_ref[0, column, : rows[0]] = made_ref[pl.ds(start, rows[0])]

        for quarter in range(4):
            for out_ref, at in ((kept_ref, core), (away_ref, 1 - core)):

                @pl.when((step == quarter + 1) & (at == quarter % 2))
                def _(out_ref=out_ref, quarter=quarter):
                    made = contract_first(down_ref[...], grad_ref[...]).astype(LOW)
                    out_ref[0, quarter // 2, rows[0] :] = made

    return pl.pallas_call(
        body,
        grid=(5,),
        in_specs=[
            pl.BlockSpec(memory_space=pltpu.SMEM),
            whole(attention_low),
            pl.BlockSpec((tokens, rows[1]), lambda t: (0, jnp.maximum(t - 1, 0))),
            whole(grad_out),
        ],
        out_specs=[whole(shape)] * 2,
        out_shape=[shape] * 2,
        scratch_shapes=[pltpu.VMEM((dense, width), LOW)],
        compiler_params=ROOM,
        cost_estimate=cost(11.0),
    )(grid.where, attention_low, hidden_low, grad_out)


def halve_columns(grid, kept, arrived):
    count, _, rows, width = kept.shape

    def body(where_ref, kept_ref, arrived_ref, here_ref, there_ref):
        column = where_ref[2]
        for ref, at in ((here_ref, column), (there_ref, 1 - column)):
            ref[...] = sum_low(kept_ref[at], arrived_ref[at])

    both = pl.BlockSpec((None, 2, rows, width), lambda t: (t, 0, 0, 0))
    one = pl.BlockSpec((None, rows, width), lambda t: (t, 0, 0))
    return pl.pallas_call(
        body,
        grid=(count,),
        in_specs=[pl.BlockSpec(memory_space=pltpu.SMEM), both, both],
        out_specs=[one, one],
        out_shape=[low_shape(count, rows, width)] * 2,
        compiler_params=ROOM,
        cost_estimate=cost(4.5),
    )(grid.where, kept, arrived)


class ColumnReturn:
    def __init__(self, grid, kept, arrived):
        zn, yn = grid.z_count, grid.y_count
        self.grid, self.shape = grid, kept.shape[1:]

        def body(z, y, x, c, ins, outs):
            for k in range(zn):
                for at in range(yn):
                    rank = lax.rem(z + k, zn) * yn + at
                    outs[k][at] = sum_low(ins[0][rank], ins[1][rank])

        cut = grid.local(body, [kept, arrived], [low_shape(yn, *self.shape)] * zn)
        self.by_z = {0: cut[0]}
        self.moving = {k: grid.start(cut[k], z=k) for k in grid.steps()}

    def end_z(self):
        grid, zn, yn = self.grid, self.grid.z_count, self.grid.y_count
        self.by_z.update(grid.wait(self.moving))

        def body(z, y, x, c, ins, outs):
            for dy in range(yn):
                for k in range(zn):
                    outs[dy][k] = ins[k][lax.rem(y + dy, yn)]

        self.cut = grid.local(body, [self.by_z[k] for k in range(zn)], [low_shape(zn, *self.shape)] * yn)

    def begin_y(self):
        self.moving = [self.grid.start(self.cut[dy], y=dy) for dy in range(1, self.grid.y_count)]

    def end(self):
        return [self.cut[0], *self.grid.wait(self.moving)]


def lay_columns(grid, found, parts):
    zn, yn, ranks = grid.z_count, grid.y_count, grid.rank_count
    rows, width = found[0].shape[1:]
    width = width // parts

    if width % 128 == 0:

        def body(z, y, x, c, ins, outs):
            for dy, ref in enumerate(ins):
                for k in range(zn):
                    rank = lax.rem(z - k + zn, zn) * yn + lax.rem(y - dy + yn, yn)
                    for part in range(parts):
                        start = pl.multiple_of((part * ranks + rank) * width, 128)
                        item = ref[k, :, part * width : (part + 1) * width]
                        outs[0][:, pl.ds(start, width)] = item.astype(WIDE)

        return grid.local(body, found, [jax.ShapeDtypeStruct((rows, parts * ranks * width), WIDE)])[0]
    laid = jnp.zeros((rows, parts, ranks, width), LOW)
    for dy, item in enumerate(found):
        for k in range(zn):
            rank = (grid.z - k) % zn * yn + (grid.y - dy) % yn
            laid = lax.dynamic_update_index_in_dim(laid, item[k].reshape(rows, parts, width), rank, 2)
    return laid.reshape(rows, -1).astype(WIDE)


class VectorGather:
    def __init__(self, grid, row):
        self.grid, self.block = grid, row[None]
        self.ways = [{"c": 1}]
        self.ways += [{"y": 1 << i} for i in range((grid.y_count - 1).bit_length())]
        self.ways += [{"z": 1 << i} for i in range((grid.z_count - 1).bit_length())]
        self.ways += [{"x": 1}]

    def begin(self):
        self.moving = self.grid.start(self.block, **self.ways.pop(0))

    def end(self):
        self.block = jnp.concatenate([self.block, self.grid.wait(self.moving)], 0)

    def step(self):
        self.begin()
        self.end()

    def result(self):
        grid, zn, yn = self.grid, self.grid.z_count, self.grid.y_count
        device = jnp.arange(zn * yn * 4, dtype=jnp.int32)
        far_z = (grid.z - device // (4 * yn)) % zn
        far_y = (grid.y - device // 4 % yn) % yn
        far_x = (grid.x - device // 2) % 2
        far_c = (grid.c - device) % 2
        return self.block[((far_x * zn + far_z) * yn + far_y) * 2 + far_c]


def unfold_vectors(grid, block, sizes, block_len, seqs):
    zn, yn = grid.z_count, grid.y_count
    ranks, devices = grid.rank_count, grid.rank_count * 4
    cuts = [sum(sizes[:i]) for i in range(len(sizes) + 1)]
    slots = sizes[6] // 2
    head, hidden = sizes[2] * devices // (3 * ranks), sizes[4] * devices // ranks
    third = sizes[2] * devices // 3
    rows = 8 * block_len
    length = yn * rows
    half = ROT // 2
    lane = np.arange(128) % HEAD
    freqs = np.float32(ROPE_BASE) ** (-((lane % half).astype(np.float32) * np.float32(2.0 / ROT)))
    turned = (lane < ROT).astype(np.float32)
    sign = np.where(lane < half, -1.0, 1.0).astype(np.float32) * turned
    marks = jnp.asarray(np.stack([freqs.astype(np.float32), turned, sign]))

    def body(where_ref, block_ref, mark_ref, *refs):
        z, y, x, c = [where_ref[i] for i in range(4)]
        gain_ref, shift_ref, in_ref, out_ref, cos_ref, sin_ref, column_ref, row_ref = refs[:8]
        wide_ref, qkv_ref, up_ref = refs[8:]
        wide_ref[...] = block_ref[...].astype(WIDE)

        def row_of(far_z, far_y, far_x, far_c):
            at = ((far_x * zn + far_z) * yn + far_y) * 2 + far_c
            return wide_ref[pl.ds(at, 1), :]

        for device in range(devices):
            row = row_of(
                lax.rem(z - device // (4 * yn) + zn, zn),
                lax.rem(y - device // 4 % yn + yn, yn),
                lax.rem(x + device // 2, 2),
                lax.rem(c + device, 2),
            )
            item = [row[:, cuts[i] : cuts[i + 1]] for i in range(6)]
            here = [pl.ds(device * sizes[i], sizes[i]) for i in range(6)]
            gain_ref[:, here[0]] = item[0]
            shift_ref[:, here[1]] = item[1]
            qkv_ref[:, here[2]] = item[2]
            out_ref[:, here[3]] = item[3] + item[5]
            up_ref[:, here[4]] = item[4]
        rank = z * yn + y
        for part in range(3):
            start = pl.multiple_of(part * third + rank * head, 128)
            in_ref[:, part * head : (part + 1) * head] = qkv_ref[:, pl.ds(start, head)]
        in_ref[:, 3 * head :] = up_ref[:, pl.ds(pl.multiple_of(rank * hidden, 128), hidden)]

        parity = lax.rem(z + x, 2)
        slot_at = lax.broadcasted_iota(jnp.int32, (1, slots), 1)
        tall = lax.broadcasted_iota(jnp.int32, (block_len, 128), 0).astype(WIDE)
        flat = lax.broadcasted_iota(jnp.int32, (1, block_len), 1).astype(WIDE)
        for i in range(seqs):
            row = row_of(2 * i + parity, 0, 0, 0)
            order = jnp.where(c == 0, row[:, cuts[6] : cuts[6] + slots], row[:, cuts[6] + slots : cuts[7]])
            for dy in range(yn):
                for near in range(4):
                    ctx = (lax.rem(y - dy + yn, yn) * 2 + lax.rem(x + near // 2, 2)) * 2 + lax.rem(c + near, 2)
                    for at in range(2):
                        value = jnp.sum(jnp.where(slot_at == 2 * ctx + at, order, 0.0), 1, keepdims=True) * block_len
                        place = value + tall
                        angle = place * mark_ref[0:1, :]
                        inside = (near * 2 + at) * block_len
                        here = pl.ds((dy * seqs + i) * rows + inside, block_len)
                        cos_ref[here, :] = jnp.where(mark_ref[1:2, :] > 0.0, jnp.cos(angle), 1.0)
                        sin_ref[here, :] = jnp.sin(angle) * mark_ref[2:3, :]
                        there = dy * rows + inside
                        column_ref[pl.ds(i * length + there, block_len), :] = place[:, :1]
                        row_ref[i, :, there : there + block_len] = value + flat

    wide = lambda *shape: jax.ShapeDtypeStruct(shape, WIDE)
    tokens = seqs * length
    vmem = pl.BlockSpec(memory_space=pltpu.VMEM)
    return pl.pallas_call(
        body,
        in_specs=[pl.BlockSpec(memory_space=pltpu.SMEM), vmem, vmem],
        out_specs=[vmem] * 8,
        out_shape=[
            wide(1, sizes[0] * devices), wide(1, sizes[1] * devices), wide(1, 3 * head + hidden),
            wide(1, sizes[3] * devices), wide(tokens, 128), wide(tokens, 128), wide(tokens, 1), wide(seqs, 1, length),
        ],
        scratch_shapes=[
            pltpu.VMEM(block.shape, WIDE), pltpu.VMEM((1, 3 * third), WIDE), pltpu.VMEM((1, hidden * ranks), WIDE),
        ],
        compiler_params=ROOM,
        cost_estimate=LIGHT,
    )(grid.where, block, marks)


class VectorSum:
    def __init__(self, grid, rows):
        zn, yn = grid.z_count, grid.y_count
        self.grid, self.cut = grid, rows.reshape(zn, yn, 2, 2, -1)
        self.ways = [("c", 3, grid.c, 2), ("x", 2, grid.x, 2), ("y", 1, grid.y, yn), ("z", 0, grid.z, zn)]

    def begin(self):
        way, axis, index, count = self.ways.pop(0)
        pick = lambda far: lax.dynamic_index_in_dim(self.cut, (index + far) % count, axis, keepdims=False)
        self.kept = pick(0)
        self.moving = [self.grid.start(pick(far), **{way: far}) for far in range(1, count)]

    def end(self):
        self.cut = sum(self.grid.wait(self.moving), self.kept)


def contract_last(left, right):
    return lax.dot_general(
        left, right, (((1,), (1,)), ((), ())), preferred_element_type=WIDE
    )


def contract_first(left, right):
    return lax.dot_general(
        left, right, (((0,), (0,)), ((), ())), preferred_element_type=WIDE
    )


def whole(array):
    return pl.BlockSpec(array.shape, lambda *at: (0,) * array.ndim)


def swap_halves(field):
    width = field.shape[-1]
    half = ROT // 2
    if width % 128 == 0:
        after = pltpu.roll(field, width - half, 1)
        before = pltpu.roll(field, half, 1)
    else:
        after = jnp.concatenate([field[:, half:], field[:, :half]], 1)
        before = jnp.concatenate([field[:, width - half :], field[:, : width - half]], 1)
    lane = lax.broadcasted_iota(jnp.int32, field.shape, 1) % HEAD
    return jnp.where(lane < half, after, before)


def turned_heads(query_ref, key_ref, value_ref, cos_ref, sin_ref):
    rows = (-1, cos_ref.shape[-1])
    cosine, sine = cos_ref[...].reshape(rows), sin_ref[...].reshape(rows)
    query = query_ref[...].reshape(rows)
    query_all = (query * cosine + swap_halves(query) * sine).astype(LOW)
    key = key_ref[...].reshape(rows)
    key_all = (key * cosine + swap_halves(key) * sine).astype(LOW)
    value_all = value_ref[...].reshape(rows).astype(LOW)
    return cosine, sine, query_all, key_all, value_all


def probability_of(query_low, key_low, allowed):
    scores = jnp.where(allowed, contract_last(query_low, key_low) * HEAD**-0.5, -1e30)
    weights = jnp.exp(scores - jnp.max(scores, -1, keepdims=True))
    return weights * (1.0 / jnp.sum(weights, -1, keepdims=True))


def forward_body(
    query_ref, key_ref, value_ref, cos_ref, sin_ref, column_ref, row_ref, mixed_ref, kept_ref
):
    _, _, query_all, key_all, value_all = turned_heads(query_ref, key_ref, value_ref, cos_ref, sin_ref)
    allowed = row_ref[...] <= column_ref[...]
    outs = []
    for at in range(query_all.shape[1] // HEAD):
        part = slice(at * HEAD, (at + 1) * HEAD)
        probability_low = probability_of(query_all[:, part], key_all[:, part], allowed).astype(LOW)
        kept_ref[at] = probability_low
        outs.append(jnp.dot(probability_low, value_all[:, part], preferred_element_type=WIDE))
    mixed_ref[...] = jnp.concatenate(outs, 1).astype(LOW).reshape(mixed_ref.shape)


def backward_body(
    query_ref, key_ref, value_ref, cos_ref, sin_ref, grad_ref, kept_ref, grad_query_ref, grad_key_ref, grad_value_ref
):
    cosine, sine, query_all, key_all, value_all = turned_heads(query_ref, key_ref, value_ref, cos_ref, sin_ref)
    grad_all = grad_ref[...].reshape(value_all.shape)
    scale = HEAD**-0.5
    outs = []
    for at in range(query_all.shape[1] // HEAD):
        part = slice(at * HEAD, (at + 1) * HEAD)
        query_low, key_low = query_all[:, part], key_all[:, part]
        value_low, grad_low = value_all[:, part], grad_all[:, part]
        probability_low = kept_ref[at]
        mixed = jnp.dot(probability_low, value_low, preferred_element_type=WIDE)
        delta = jnp.sum(grad_low.astype(WIDE) * mixed, -1, keepdims=True)
        grad_probability = contract_last(grad_low, value_low)
        grad_scores = (probability_low.astype(WIDE) * (grad_probability - delta)).astype(LOW)
        grad_value = contract_first(probability_low, grad_low)
        grad_query = jnp.dot(grad_scores, key_low, preferred_element_type=WIDE) * scale
        grad_key = contract_first(grad_scores, query_low) * scale
        outs.append((grad_query, grad_key, grad_value))
    grad_query, grad_key, grad_value = [jnp.concatenate(item, 1) for item in zip(*outs)]
    block = grad_query_ref.shape
    grad_query = grad_query * cosine - swap_halves(grad_query) * sine
    grad_key = grad_key * cosine - swap_halves(grad_key) * sine
    grad_query_ref[...] = grad_query.astype(LOW).reshape(block)
    grad_key_ref[...] = grad_key.astype(LOW).reshape(block)
    grad_value_ref[...] = grad_value.astype(LOW).reshape(block)


def attend(qkv, cosine, sine, yn, seqs, column=None, row=None, grad_attention=None, kept=None):
    backward = grad_attention is not None
    tokens, width = qkv.shape[0], qkv.shape[1] // 3
    lanes = min(128, width)
    length = tokens // seqs
    rows = length // yn
    block = (yn, None, rows, lanes)
    cut = lambda array: array.reshape(yn, seqs, rows, array.shape[-1])
    field = pl.BlockSpec(block, lambda s, h: (0, s, 0, h))
    table = pl.BlockSpec(block, lambda s, h: (0, s, 0, 0))
    square = pl.BlockSpec((None, lanes // HEAD, length, length), lambda s, h: (s, h, 0, 0))
    low = low_shape(yn, seqs, rows, width)
    if width % 128 == 0:
        thirds = [cut(qkv)] * 3
        blocks = [
            pl.BlockSpec(block, lambda s, h, part=part: (0, s, 0, part * (width // lanes) + h)) for part in range(3)
        ]
    else:
        thirds = [cut(qkv[:, part * width : (part + 1) * width]) for part in range(3)]
        blocks = [field] * 3
    inputs = [*thirds, cut(cosine[:, :lanes]), cut(sine[:, :lanes])]
    blocks = blocks + [table, table]
    if backward:
        body, inputs, blocks = backward_body, inputs + [cut(grad_attention), kept], blocks + [field, square]
        outs, out_blocks = [low] * 3, [field] * 3
    else:
        body, inputs = forward_body, inputs + [column, row]
        blocks = blocks + [
            pl.BlockSpec((length, 1), lambda s, h: (s, 0)),
            pl.BlockSpec((None, 1, length), lambda s, h: (s, 0, 0)),
        ]
        outs, out_blocks = [low, low_shape(seqs, width // HEAD, length, length)], [field, square]
    made = pl.pallas_call(
        body,
        grid=(seqs, width // lanes),
        in_specs=blocks,
        out_specs=out_blocks,
        out_shape=outs,
        compiler_params=pltpu.CompilerParams(vmem_limit_bytes=40 * 1024 * 1024),
        cost_estimate=cost(13.0),
    )(*inputs)
    return [item.reshape(tokens, width) if item.shape == low.shape else item for item in made]


def normalize(parts, gain_vec, shift_vec):
    span, width = parts[0].shape
    tile = min(span, 128)
    each = span // tile

    def body(*refs):
        step = pl.program_id(0)
        gain_ref, shift_ref, normed_ref, unit_ref = refs[len(parts) :]
        for at, ref in enumerate(refs[: len(parts)]):

            @pl.when(step // each == at)
            def _(ref=ref):
                inputs = ref[...].astype(WIDE)
                centre = inputs - jnp.mean(inputs, -1, keepdims=True)
                spread = jnp.mean(centre * centre, -1, keepdims=True)
                unit = centre * lax.rsqrt(spread + NORM_EPS)
                normed_ref[...] = (unit * gain_ref[...] + shift_ref[...]).astype(LOW)
                unit_ref[...] = unit.astype(LOW)

    block = (tile, width)
    clamp = lambda at: pl.BlockSpec(block, lambda t: (jnp.clip(t - at * each, 0, each - 1), 0))
    vector = pl.BlockSpec((1, width), lambda t: (0, 0))
    return pl.pallas_call(
        body,
        grid=(len(parts) * each,),
        in_specs=[clamp(at) for at in range(len(parts))] + [vector, vector],
        out_specs=[pl.BlockSpec(block, lambda t: (t, 0))] * 2,
        out_shape=[low_shape(len(parts) * span, width)] * 2,
        compiler_params=ROOM,
        cost_estimate=cost(8.0),
    )(*parts, gain_vec, shift_vec)


def bend(up):
    bent = jnp.tanh(GELU_SCALE * (up + GELU_CUBIC * up * up * up))
    slope = 0.5 * (1.0 + bent) + 0.5 * up * (1.0 - bent * bent) * GELU_SCALE * (1.0 + 3.0 * GELU_CUBIC * up * up)
    return (0.5 * up * (1.0 + bent)).astype(LOW), slope.astype(LOW)


def project(normed_low, w_in, bias, split):
    tokens, total = normed_low.shape[0], w_in.shape[1]
    if split % 256 or total % 256:
        made = jnp.dot(normed_low, w_in, preferred_element_type=WIDE) + bias
        return made[:, :split], *bend(made[:, split:])
    heads = split // 256

    def body(normed_ref, w_ref, bias_ref, qkv_ref, hidden_ref, slope_ref):
        step = pl.program_id(0)
        made = jnp.dot(normed_ref[...], w_ref[...], preferred_element_type=WIDE) + bias_ref[...]

        @pl.when(step < heads)
        def _():
            qkv_ref[...] = made

        @pl.when(step >= heads)
        def _():
            hidden_ref[...], slope_ref[...] = bend(made)

    late = pl.BlockSpec((tokens, 256), lambda t: (0, jnp.maximum(t - heads, 0)))
    return pl.pallas_call(
        body,
        grid=(total // 256,),
        in_specs=[
            whole(normed_low),
            pl.BlockSpec((w_in.shape[0], 256), lambda t: (0, t)),
            pl.BlockSpec((1, 256), lambda t: (0, t)),
        ],
        out_specs=[pl.BlockSpec((tokens, 256), lambda t: (0, jnp.minimum(t, heads - 1))), late, late],
        out_shape=[jax.ShapeDtypeStruct((tokens, split), WIDE)] + [low_shape(tokens, total - split)] * 2,
        compiler_params=ROOM,
        cost_estimate=cost(16.0),
    )(normed_low, w_in, bias)


def project_back(grad_out, w_out, slope, dense_rows):
    tokens, width = grad_out.shape
    if dense_rows % 256 or w_out.shape[0] % 256:
        return (
            contract_last(grad_out, w_out[:dense_rows]).astype(LOW),
            (contract_last(grad_out, w_out[dense_rows:]) * slope.astype(WIDE)).astype(LOW),
        )
    first = dense_rows // 256

    def body(grad_ref, w_ref, slope_ref, attention_ref, up_ref):
        step = pl.program_id(0)
        made = contract_last(grad_ref[...], w_ref[...])

        @pl.when(step < first)
        def _():
            attention_ref[...] = made.astype(LOW)

        @pl.when(step >= first)
        def _():
            up_ref[...] = (made * slope_ref[...].astype(WIDE)).astype(LOW)

    late = pl.BlockSpec((tokens, 256), lambda t: (0, jnp.maximum(t - first, 0)))
    return pl.pallas_call(
        body,
        grid=(w_out.shape[0] // 256,),
        in_specs=[whole(grad_out), pl.BlockSpec((256, width), lambda t: (t, 0)), late],
        out_specs=[pl.BlockSpec((tokens, 256), lambda t: (0, jnp.minimum(t, first - 1))), late],
        out_shape=[low_shape(tokens, dense_rows), low_shape(*slope.shape)],
        compiler_params=ROOM,
        cost_estimate=cost(10.0),
    )(grad_out, w_out, slope)


def out_part(attention_low, hidden_low, w_out, dy, rows):
    head, hidden, width = attention_low.shape[1], hidden_low.shape[1], w_out.shape[1]
    if head % 128:
        here = slice(dy * rows, (dy + 1) * rows)
        joined = jnp.concatenate([attention_low[here], hidden_low[here]], 1)
        return jnp.dot(joined, w_out, preferred_element_type=WIDE).astype(LOW)

    def body(attention_ref, hidden_ref, w_ref, out_ref):
        made = jnp.dot(attention_ref[...], w_ref[:head], preferred_element_type=WIDE)
        made += jnp.dot(hidden_ref[...], w_ref[head:], preferred_element_type=WIDE)
        out_ref[...] = made.astype(LOW)

    tile = min(width, 512)
    return pl.pallas_call(
        body,
        grid=(width // tile,),
        in_specs=[
            pl.BlockSpec((rows, head), lambda t: (dy, 0)),
            pl.BlockSpec((rows, hidden), lambda t: (dy, 0)),
            pl.BlockSpec((w_out.shape[0], tile), lambda t: (0, t)),
        ],
        out_specs=pl.BlockSpec((rows, tile), lambda t: (0, t)),
        out_shape=low_shape(rows, width),
        compiler_params=ROOM,
        cost_estimate=cost(5.3),
    )(attention_low, hidden_low, w_out)


def in_part(grads, w_in, unit_low, dy, rows):
    widths = [item.shape[1] for item in grads]
    starts = [sum(widths[:i]) for i in range(len(widths))]
    width = w_in.shape[0]
    if widths[0] % 128:
        here = slice(dy * rows, (dy + 1) * rows)
        made = contract_last(jnp.concatenate([item[here] for item in grads], 1), w_in)
        return made.astype(LOW), jnp.sum(made * unit_low[here].astype(WIDE), 0), jnp.sum(made, 0)

    def body(*refs):
        w_ref, unit_ref, out_ref, gain_ref, shift_ref = refs[len(grads) :]
        made = None
        for ref, start, size in zip(refs, starts, widths):
            term = contract_last(ref[...], w_ref[:, start : start + size])
            made = term if made is None else made + term
        out_ref[...] = made.astype(LOW)
        gain_ref[...] = jnp.sum(made * unit_ref[...].astype(WIDE), 0, keepdims=True)
        shift_ref[...] = jnp.sum(made, 0, keepdims=True)

    tile = min(width, 512)
    vector = pl.BlockSpec((1, tile), lambda t: (0, t))
    made, gain, shift = pl.pallas_call(
        body,
        grid=(width // tile,),
        in_specs=[pl.BlockSpec((rows, size), lambda t: (dy, 0)) for size in widths]
        + [
            pl.BlockSpec((tile, w_in.shape[1]), lambda t: (t, 0)),
            pl.BlockSpec((rows, tile), lambda t: (dy, t)),
        ],
        out_specs=[pl.BlockSpec((rows, tile), lambda t: (0, t)), vector, vector],
        out_shape=[low_shape(rows, width)] + [jax.ShapeDtypeStruct((1, width), WIDE)] * 2,
        compiler_params=ROOM,
        cost_estimate=cost(7.0),
    )(*grads, w_in, unit_low)
    return made, gain[0], shift[0]


def rotary_tables(places):
    lane = jnp.arange(128, dtype=jnp.int32) % HEAD
    half = ROT // 2
    freqs = jnp.asarray(ROPE_BASE, WIDE) ** (-((lane % half).astype(WIDE) * (2.0 / ROT)))
    angles = places.astype(WIDE)[:, None] * freqs
    turned = (lane < ROT)[None, :]
    sign = jnp.where(lane < half, -1.0, 1.0)
    return jnp.where(turned, jnp.cos(angles), 1.0), jnp.where(turned, jnp.sin(angles) * sign, 0.0)


def unfold_rows(grid, gathered, sizes, block_len, group_seqs):
    zn, yn, ranks = grid.z_count, grid.y_count, grid.rank_count
    cuts = [sum(sizes[:i]) for i in range(len(sizes) + 1)]
    gain_full, shift_full, bias_qkv, bias_dense, bias_up, bias_down = [
        gathered[:, cuts[i] : cuts[i + 1]].reshape(-1).astype(WIDE) for i in range(6)
    ]
    orders = gathered[:: grid.ctx_count, cuts[6] :].reshape(zn, 2, -1).astype(jnp.int32)

    ctx_from = jnp.stack(
        [
            (((grid.y - dy) % yn) * 2 + (grid.x ^ dx)) * 2 + (grid.c ^ dc)
            for dy in range(yn)
            for dx in range(2)
            for dc in range(2)
        ]
    )
    z_from = jnp.stack([(grid.z - 2 * i - grid.parity) % zn for i in range(group_seqs)])
    own_orders = lax.dynamic_index_in_dim(orders, grid.c, 1, keepdims=False)[z_from]
    slots = (ctx_from[:, None] * 2 + jnp.arange(2)).reshape(-1)
    places = own_orders[:, slots].reshape(group_seqs, yn, -1).swapaxes(0, 1)
    places = (places[..., None] * block_len + jnp.arange(block_len)).reshape(-1)
    cosine, sine = rotary_tables(places)


    bias_in = jnp.concatenate(
        [
            lax.dynamic_index_in_dim(bias_qkv.reshape(3, ranks, -1), grid.rank, 1, keepdims=False).reshape(-1),
            place(bias_up.reshape(ranks, -1), grid.rank),
        ]
    )
    column = places.reshape(yn, group_seqs, -1).swapaxes(0, 1).reshape(-1).astype(WIDE)
    return (
        gain_full[None], shift_full[None], bias_in[None], (bias_dense + bias_down)[None], cosine, sine,
        column[:, None], column.reshape(group_seqs, 1, -1),
    )


def on_device(
    tokens, block_order, ln_gain, ln_bias, w_qkv, b_qkv, w_dense, b_dense, w_fc1, b_fc1, w_fc2, b_fc2, cotangent,
):
    grid = Grid()
    seqs, span, model_width = tokens.shape
    zn, yn, ranks = grid.z_count, grid.y_count, grid.rank_count
    device_count = ranks * 4
    length = span * grid.ctx_count
    block_len = span // 2
    group_seqs = zn // 2
    head_width = model_width // ranks

    split = 3 * head_width
    dense_rows = 4 * w_dense.shape[0]
    rows = group_seqs * length // yn
    seq_rows = length // yn
    last = group_seqs - 1

    def ordered(spreads):
        return [spreads[i].parts[dy] for dy in range(yn) for i in range(group_seqs)]

    def rows_of(array, i):
        return array[i * seq_rows : (i + 1) * seq_rows]

    def across_x(ks):
        own = near[ks[0]][None] if len(ks) == 1 else grid.pile(*[near[k][None] for k in ks])
        return ks, own, grid.start(own, x=1)

    def both_columns(group):
        ks, own, moving = group
        return ks, grid.pile(own[None], grid.wait(moving)[None])

    away, own_tokens, own_cotangent = part_cores(grid, tokens, cotangent)
    moving = grid.start(away, c=1)
    down_moving = grid.start(w_fc2, x=1)
    others = grid.wait(moving)
    ring = Ring(grid, grid.pile(own_tokens, others[:span]))
    ring.begin(1)
    ahead, across = cut_columns(grid, *grid.after((w_qkv, w_fc1)))
    across = [grid.start(part, y=dy + 1) for dy, part in enumerate(across)]
    vectors = (ln_gain, ln_bias, b_qkv, b_dense, b_fc1, b_fc2, block_order.astype(LOW).reshape(-1))
    sizes = [item.shape[0] for item in vectors]
    down_moving = grid.wait(down_moving)
    dense_moving = grid.start(w_dense, x=1)
    gather = VectorGather(grid, jnp.concatenate(grid.after(vectors)))
    gather.begin()
    ring.end()
    spreads = [Spread(grid, ring.pair(0))]
    ring.begin(2)
    gather.end()
    across = grid.wait(across)
    gather.begin()

    def pack(z, y, x, c, ins, outs):
        for k in range(zn):
            outs[k][0] = ins[k][...]
            for dy in range(1, yn):
                outs[k][dy] = ins[zn + dy - 1][k]

    near = grid.local(pack, [*ahead, *across], [low_shape(yn, *ahead[0].shape)] * zn)
    near = dict(enumerate(near))
    near[zn - 1] = grid.start(near[zn - 1], z=-1)
    gather.end()
    gather.begin()
    dense_moving = grid.wait(dense_moving)

    def stack_out(z, y, x, c, ins, outs):
        for at in range(2):
            dense = ins[2 * at].shape[0]
            outs[0][at, :dense] = ins[2 * at][...]
            outs[0][at, dense:] = ins[2 * at + 1][...]

    out_rows = grid.local(
        stack_out,
        grid.after([w_dense, w_fc2, dense_moving, down_moving]),
        [low_shape(2, w_dense.shape[0] + w_fc2.shape[0], model_width)],
    )[0]
    spreads[0].end_x()
    spreads[0].begin_y()
    group_own = across_x([0])
    ring.end()
    near[zn - 1] = grid.wait(near[zn - 1])
    gather.end()
    ring.finish()
    spreads += [Spread(grid, ring.pair(i)) for i in range(1, group_seqs)]
    rest = [k for k in grid.steps() if k != zn - 1]
    moving = {k: grid.start(near[k], z=k) for k in rest}
    gather.begin()
    group_own = both_columns(group_own)
    spreads[0].end_y()
    for spread in spreads[1:]:
        spread.end_x()
    spreads[1].begin_y()
    group_far = across_x([zn - 1])
    near.update(grid.wait(moving))
    gather.end()
    group_far = both_columns(group_far)
    group_rest = across_x(rest)
    met_grad = grid.pile(own_cotangent, others[span:])
    ring = Ring(grid, met_grad)
    ring.begin(1)

    def beside(z, y, x, c, ins, outs):
        for at, ref in enumerate(ins):
            outs[0][:, at : at + 1] = ref[...]

    first = group_own[0] + group_far[0]
    first_rows = grid.local(beside, [group_own[1], group_far[1]], [low_shape(2, 2, *group_own[1].shape[2:])])[0]
    first_moving = grid.start(first_rows, c=1)
    while gather.ways:
        gather.step()
    if head_width % 128 == 0:
        unfolded = grid.hold(unfold_vectors(grid, gather.block, sizes, block_len, group_seqs))
    else:
        unfolded = unfold_rows(grid, gather.result(), sizes, block_len, group_seqs)
    gain_full, shift_full, bias_in, bias_out, cosine, sine, column, row = unfolded
    spreads[1].end_y()
    for spread in spreads[2:]:
        spread.begin_y()
        spread.end_y()
    normed_low, unit_low = grid.hold(normalize(ordered(spreads), gain_full, shift_full))
    first_moving = grid.wait(first_moving)
    group_rest = both_columns(group_rest)
    rest_moving = grid.start(group_rest[1], c=1)
    out_moving = grid.start(out_rows, c=1)
    ring.end()
    grads = [Spread(grid, ring.pair(0))]
    ring.begin(2)
    rest_moving = grid.wait(rest_moving)
    w_in = grid.hold(join_columns(grid, [(first, first_rows, first_moving), (*group_rest, rest_moving)]))
    grads[0].end_x()
    grads[0].begin_y()
    ring.end()
    ring.finish()
    out_moving = grid.wait(out_moving)
    grads += [Spread(grid, ring.pair(i)) for i in range(1, group_seqs)]

    qkv, hidden_low, slope = grid.hold(project(grid.after(normed_low), w_in, bias_in, split))
    grid.pages = False
    for spread in grads[1:]:
        spread.end_x()
    grads[1].begin_y()
    w_out = grid.hold(join_out(grid, *grid.after((out_rows, out_moving)), w_dense.shape[0]))
    attention_low, kept = grid.hold(attend(grid.after(qkv), cosine, sine, yn, group_seqs, column=column, row=row))
    out_parts = {}
    for dy in range(yn - 1, -1, -1):
        out_parts[dy] = grid.hold(out_part(grid.after(attention_low), hidden_low, w_out, dy, rows))
    grads[0].end_y()
    grads[1].end_y()
    for spread in grads[2:]:
        spread.begin_y()
        spread.end_y()

    out_sums = {i: TokenSum(grid, rows_of(out_parts[yn - 1], i), yn - 1) for i in range(last, -1, -1)}
    grad_out = grid.pile(*grid.after(ordered(grads)))
    grad_attention_low, grad_up_low = grid.hold(project_back(grad_out, w_out, slope, dense_rows))
    up_kept, up_away, (sum_up,) = grid.hold(halves_in(grid, grid.after(normed_low), [grad_up_low]))

    def finish_y(sums, parts, i):
        for dy in range(yn - 2, -1, -1):
            sums[i].more(rows_of(parts[dy], i))

    finish_y(out_sums, out_parts, last)
    out_sums[last].begin_x()
    up_moving = grid.start(up_away, c=1)
    up_kept, up_away = halve_columns(grid, up_kept, grid.wait(up_moving))
    up_moving = grid.start(up_away, x=1)
    grads_qkv = grid.hold(
        attend(grid.after(qkv), cosine, sine, yn, group_seqs, grad_attention=grad_attention_low, kept=kept)
    )
    grads_in = [*grads_qkv, grad_up_low]
    out_ring = RingSum(grid)
    out_ring.pieces[2 * last], out_ring.pieces[2 * last + 1] = out_sums[last].end_x()
    for i in range(last - 1, 0, -1):
        finish_y(out_sums, out_parts, i)
        out_sums[i].begin_x()
        out_ring.pieces[2 * i], out_ring.pieces[2 * i + 1] = out_sums[i].end_x()
    out_ring.begin_far()
    in_parts, gain_parts, shift_parts = {}, {}, {}

    def make_in_part(dy):
        in_parts[dy], gain_parts[dy], shift_parts[dy] = grid.hold(
            in_part(grid.after(grads_in), w_in, unit_low, dy, rows)
        )

    make_in_part(yn - 1)
    finish_y(out_sums, out_parts, 0)
    in_sums = {last: TokenSum(grid, rows_of(in_parts[yn - 1], last), yn - 1)}
    out_sums[0].begin_x()
    for dy in range(yn - 2, -1, -1):
        make_in_part(dy)
    out_ring.end_far()
    up_moving = grid.wait(up_moving)
    for i in range(last - 1, -1, -1):
        in_sums[i] = TokenSum(grid, rows_of(in_parts[yn - 1], i), yn - 1)
    out_ring.pieces[0], out_ring.pieces[1] = out_sums[0].end_x()
    out_ring.begin_near()
    qkv_kept, qkv_away, sums_qkv = grid.hold(halves_in(grid, grid.after(normed_low), grads_qkv))
    qkv_moving = grid.start(qkv_away, c=1)
    finish_y(in_sums, in_parts, last)
    in_sums[last].begin_x()
    out_kept, out_away = grid.hold(halves_out(grid, *grid.after((attention_low, hidden_low)), grad_out))
    qkv_kept, qkv_away = halve_columns(grid, qkv_kept, grid.wait(qkv_moving))
    out_ring.end_near()
    up_return = ColumnReturn(grid, up_kept, up_moving)
    in_ring = RingSum(grid)
    in_ring.pieces[2 * last], in_ring.pieces[2 * last + 1] = in_sums[last].end_x()
    qkv_moving = grid.start(qkv_away, x=1)
    for i in range(last - 1, -1, -1):
        finish_y(in_sums, in_parts, i)
        if i:
            in_sums[i].begin_x()
            in_ring.pieces[2 * i], in_ring.pieces[2 * i + 1] = in_sums[i].end_x()
    projected = out_ring.end()
    up_return.end_z()
    in_ring.begin_far()
    in_sums[0].begin_x()
    up_return.begin_y()
    out_moving = grid.start(out_away, c=1)
    output = grid.hold((tokens.astype(WIDE) + projected + bias_out).astype(LOW))
    qkv_moving = grid.wait(qkv_moving)
    out_kept, out_away = halve_columns(grid, out_kept, grid.wait(out_moving))
    in_ring.pieces[0], in_ring.pieces[1] = in_sums[0].end_x()
    up_found = up_return.end()
    out_moving = grid.start(out_away, x=1)
    in_ring.end_far()
    in_ring.begin_near()
    qkv_return = ColumnReturn(grid, qkv_kept, qkv_moving)
    grad_w_up = grid.hold(lay_columns(grid, up_found, 1))

    def laid(part, count):
        whole = jnp.zeros((count, ranks, part.shape[-1]), WIDE)
        whole = lax.dynamic_update_index_in_dim(whole, part, grid.rank, 1)
        return whole.reshape(device_count, -1)

    own_grad = cotangent.astype(WIDE)
    sums = jnp.concatenate(
        grid.after(
            [
                sum(gain_parts.values()).reshape(device_count, -1),
                sum(shift_parts.values()).reshape(device_count, -1),
                laid(jnp.concatenate(sums_qkv, 0), 3),
                jnp.sum(own_grad, (0, 1)).reshape(device_count, -1),
                laid(sum_up, 1),
            ]
        ),
        1,
    )
    sums = VectorSum(grid, grid.hold(sums))
    in_ring.end_near()
    sums.begin()
    grad_normed = in_ring.end()
    sums.end()
    qkv_return.end_z()
    qkv_return.begin_y()
    sums.begin()
    qkv_found = qkv_return.end()
    sums.end()
    sums.begin()
    sums.end()
    sums.begin()
    sums.end()
    grad_w_out = (out_kept.astype(WIDE) + grid.wait(out_moving).astype(WIDE))[0]

    own_inputs = tokens.astype(WIDE)
    centre = own_inputs - jnp.mean(own_inputs, -1, keepdims=True)
    turn = lax.rsqrt(jnp.mean(centre * centre, -1, keepdims=True) + NORM_EPS)
    own_unit = centre * turn
    scaled = grad_normed * gain_full
    token_grad = (
        own_grad
        + turn
        * (scaled - jnp.mean(scaled, -1, keepdims=True) - own_unit * jnp.mean(scaled * own_unit, -1, keepdims=True))
    ).astype(LOW)
    grad_w_qkv = lay_columns(grid, qkv_found, 3)

    sums = sums.cut
    grad_gain, grad_shift = sums[: sizes[0]], sums[sizes[0] : 2 * sizes[0]]
    rest = sums[2 * sizes[0] :]
    grad_bias_qkv = rest[: sizes[2]]
    grad_bias_out = rest[sizes[2] : sizes[2] + sizes[3]]
    grad_bias_up = rest[sizes[2] + sizes[3] :]
    grad_w_dense = grad_w_out[: w_dense.shape[0]]
    grad_w_down = grad_w_out[w_dense.shape[0] :]
    return (
        output, token_grad, grad_gain, grad_shift, grad_w_qkv, grad_bias_qkv,
        grad_w_dense, grad_bias_out, grad_w_up, grad_bias_up, grad_w_down, grad_bias_out,
    )


def solution(mesh):
    rows = P(("dp", "ctx"), None)
    vector = P(("dp", "ctx"))
    spread = P("dp", "ctx", None)
    in_specs = (
        spread, P("dp", None), vector, vector, rows, vector, rows, vector, rows, vector, rows, vector, spread,
    )
    out_specs = (
        spread, spread, vector, vector, rows, vector, rows, vector, rows, vector, rows, vector,
    )
    return jax.shard_map(on_device, mesh=mesh, in_specs=in_specs, out_specs=out_specs, check_vma=False)
```

```python
from functools import partial

import jax
import jax.numpy as jnp
import numpy as np
from jax import lax
from jax.experimental import pallas as pl
from jax.experimental.pallas import tpu as pltpu
from jax.sharding import PartitionSpec as P

HEAD = 64
ROT = 32
ROPE_BASE = 10000
NORM_EPS = 1e-05
BOTH = ("dp", "ctx")
LOW = jnp.bfloat16
WIDE = jnp.float32
GELU_SCALE = 0.7978845608028654
GELU_CUBIC = 0.044715


COST_SCALE = 20_000_000


LIGHT = pl.CostEstimate(flops=1024, bytes_accessed=1024, transcendentals=1)


def cost(micros):
    return pl.CostEstimate(flops=int(micros * COST_SCALE), bytes_accessed=1024, transcendentals=1)
ROOM = pltpu.CompilerParams(vmem_limit_bytes=48 * 1024 * 1024)


def low_shape(*shape):
    return jax.ShapeDtypeStruct(shape, LOW)


def place(array, index):
    return lax.dynamic_index_in_dim(array, index, 0, keepdims=False)


def turn_page(token):
    def body(token_ref, copy_ref):
        copy_ref[...] = token_ref[...]

    return pl.pallas_call(
        body,
        out_shape=jax.ShapeDtypeStruct(token.shape, token.dtype),
        cost_estimate=pl.CostEstimate(flops=100_000_000_000, bytes_accessed=8192, transcendentals=0),
    )(token)


class Grid:
    def __init__(self):
        self.z_count = lax.axis_size("dp")
        self.ctx_count = lax.axis_size("ctx")
        self.y_count = self.ctx_count // 4
        ctx = lax.axis_index("ctx")
        self.z = lax.axis_index("dp")
        self.y = ctx // 4
        self.x = (ctx // 2) % 2
        self.c = ctx % 2
        self.where = jnp.stack([self.z, self.y, self.x, self.c]).astype(jnp.int32)
        self.rank = self.z * self.y_count + self.y
        self.rank_count = self.z_count * self.y_count
        self.parity = (self.z + self.x) % 2
        self.token = jnp.zeros((8, 128), WIDE)
        self.started, self.pages = False, True

    def steps(self):
        order = sorted(range(1, self.z_count), key=lambda k: (min(k, self.z_count - k), k))
        return order

    def after(self, value):
        self.page()
        return lax.optimization_barrier((value, self.token))[0]

    def hold(self, value):
        self.page()
        value, self.token = lax.optimization_barrier((value, self.token))
        return value

    wait = hold

    def page(self):
        if self.started and self.pages:
            self.token = turn_page(self.token)
        self.started = False

    def swap(self, value, bit):
        pairs = [(device, device ^ (1 << bit)) for device in range(self.rank_count * 4)]
        return self.send(value, pairs)

    def turn(self):
        self.token = turn_page(self.token)
        self.started = False

    def start(self, value, z=0, y=0, x=0, c=0):
        pairs = []
        for z_at in range(self.z_count):
            for y_at in range(self.y_count):
                for x_at in range(2):
                    for c_at in range(2):
                        z_to = (z_at + z) % self.z_count
                        y_to = (y_at + y) % self.y_count
                        source = ((z_at * self.y_count + y_at) * 2 + x_at) * 2 + c_at
                        target = ((z_to * self.y_count + y_to) * 2 + (x_at ^ x)) * 2 + (c_at ^ c)
                        pairs.append((source, target))
        return self.send(value, pairs)

    def send(self, value, pairs):
        value = lax.optimization_barrier((value, self.token))[0]
        self.started = True
        return lax.ppermute(value, BOTH, pairs)

    def local(self, body, inputs, outs):
        count = len(inputs)

        def whole_body(where_ref, *refs):
            body(*[where_ref[i] for i in range(4)], refs[:count], refs[count:])

        vmem = pl.BlockSpec(memory_space=pltpu.VMEM)
        return pl.pallas_call(
            whole_body,
            in_specs=[pl.BlockSpec(memory_space=pltpu.SMEM)] + [vmem] * count,
            out_specs=[vmem] * len(outs),
            out_shape=outs,
            compiler_params=ROOM,
            cost_estimate=cost(1.5),
        )(self.where, *inputs)

    def pile(self, *arrays):
        lengths = [item.shape[0] for item in arrays]
        starts = [sum(lengths[:i]) for i in range(len(lengths))]

        def body(z, y, x, c, ins, outs):
            for ref, start, length in zip(ins, starts, lengths):
                outs[0][start : start + length] = ref[...]

        shape = (sum(lengths), *arrays[0].shape[1:])
        return self.local(body, arrays, [jax.ShapeDtypeStruct(shape, arrays[0].dtype)])[0]


def mover(grid, plan, inputs, outs):
    count = len(inputs)

    def copies_of(where_ref, refs, sems):
        at = [where_ref[i] for i in range(4)]
        listed = plan(*at, refs[:count], refs[count:])
        return [pltpu.make_async_copy(source, target, sems.at[i]) for i, (source, target) in enumerate(listed)]

    def body(where_ref, *refs):
        copies = copies_of(where_ref, refs[:-1], refs[-1])
        for copy in copies:
            copy.start()
        for copy in copies:
            copy.wait()

    most = 4 * max(4, grid.rank_count)
    return pl.pallas_call(
        body,
        in_specs=[pl.BlockSpec(memory_space=pltpu.SMEM)] + [pl.BlockSpec(memory_space=pltpu.VMEM)] * count,
        out_specs=[pl.BlockSpec(memory_space=pltpu.HBM)] * len(outs),
        out_shape=outs,
        scratch_shapes=[pltpu.SemaphoreType.DMA((most,))],
        compiler_params=pltpu.CompilerParams(vmem_limit_bytes=24 * 1024 * 1024),
        cost_estimate=LIGHT,
    )(grid.where, *inputs)


def part_cores(grid, tokens, cotangent):
    span, width = tokens.shape[1:]

    def body(z, y, x, c, ins, outs):
        for at, ref in enumerate(ins):
            outs[0][at * span : (at + 1) * span] = ref[1 - c]
            outs[1 + at][...] = ref[c]

    shapes = [low_shape(2 * span, width), low_shape(span, width), low_shape(span, width)]
    return grid.local(body, [tokens, cotangent], shapes)


def pair_of(grid, even, odd):
    def body(z, y, x, c, ins, outs):
        swap = lax.rem(z + x, 2)
        for first in range(2):

            @pl.when(swap == first)
            def _(first=first):
                outs[0][...] = ins[first][...]
                outs[1][...] = ins[1 - first][...]

    return grid.local(body, [even, odd], [low_shape(*even.shape)] * 2)


class Ring:
    def __init__(self, grid, first):
        self.grid, self.pieces, self.moving = grid, {0: first}, {}

    def begin(self, r):
        zn = self.grid.z_count
        self.moving[r] = self.grid.start(self.pieces[r - 1], z=1)
        if zn - r > zn // 2:
            self.moving[zn - r] = self.grid.start(self.pieces[(zn - r + 1) % zn], z=-1)

    def end(self):
        self.pieces.update(self.grid.wait(self.moving))
        self.moving = {}

    def finish(self):
        for r in range(3, self.grid.z_count // 2 + 1):
            self.begin(r)
            self.end()

    def pair(self, i):
        return pair_of(self.grid, self.pieces[2 * i], self.pieces[2 * i + 1])


class Spread:
    def __init__(self, grid, pair):
        self.grid = grid
        self.keep, away = pair
        self.moving = grid.start(away, x=1)

    def end_x(self):
        self.parts = [self.grid.pile(self.keep, self.grid.wait(self.moving))]

    def begin_y(self):
        self.moving = self.grid.start(self.parts[-1], y=1)

    def end_y(self):
        self.parts.append(self.grid.wait(self.moving))
        for _ in range(2, self.grid.y_count):
            self.begin_y()
            self.parts.append(self.grid.wait(self.moving))


def sum_low(left, right):
    return (left.astype(WIDE) + right.astype(WIDE)).astype(LOW)


class TokenSum:
    def __init__(self, grid, part, dy):
        self.grid = grid
        self.moving = grid.start(part, y=-1)
        self.left = dy - 1

    def more(self, part):
        arrived = self.grid.wait(self.moving)
        if self.left:
            self.moving = self.grid.start(sum_low(part, arrived), y=-1)
            self.left -= 1
            return
        span = arrived.shape[0] // 2

        def body(z, y, x, c, ins, outs):
            for at in range(2):
                here = slice(at * span, (at + 1) * span)
                outs[at][...] = sum_low(ins[0][here], ins[1][here])

        self.kept, self.away = self.grid.local(body, [part, arrived], [low_shape(span, arrived.shape[1])] * 2)

    def begin_x(self):
        self.moving = self.grid.start(self.away, x=1)

    def end_x(self):
        return pair_of(self.grid, self.kept, self.grid.wait(self.moving))


class RingSum:
    def __init__(self, grid):
        self.grid, self.pieces = grid, {}

    def add(self, left, right):
        def body(z, y, x, c, ins, outs):
            outs[0][...] = sum_low(ins[0][...], ins[1][...])

        return self.grid.local(body, [left, right], [low_shape(*left.shape)])[0]

    def begin_far(self):
        grid, zn, pieces = self.grid, self.grid.z_count, self.pieces
        down, up = zn // 2, zn // 2 + 1
        while down > 2:
            arrived = grid.wait(grid.start(pieces[down], z=-1))
            down -= 1
            pieces[down] = self.add(pieces[down], arrived)
        while up < zn - 1:
            arrived = grid.wait(grid.start(pieces[up], z=1))
            up += 1
            pieces[up] = self.add(pieces[up], arrived)
        self.moving = grid.start(pieces[2], z=-1), grid.start(pieces[zn - 1], z=1)

    def end_far(self):
        self.down, self.up = self.grid.wait(self.moving)

    def begin_near(self):
        self.moving = self.grid.start(self.add(self.pieces[1], self.down), z=-1)

    def end_near(self):
        near = self.grid.wait(self.moving)
        span = near.shape[0] // 2

        def body(z, y, x, c, ins, outs):
            total = ins[0][...].astype(WIDE) + ins[1][...].astype(WIDE) + ins[2][...].astype(WIDE)
            outs[0][...] = total[:span]
            outs[1][...] = total[span:].astype(LOW)

        shapes = [jax.ShapeDtypeStruct((span, near.shape[1]), WIDE), low_shape(span, near.shape[1])]
        self.own, away = self.grid.local(body, [self.pieces[0], self.up, near], shapes)
        self.moving = self.grid.start(away, c=1)

    def end(self):
        return self.own, self.grid.wait(self.moving)


def finish_output(grid, tokens, own, other, bias_out):
    def body(z, y, x, c, ins, outs):
        for ref, at in ((ins[1], c), (ins[2], 1 - c)):
            outs[0][at] = (ins[0][at].astype(WIDE) + ref[...].astype(WIDE) + ins[3][...]).astype(LOW)

    return grid.local(body, [tokens, own, other, bias_out], [low_shape(*tokens.shape)])[0]


def finish_grad(grid, tokens, cotangent, own, other, gain_vec):
    def body(z, y, x, c, ins, outs):
        for ref, at in ((ins[2], c), (ins[3], 1 - c)):
            inputs = ins[0][at].astype(WIDE)
            centre = inputs - jnp.mean(inputs, -1, keepdims=True)
            turn = lax.rsqrt(jnp.mean(centre * centre, -1, keepdims=True) + NORM_EPS)
            unit = centre * turn
            scaled = ref[...].astype(WIDE) * ins[4][...]
            along = jnp.mean(scaled * unit, -1, keepdims=True)
            change = turn * (scaled - jnp.mean(scaled, -1, keepdims=True) - unit * along)
            outs[0][at] = (ins[1][at].astype(WIDE) + change).astype(LOW)

    return grid.local(body, [tokens, cotangent, own, other, gain_vec], [low_shape(*tokens.shape)])[0]


def cut_columns(grid, w_qkv, w_up):
    zn, yn, ranks = grid.z_count, grid.y_count, grid.rank_count
    rows, third, wide = w_qkv.shape[0], w_qkv.shape[1] // 3, w_up.shape[1]
    head, hidden = third // ranks, wide // ranks
    width = 3 * head + hidden
    outs = [low_shape(rows, width)] * zn + [low_shape(zn, rows, width)] * (yn - 1)

    def plan(z, y, x, c, ins, refs):
        copies = []
        for dy in range(yn):
            for k in range(zn):
                rank = lax.rem(z + k, zn) * yn + lax.rem(y + dy, yn)
                target = refs[k] if dy == 0 else refs[zn + dy - 1].at[k]
                for part in range(3):
                    start = pl.multiple_of(part * third + rank * head, 128)
                    copies.append((ins[0].at[:, pl.ds(start, head)], target.at[:, pl.ds(part * head, head)]))
                start = pl.multiple_of(rank * hidden, 128)
                copies.append((ins[1].at[:, pl.ds(start, hidden)], target.at[:, pl.ds(3 * head, hidden)]))
        return copies

    if head % 128 == 0:
        made = mover(grid, plan, [w_qkv, w_up], outs)
    else:
        heads = w_qkv.reshape(rows, 3, ranks, head)
        hiddens = w_up.reshape(rows, ranks, hidden)

        def block(k, dy):
            rank = (grid.z + k) % zn * yn + (grid.y + dy) % yn
            mine = lax.dynamic_index_in_dim(heads, rank, 2, keepdims=False).reshape(rows, 3 * head)
            return jnp.concatenate([mine, lax.dynamic_index_in_dim(hiddens, rank, 1, keepdims=False)], 1)

        made = [block(k, 0) for k in range(zn)] + [
            jnp.stack([block(k, dy) for k in range(zn)]) for dy in range(1, yn)
        ]
    return made[:zn], made[zn:]


def join_columns(grid, groups):
    zn, yn = grid.z_count, grid.y_count
    rows, width = groups[0][1].shape[-2:]
    flat = [item for group in groups for item in group[1:]]

    def body(where_ref, *refs):
        z, y, x, c = [where_ref[i] for i in range(4)]
        for at_group, group in enumerate(groups):
            for way in range(4):
                column, core = lax.rem(x + way % 2, 2), lax.rem(c + way // 2, 2)
                for at, k in enumerate(group[0]):
                    for dy in range(yn):
                        rank = lax.rem(z - k + zn, zn) * yn + lax.rem(y - dy + yn, yn)
                        start = pl.multiple_of(((rank * 2 + column) * 2 + core) * rows, rows)
                        refs[-1][pl.ds(start, rows)] = refs[2 * at_group + way // 2][way % 2, at, dy]

    vmem = pl.BlockSpec(memory_space=pltpu.VMEM)
    return pl.pallas_call(
        body,
        in_specs=[pl.BlockSpec(memory_space=pltpu.SMEM)] + [vmem] * len(flat),
        out_specs=vmem,
        out_shape=low_shape(zn * yn * 4 * rows, width),
        compiler_params=ROOM,
        cost_estimate=LIGHT,
    )(grid.where, *flat)


def join_out(grid, here, there, dense_rows):
    down_rows = here.shape[1] - dense_rows

    def plan(z, y, x, c, ins, outs):
        copies = []
        for way in range(4):
            source = ins[way // 2].at[way % 2]
            at = lax.rem(x + way % 2, 2) * 2 + lax.rem(c + way // 2, 2)
            first = pl.multiple_of(at * dense_rows, dense_rows)
            second = pl.multiple_of(4 * dense_rows + at * down_rows, dense_rows)
            copies.append((source.at[pl.ds(0, dense_rows)], outs[0].at[pl.ds(first, dense_rows)]))
            copies.append((source.at[pl.ds(dense_rows, down_rows)], outs[0].at[pl.ds(second, down_rows)]))
        return copies

    return mover(grid, plan, [here, there], [low_shape(4 * here.shape[1], here.shape[2])])[0]


def halves_in(grid, left, rights):
    tokens, ranks = left.shape[0], grid.rank_count
    widths = [item.shape[1] for item in rights]
    width = sum(widths)
    quad = left.shape[1] // ranks
    rows = quad // 4
    sums = [jax.ShapeDtypeStruct((1, size), WIDE) for size in widths]
    if quad % 128:
        made = contract_first(left, jnp.concatenate(rights, 1)).astype(LOW).reshape(ranks, 2, 2, rows, width)
        pick = lambda index: lax.dynamic_index_in_dim(made, index, 2, keepdims=False)
        return pick(grid.c), pick(1 - grid.c), [jnp.sum(item.astype(WIDE), 0, keepdims=True) for item in rights]
    starts = [sum(widths[:i]) for i in range(len(widths))]

    def body(where_ref, left_ref, *refs):
        core = where_ref[3]
        ins, (kept_ref, away_ref, *sum_refs), made_ref = refs[: len(rights)], refs[len(rights) : -1], refs[-1]
        for ref, start, size in zip(ins, starts, widths):
            made_ref[:, start : start + size] = contract_first(left_ref[...], ref[...]).astype(LOW)
        for column in range(2):
            for out_ref, at in ((kept_ref, core), (away_ref, 1 - core)):
                start = pl.multiple_of((2 * column + at) * rows, rows)
                out_ref[column] = made_ref[pl.ds(start, rows)]

        @pl.when(pl.program_id(0) == 0)
        def _():
            for ref, sum_ref in zip(ins, sum_refs):
                sum_ref[...] = jnp.sum(ref[...].astype(WIDE), 0, keepdims=True)

    half = pl.BlockSpec((None, 2, rows, width), lambda t: (t, 0, 0, 0))
    made = pl.pallas_call(
        body,
        grid=(ranks,),
        in_specs=[pl.BlockSpec(memory_space=pltpu.SMEM), pl.BlockSpec((tokens, quad), lambda t: (0, t))]
        + [whole(item) for item in rights],
        out_specs=[half, half] + [whole(item) for item in sums],
        out_shape=[low_shape(ranks, 2, rows, width)] * 2 + sums,
        scratch_shapes=[pltpu.VMEM((quad, width), LOW)],
        compiler_params=ROOM,
        cost_estimate=cost(8.0),
    )(grid.where, left, *rights)
    return made[0], made[1], made[2:]


def halves_out(grid, attention_low, hidden_low, grad_out):
    tokens, width = grad_out.shape
    dense, down = attention_low.shape[1], hidden_low.shape[1]
    rows = (dense // 4, down // 4)
    shape = low_shape(1, 2, sum(rows), width)
    if dense % 128 or down % 512:
        made = [
            contract_first(item, grad_out).astype(LOW).reshape(2, 2, -1, width) for item in (attention_low, hidden_low)
        ]
        pick = lambda index: jnp.concatenate(
            [lax.dynamic_index_in_dim(item, index, 1, keepdims=False) for item in made], 1
        )[None]
        return pick(grid.c), pick(1 - grid.c)

    def body(where_ref, dense_ref, down_ref, grad_ref, kept_ref, away_ref, made_ref):
        core, step = where_ref[3], pl.program_id(0)

        @pl.when(step == 0)
        def _():
            made_ref[...] = contract_first(dense_ref[...], grad_ref[...]).astype(LOW)
            for column in range(2):
                for out_ref, at in ((kept_ref, core), (away_ref, 1 - core)):
                    start = pl.multiple_of((2 * column + at) * rows[0], rows[0])
                    out_ref[0, column, : rows[0]] = made_ref[pl.ds(start, rows[0])]

        for quarter in range(4):
            for out_ref, at in ((kept_ref, core), (away_ref, 1 - core)):

                @pl.when((step == quarter + 1) & (at == quarter % 2))
                def _(out_ref=out_ref, quarter=quarter):
                    made = contract_first(down_ref[...], grad_ref[...]).astype(LOW)
                    out_ref[0, quarter // 2, rows[0] :] = made

    return pl.pallas_call(
        body,
        grid=(5,),
        in_specs=[
            pl.BlockSpec(memory_space=pltpu.SMEM),
            whole(attention_low),
            pl.BlockSpec((tokens, rows[1]), lambda t: (0, jnp.maximum(t - 1, 0))),
            whole(grad_out),
        ],
        out_specs=[whole(shape)] * 2,
        out_shape=[shape] * 2,
        scratch_shapes=[pltpu.VMEM((dense, width), LOW)],
        compiler_params=ROOM,
        cost_estimate=cost(11.0),
    )(grid.where, attention_low, hidden_low, grad_out)


def halve_columns(grid, kept, arrived):
    count, _, rows, width = kept.shape

    def body(where_ref, kept_ref, arrived_ref, here_ref, there_ref):
        column = where_ref[2]
        for ref, at in ((here_ref, column), (there_ref, 1 - column)):
            ref[...] = sum_low(kept_ref[at], arrived_ref[at])

    both = pl.BlockSpec((None, 2, rows, width), lambda t: (t, 0, 0, 0))
    one = pl.BlockSpec((None, rows, width), lambda t: (t, 0, 0))
    return pl.pallas_call(
        body,
        grid=(count,),
        in_specs=[pl.BlockSpec(memory_space=pltpu.SMEM), both, both],
        out_specs=[one, one],
        out_shape=[low_shape(count, rows, width)] * 2,
        compiler_params=ROOM,
        cost_estimate=cost(4.5),
    )(grid.where, kept, arrived)


class ColumnReturn:
    def __init__(self, grid, kept, arrived):
        zn, yn = grid.z_count, grid.y_count
        self.grid, self.shape = grid, kept.shape[1:]

        def body(z, y, x, c, ins, outs):
            for k in range(zn):
                for at in range(yn):
                    rank = lax.rem(z + k, zn) * yn + at
                    outs[k][at] = sum_low(ins[0][rank], ins[1][rank])

        cut = grid.local(body, [kept, arrived], [low_shape(yn, *self.shape)] * zn)
        self.by_z = {0: cut[0]}
        self.moving = {k: grid.start(cut[k], z=k) for k in grid.steps()}

    def end_z(self):
        grid, zn, yn = self.grid, self.grid.z_count, self.grid.y_count
        self.by_z.update(grid.wait(self.moving))

        def body(z, y, x, c, ins, outs):
            for dy in range(yn):
                for k in range(zn):
                    outs[dy][k] = ins[k][lax.rem(y + dy, yn)]

        self.cut = grid.local(body, [self.by_z[k] for k in range(zn)], [low_shape(zn, *self.shape)] * yn)

    def begin_y(self):
        self.moving = [self.grid.start(self.cut[dy], y=dy) for dy in range(1, self.grid.y_count)]

    def end(self):
        return [self.cut[0], *self.grid.wait(self.moving)]


def lay_columns(grid, found, parts):
    zn, yn, ranks = grid.z_count, grid.y_count, grid.rank_count
    rows, width = found[0].shape[1:]
    width = width // parts

    if width % 128 == 0:

        def body(z, y, x, c, ins, outs):
            for dy, ref in enumerate(ins):
                for k in range(zn):
                    rank = lax.rem(z - k + zn, zn) * yn + lax.rem(y - dy + yn, yn)
                    for part in range(parts):
                        start = pl.multiple_of((part * ranks + rank) * width, 128)
                        item = ref[k, :, part * width : (part + 1) * width]
                        outs[0][:, pl.ds(start, width)] = item.astype(WIDE)

        return grid.local(body, found, [jax.ShapeDtypeStruct((rows, parts * ranks * width), WIDE)])[0]
    laid = jnp.zeros((rows, parts, ranks, width), LOW)
    for dy, item in enumerate(found):
        for k in range(zn):
            rank = (grid.z - k) % zn * yn + (grid.y - dy) % yn
            laid = lax.dynamic_update_index_in_dim(laid, item[k].reshape(rows, parts, width), rank, 2)
    return laid.reshape(rows, -1).astype(WIDE)


class VectorGather:
    def __init__(self, grid, row):
        self.grid, self.block = grid, row[None]
        bits = (grid.rank_count * 4).bit_length() - 1
        self.bits = [0, *range(bits - (grid.z_count - 1).bit_length(), bits)]
        self.bits += [bit for bit in range(bits - 1, 0, -1) if bit not in self.bits]
        self.ways = list(self.bits)

    def begin(self):
        self.moving = self.grid.swap(self.block, self.ways.pop(0))

    def end(self):
        self.block = self.grid.pile(self.block, self.grid.wait(self.moving))

    def step(self):
        self.begin()
        self.end()

    def row_of(self, here, device):
        return sum(
            lax.rem(lax.rem(here // (1 << bit), 2) + (device >> bit) % 2, 2) * (1 << at)
            for at, bit in enumerate(self.bits)
        )

    def result(self):
        grid = self.grid
        here = (grid.rank * 2 + grid.x) * 2 + grid.c
        return self.block[jnp.stack([self.row_of(here, device) for device in range(grid.rank_count * 4)])]


def unfold_vectors(grid, gather, sizes, block_len, seqs):
    zn, yn, block = grid.z_count, grid.y_count, gather.block
    ranks, devices = grid.rank_count, grid.rank_count * 4
    cuts = [sum(sizes[:i]) for i in range(len(sizes) + 1)]
    slots = sizes[6] // 2
    head, hidden = sizes[2] * devices // (3 * ranks), sizes[4] * devices // ranks
    third = sizes[2] * devices // 3
    rows = 8 * block_len
    length = yn * rows
    half = ROT // 2
    lane = np.arange(128) % HEAD
    freqs = np.float32(ROPE_BASE) ** (-((lane % half).astype(np.float32) * np.float32(2.0 / ROT)))
    turned = (lane < ROT).astype(np.float32)
    sign = np.where(lane < half, -1.0, 1.0).astype(np.float32) * turned
    marks = jnp.asarray(np.stack([freqs.astype(np.float32), turned, sign]))

    def body(where_ref, block_ref, mark_ref, *refs):
        z, y, x, c = [where_ref[i] for i in range(4)]
        gain_ref, shift_ref, in_ref, out_ref, cos_ref, sin_ref, column_ref, row_ref = refs[:8]
        qkv_ref, up_ref = refs[8:]
        here_at = ((z * yn + y) * 2 + x) * 2 + c
        for device in range(devices):
            row = block_ref[pl.ds(gather.row_of(here_at, device), 1), :]
            item = [row[:, cuts[i] : cuts[i + 1]] for i in range(6)]
            here = [pl.ds(device * sizes[i], sizes[i]) for i in range(6)]
            gain_ref[:, here[0]] = item[0]
            shift_ref[:, here[1]] = item[1]
            qkv_ref[:, here[2]] = item[2]
            out_ref[:, here[3]] = item[3] + item[5]
            up_ref[:, here[4]] = item[4]
        rank = z * yn + y
        for part in range(3):
            start = pl.multiple_of(part * third + rank * head, 128)
            in_ref[:, part * head : (part + 1) * head] = qkv_ref[:, pl.ds(start, head)]
        in_ref[:, 3 * head :] = up_ref[:, pl.ds(pl.multiple_of(rank * hidden, 128), hidden)]

        def order_row(source):
            parts = [
                jnp.where(source == at, block_ref[pl.ds(gather.row_of(here_at, at * 4 * yn), 1), :], 0.0)
                for at in range(zn)
            ]
            return sum(parts)

        parity = lax.rem(z + x, 2)
        slot_at = lax.broadcasted_iota(jnp.int32, (1, slots), 1)
        tall = lax.broadcasted_iota(jnp.int32, (block_len, 128), 0).astype(WIDE)
        flat = lax.broadcasted_iota(jnp.int32, (1, block_len), 1).astype(WIDE)
        for i in range(seqs):
            row = order_row(lax.rem(z - 2 * i - parity + 2 * zn, zn))
            order = jnp.where(c == 0, row[:, cuts[6] : cuts[6] + slots], row[:, cuts[6] + slots : cuts[7]])
            for dy in range(yn):
                for near in range(4):
                    ctx = (lax.rem(y - dy + yn, yn) * 2 + lax.rem(x + near // 2, 2)) * 2 + lax.rem(c + near, 2)
                    for at in range(2):
                        value = jnp.sum(jnp.where(slot_at == 2 * ctx + at, order, 0.0), 1, keepdims=True) * block_len
                        place = value + tall
                        angle = place * mark_ref[0:1, :]
                        inside = (near * 2 + at) * block_len
                        here = pl.ds((dy * seqs + i) * rows + inside, block_len)
                        cos_ref[here, :] = jnp.where(mark_ref[1:2, :] > 0.0, jnp.cos(angle), 1.0)
                        sin_ref[here, :] = jnp.sin(angle) * mark_ref[2:3, :]
                        there = dy * rows + inside
                        column_ref[pl.ds(i * length + there, block_len), :] = place[:, :1]
                        row_ref[i, :, there : there + block_len] = value + flat

    wide = lambda *shape: jax.ShapeDtypeStruct(shape, WIDE)
    tokens = seqs * length
    vmem = pl.BlockSpec(memory_space=pltpu.VMEM)
    return pl.pallas_call(
        body,
        in_specs=[pl.BlockSpec(memory_space=pltpu.SMEM), vmem, vmem],
        out_specs=[vmem] * 8,
        out_shape=[
            wide(1, sizes[0] * devices), wide(1, sizes[1] * devices), wide(1, 3 * head + hidden),
            wide(1, sizes[3] * devices), wide(tokens, 128), wide(tokens, 128), wide(tokens, 1), wide(seqs, 1, length),
        ],
        scratch_shapes=[
            pltpu.VMEM((1, 3 * third), WIDE), pltpu.VMEM((1, hidden * ranks), WIDE),
        ],
        compiler_params=ROOM,
        cost_estimate=LIGHT,
    )(grid.where, block, marks)


class VectorSum:
    def __init__(self, grid, rows):
        self.grid, self.terms, self.bit = grid, [rows], 0

    def begin(self):
        grid, bit, yn = self.grid, self.bit, self.grid.y_count
        count, width = self.terms[0].shape

        def body(z, y, x, c, ins, outs):
            own = lax.rem((((z * yn + y) * 2 + x) * 2 + c) // (1 << bit), 2)
            for at in range(count // 2):
                for out, pick in zip(outs, (own, 1 - own)):
                    row = pl.ds(2 * at + pick, 1)
                    out[at : at + 1, :] = sum(ref[row, :] for ref in ins)

        kept, away = grid.local(body, self.terms, [jax.ShapeDtypeStruct((count // 2, width), WIDE)] * 2)
        self.kept, self.moving = kept, grid.swap(away, bit)
        self.bit += 1

    def end(self):
        self.terms = [self.kept, self.grid.wait(self.moving)]

    def result(self):
        while self.terms[0].shape[0] > 1:
            self.begin()
            self.end()
        return sum(self.terms)[0]


def fold_vectors(grid, gains, shifts, sums_qkv, sum_up, cotangent, sizes):
    devices, ranks, yn = grid.rank_count * 4, grid.rank_count, grid.y_count
    head, hidden = sums_qkv[0].shape[1], sum_up.shape[1]
    third = head * ranks
    chunks = (sizes[0], sizes[1], sizes[2], sizes[3], sizes[4])
    starts = [sum(chunks[:i]) for i in range(len(chunks))]
    count = len(gains)

    def body(where_ref, *refs):
        ins, out_ref, qkv_ref, up_ref = refs[:-3], refs[-3], refs[-2], refs[-1]
        rank = where_ref[0] * yn + where_ref[1]
        gain = sum(ref[...] for ref in ins[:count])
        shift = sum(ref[...] for ref in ins[count : 2 * count])
        grad = jnp.sum(ins[2 * count + 4][...].astype(WIDE), (0, 1))[None]
        qkv_ref[...] = jnp.zeros_like(qkv_ref)
        up_ref[...] = jnp.zeros_like(up_ref)
        for part in range(3):
            qkv_ref[:, pl.ds(pl.multiple_of(part * third + rank * head, 128), head)] = ins[2 * count + part][...]
        up_ref[:, pl.ds(pl.multiple_of(rank * hidden, 128), hidden)] = ins[2 * count + 3][...]
        for device in range(devices):
            for start, size, whole_row in zip(starts, chunks, (gain, shift, qkv_ref, grad, up_ref)):
                item = whole_row[:, device * size : (device + 1) * size]
                out_ref[device : device + 1, start : start + size] = item

    vmem = pl.BlockSpec(memory_space=pltpu.VMEM)
    inputs = [*gains, *shifts, *sums_qkv, sum_up, cotangent]
    return pl.pallas_call(
        body,
        in_specs=[pl.BlockSpec(memory_space=pltpu.SMEM)] + [vmem] * len(inputs),
        out_specs=vmem,
        out_shape=jax.ShapeDtypeStruct((devices, sum(chunks)), WIDE),
        scratch_shapes=[pltpu.VMEM((1, 3 * third), WIDE), pltpu.VMEM((1, hidden * ranks), WIDE)],
        compiler_params=ROOM,
        cost_estimate=cost(3.0),
    )(grid.where, *inputs)


def contract_last(left, right):
    return lax.dot_general(
        left, right, (((1,), (1,)), ((), ())), preferred_element_type=WIDE
    )


def contract_first(left, right):
    return lax.dot_general(
        left, right, (((0,), (0,)), ((), ())), preferred_element_type=WIDE
    )


def whole(array):
    return pl.BlockSpec(array.shape, lambda *at: (0,) * array.ndim)


def swap_halves(field):
    width = field.shape[-1]
    half = ROT // 2
    if width % 128 == 0:
        after = pltpu.roll(field, width - half, 1)
        before = pltpu.roll(field, half, 1)
    else:
        after = jnp.concatenate([field[:, half:], field[:, :half]], 1)
        before = jnp.concatenate([field[:, width - half :], field[:, : width - half]], 1)
    lane = lax.broadcasted_iota(jnp.int32, field.shape, 1) % HEAD
    return jnp.where(lane < half, after, before)


def turned_heads(query_ref, key_ref, value_ref, cos_ref, sin_ref):
    rows = (-1, cos_ref.shape[-1])
    cosine, sine = cos_ref[...].reshape(rows), sin_ref[...].reshape(rows)
    query = query_ref[...].reshape(rows)
    query_all = (query * cosine + swap_halves(query) * sine).astype(LOW)
    key = key_ref[...].reshape(rows)
    key_all = (key * cosine + swap_halves(key) * sine).astype(LOW)
    value_all = value_ref[...].reshape(rows).astype(LOW)
    return cosine, sine, query_all, key_all, value_all


def probability_of(query_low, key_low, allowed):
    scores = jnp.where(allowed, contract_last(query_low, key_low) * HEAD**-0.5, -1e30)
    weights = jnp.exp(scores - jnp.max(scores, -1, keepdims=True))
    return weights * (1.0 / jnp.sum(weights, -1, keepdims=True))


def forward_body(
    query_ref, key_ref, value_ref, cos_ref, sin_ref, column_ref, row_ref, mixed_ref, kept_ref
):
    _, _, query_all, key_all, value_all = turned_heads(query_ref, key_ref, value_ref, cos_ref, sin_ref)
    allowed = row_ref[...] <= column_ref[...]
    outs = []
    for at in range(query_all.shape[1] // HEAD):
        part = slice(at * HEAD, (at + 1) * HEAD)
        probability_low = probability_of(query_all[:, part], key_all[:, part], allowed).astype(LOW)
        kept_ref[at] = probability_low
        outs.append(jnp.dot(probability_low, value_all[:, part], preferred_element_type=WIDE))
    mixed_ref[...] = jnp.concatenate(outs, 1).astype(LOW).reshape(mixed_ref.shape)


def backward_body(
    query_ref, key_ref, value_ref, cos_ref, sin_ref, grad_ref, kept_ref, grad_query_ref, grad_key_ref, grad_value_ref
):
    cosine, sine, query_all, key_all, value_all = turned_heads(query_ref, key_ref, value_ref, cos_ref, sin_ref)
    grad_all = grad_ref[...].reshape(value_all.shape)
    scale = HEAD**-0.5
    outs = []
    for at in range(query_all.shape[1] // HEAD):
        part = slice(at * HEAD, (at + 1) * HEAD)
        query_low, key_low = query_all[:, part], key_all[:, part]
        value_low, grad_low = value_all[:, part], grad_all[:, part]
        probability_low = kept_ref[at]
        mixed = jnp.dot(probability_low, value_low, preferred_element_type=WIDE)
        delta = jnp.sum(grad_low.astype(WIDE) * mixed, -1, keepdims=True)
        grad_probability = contract_last(grad_low, value_low)
        grad_scores = (probability_low.astype(WIDE) * (grad_probability - delta)).astype(LOW)
        grad_value = contract_first(probability_low, grad_low)
        grad_query = jnp.dot(grad_scores, key_low, preferred_element_type=WIDE) * scale
        grad_key = contract_first(grad_scores, query_low) * scale
        outs.append((grad_query, grad_key, grad_value))
    grad_query, grad_key, grad_value = [jnp.concatenate(item, 1) for item in zip(*outs)]
    block = grad_query_ref.shape
    grad_query = grad_query * cosine - swap_halves(grad_query) * sine
    grad_key = grad_key * cosine - swap_halves(grad_key) * sine
    grad_query_ref[...] = grad_query.astype(LOW).reshape(block)
    grad_key_ref[...] = grad_key.astype(LOW).reshape(block)
    grad_value_ref[...] = grad_value.astype(LOW).reshape(block)


def attend(qkv, cosine, sine, yn, seqs, column=None, row=None, grad_attention=None, kept=None):
    backward = grad_attention is not None
    tokens, width = qkv.shape[0], qkv.shape[1] // 3
    lanes = min(128, width)
    length = tokens // seqs
    rows = length // yn
    block = (yn, None, rows, lanes)
    cut = lambda array: array.reshape(yn, seqs, rows, array.shape[-1])
    field = pl.BlockSpec(block, lambda s, h: (0, s, 0, h))
    table = pl.BlockSpec(block, lambda s, h: (0, s, 0, 0))
    square = pl.BlockSpec((None, lanes // HEAD, length, length), lambda s, h: (s, h, 0, 0))
    low = low_shape(yn, seqs, rows, width)
    if width % 128 == 0:
        thirds = [cut(qkv)] * 3
        blocks = [
            pl.BlockSpec(block, lambda s, h, part=part: (0, s, 0, part * (width // lanes) + h)) for part in range(3)
        ]
    else:
        thirds = [cut(qkv[:, part * width : (part + 1) * width]) for part in range(3)]
        blocks = [field] * 3
    inputs = [*thirds, cut(cosine[:, :lanes]), cut(sine[:, :lanes])]
    blocks = blocks + [table, table]
    if backward:
        body, inputs, blocks = backward_body, inputs + [cut(grad_attention), kept], blocks + [field, square]
        outs, out_blocks = [low] * 3, [field] * 3
    else:
        body, inputs = forward_body, inputs + [column, row]
        blocks = blocks + [
            pl.BlockSpec((length, 1), lambda s, h: (s, 0)),
            pl.BlockSpec((None, 1, length), lambda s, h: (s, 0, 0)),
        ]
        outs, out_blocks = [low, low_shape(seqs, width // HEAD, length, length)], [field, square]
    made = pl.pallas_call(
        body,
        grid=(seqs, width // lanes),
        in_specs=blocks,
        out_specs=out_blocks,
        out_shape=outs,
        compiler_params=pltpu.CompilerParams(vmem_limit_bytes=40 * 1024 * 1024),
        cost_estimate=cost(13.0),
    )(*inputs)
    return [item.reshape(tokens, width) if item.shape == low.shape else item for item in made]


def normalize(parts, gain_vec, shift_vec):
    span, width = parts[0].shape
    tile = min(span, 128)
    each = span // tile

    def body(*refs):
        step = pl.program_id(0)
        gain_ref, shift_ref, normed_ref, unit_ref = refs[len(parts) :]
        for at, ref in enumerate(refs[: len(parts)]):

            @pl.when(step // each == at)
            def _(ref=ref):
                inputs = ref[...].astype(WIDE)
                centre = inputs - jnp.mean(inputs, -1, keepdims=True)
                spread = jnp.mean(centre * centre, -1, keepdims=True)
                unit = centre * lax.rsqrt(spread + NORM_EPS)
                normed_ref[...] = (unit * gain_ref[...] + shift_ref[...]).astype(LOW)
                unit_ref[...] = unit.astype(LOW)

    block = (tile, width)
    clamp = lambda at: pl.BlockSpec(block, lambda t: (jnp.clip(t - at * each, 0, each - 1), 0))
    vector = pl.BlockSpec((1, width), lambda t: (0, 0))
    return pl.pallas_call(
        body,
        grid=(len(parts) * each,),
        in_specs=[clamp(at) for at in range(len(parts))] + [vector, vector],
        out_specs=[pl.BlockSpec(block, lambda t: (t, 0))] * 2,
        out_shape=[low_shape(len(parts) * span, width)] * 2,
        compiler_params=ROOM,
        cost_estimate=cost(8.0),
    )(*parts, gain_vec, shift_vec)


def bend(up):
    bent = jnp.tanh(GELU_SCALE * (up + GELU_CUBIC * up * up * up))
    slope = 0.5 * (1.0 + bent) + 0.5 * up * (1.0 - bent * bent) * GELU_SCALE * (1.0 + 3.0 * GELU_CUBIC * up * up)
    return (0.5 * up * (1.0 + bent)).astype(LOW), slope.astype(LOW)


def project(normed_low, w_in, bias, split):
    tokens, total = normed_low.shape[0], w_in.shape[1]
    if split % 256 or total % 256:
        made = jnp.dot(normed_low, w_in, preferred_element_type=WIDE) + bias
        return made[:, :split], *bend(made[:, split:])
    heads = split // 256

    def body(normed_ref, w_ref, bias_ref, qkv_ref, hidden_ref, slope_ref):
        step = pl.program_id(0)
        made = jnp.dot(normed_ref[...], w_ref[...], preferred_element_type=WIDE) + bias_ref[...]

        @pl.when(step < heads)
        def _():
            qkv_ref[...] = made

        @pl.when(step >= heads)
        def _():
            hidden_ref[...], slope_ref[...] = bend(made)

    late = pl.BlockSpec((tokens, 256), lambda t: (0, jnp.maximum(t - heads, 0)))
    return pl.pallas_call(
        body,
        grid=(total // 256,),
        in_specs=[
            whole(normed_low),
            pl.BlockSpec((w_in.shape[0], 256), lambda t: (0, t)),
            pl.BlockSpec((1, 256), lambda t: (0, t)),
        ],
        out_specs=[pl.BlockSpec((tokens, 256), lambda t: (0, jnp.minimum(t, heads - 1))), late, late],
        out_shape=[jax.ShapeDtypeStruct((tokens, split), WIDE)] + [low_shape(tokens, total - split)] * 2,
        compiler_params=ROOM,
        cost_estimate=cost(16.0),
    )(normed_low, w_in, bias)


def project_back(grad_out, w_out, slope, dense_rows):
    tokens, width = grad_out.shape
    if dense_rows % 256 or w_out.shape[0] % 256:
        return (
            contract_last(grad_out, w_out[:dense_rows]).astype(LOW),
            (contract_last(grad_out, w_out[dense_rows:]) * slope.astype(WIDE)).astype(LOW),
        )
    first = dense_rows // 256

    def body(grad_ref, w_ref, slope_ref, attention_ref, up_ref):
        step = pl.program_id(0)
        made = contract_last(grad_ref[...], w_ref[...])

        @pl.when(step < first)
        def _():
            attention_ref[...] = made.astype(LOW)

        @pl.when(step >= first)
        def _():
            up_ref[...] = (made * slope_ref[...].astype(WIDE)).astype(LOW)

    late = pl.BlockSpec((tokens, 256), lambda t: (0, jnp.maximum(t - first, 0)))
    return pl.pallas_call(
        body,
        grid=(w_out.shape[0] // 256,),
        in_specs=[whole(grad_out), pl.BlockSpec((256, width), lambda t: (t, 0)), late],
        out_specs=[pl.BlockSpec((tokens, 256), lambda t: (0, jnp.minimum(t, first - 1))), late],
        out_shape=[low_shape(tokens, dense_rows), low_shape(*slope.shape)],
        compiler_params=ROOM,
        cost_estimate=cost(10.0),
    )(grad_out, w_out, slope)


def out_part(attention_low, hidden_low, w_out, dy, rows, seqs):
    head, hidden, width = attention_low.shape[1], hidden_low.shape[1], w_out.shape[1]
    each = rows // seqs
    if head % 128:
        here = slice(dy * rows, (dy + 1) * rows)
        joined = jnp.concatenate([attention_low[here], hidden_low[here]], 1)
        made = jnp.dot(joined, w_out, preferred_element_type=WIDE).astype(LOW)
        return [made[i * each : (i + 1) * each] for i in range(seqs)]

    def body(attention_ref, hidden_ref, w_ref, *out_refs):
        made = jnp.dot(attention_ref[...], w_ref[:head], preferred_element_type=WIDE)
        made += jnp.dot(hidden_ref[...], w_ref[head:], preferred_element_type=WIDE)
        for i, out_ref in enumerate(out_refs):
            out_ref[...] = made[i * each : (i + 1) * each].astype(LOW)

    tile = min(width, 512)
    return pl.pallas_call(
        body,
        grid=(width // tile,),
        in_specs=[
            pl.BlockSpec((rows, head), lambda t: (dy, 0)),
            pl.BlockSpec((rows, hidden), lambda t: (dy, 0)),
            pl.BlockSpec((w_out.shape[0], tile), lambda t: (0, t)),
        ],
        out_specs=[pl.BlockSpec((each, tile), lambda t: (0, t))] * seqs,
        out_shape=[low_shape(each, width)] * seqs,
        compiler_params=ROOM,
        cost_estimate=cost(150.0),
    )(attention_low, hidden_low, w_out)


def in_part(grads, w_in, unit_low, dy, rows, seqs):
    widths = [item.shape[1] for item in grads]
    starts = [sum(widths[:i]) for i in range(len(widths))]
    width = w_in.shape[0]
    each = rows // seqs
    if widths[0] % 128:
        here = slice(dy * rows, (dy + 1) * rows)
        made = contract_last(jnp.concatenate([item[here] for item in grads], 1), w_in)
        sums = [jnp.sum(item, 0, keepdims=True) for item in (made * unit_low[here].astype(WIDE), made)]
        return [made[i * each : (i + 1) * each].astype(LOW) for i in range(seqs)], *sums

    def body(*refs):
        w_ref, unit_ref, *out_refs, gain_ref, shift_ref = refs[len(grads) :]
        made = None
        for ref, start, size in zip(refs, starts, widths):
            term = contract_last(ref[...], w_ref[:, start : start + size])
            made = term if made is None else made + term
        for i, out_ref in enumerate(out_refs):
            out_ref[...] = made[i * each : (i + 1) * each].astype(LOW)
        gain_ref[...] = jnp.sum(made * unit_ref[...].astype(WIDE), 0, keepdims=True)
        shift_ref[...] = jnp.sum(made, 0, keepdims=True)

    tile = min(width, 512)
    vector = pl.BlockSpec((1, tile), lambda t: (0, t))
    *made, gain, shift = pl.pallas_call(
        body,
        grid=(width // tile,),
        in_specs=[pl.BlockSpec((rows, size), lambda t: (dy, 0)) for size in widths]
        + [
            pl.BlockSpec((tile, w_in.shape[1]), lambda t: (t, 0)),
            pl.BlockSpec((rows, tile), lambda t: (dy, t)),
        ],
        out_specs=[pl.BlockSpec((each, tile), lambda t: (0, t))] * seqs + [vector, vector],
        out_shape=[low_shape(each, width)] * seqs + [jax.ShapeDtypeStruct((1, width), WIDE)] * 2,
        compiler_params=ROOM,
        cost_estimate=cost(7.0),
    )(*grads, w_in, unit_low)
    return made, gain, shift


def rotary_tables(places):
    lane = jnp.arange(128, dtype=jnp.int32) % HEAD
    half = ROT // 2
    freqs = jnp.asarray(ROPE_BASE, WIDE) ** (-((lane % half).astype(WIDE) * (2.0 / ROT)))
    angles = places.astype(WIDE)[:, None] * freqs
    turned = (lane < ROT)[None, :]
    sign = jnp.where(lane < half, -1.0, 1.0)
    return jnp.where(turned, jnp.cos(angles), 1.0), jnp.where(turned, jnp.sin(angles) * sign, 0.0)


def unfold_rows(grid, gathered, sizes, block_len, group_seqs):
    zn, yn, ranks = grid.z_count, grid.y_count, grid.rank_count
    cuts = [sum(sizes[:i]) for i in range(len(sizes) + 1)]
    gain_full, shift_full, bias_qkv, bias_dense, bias_up, bias_down = [
        gathered[:, cuts[i] : cuts[i + 1]].reshape(-1).astype(WIDE) for i in range(6)
    ]
    orders = gathered[:: grid.ctx_count, cuts[6] :].reshape(zn, 2, -1).astype(jnp.int32)

    ctx_from = jnp.stack(
        [
            (((grid.y - dy) % yn) * 2 + (grid.x ^ dx)) * 2 + (grid.c ^ dc)
            for dy in range(yn)
            for dx in range(2)
            for dc in range(2)
        ]
    )
    z_from = jnp.stack([(grid.z - 2 * i - grid.parity) % zn for i in range(group_seqs)])
    own_orders = lax.dynamic_index_in_dim(orders, grid.c, 1, keepdims=False)[z_from]
    slots = (ctx_from[:, None] * 2 + jnp.arange(2)).reshape(-1)
    places = own_orders[:, slots].reshape(group_seqs, yn, -1).swapaxes(0, 1)
    places = (places[..., None] * block_len + jnp.arange(block_len)).reshape(-1)
    cosine, sine = rotary_tables(places)


    bias_in = jnp.concatenate(
        [
            lax.dynamic_index_in_dim(bias_qkv.reshape(3, ranks, -1), grid.rank, 1, keepdims=False).reshape(-1),
            place(bias_up.reshape(ranks, -1), grid.rank),
        ]
    )
    column = places.reshape(yn, group_seqs, -1).swapaxes(0, 1).reshape(-1).astype(WIDE)
    return (
        gain_full[None], shift_full[None], bias_in[None], (bias_dense + bias_down)[None], cosine, sine,
        column[:, None], column.reshape(group_seqs, 1, -1),
    )


def fold_rows(grid, gain, shift, sums_qkv, sum_up, cotangent):
    ranks, devices = grid.rank_count, grid.rank_count * 4

    def laid(part, count):
        whole_rows = jnp.zeros((count, ranks, part.shape[-1]), WIDE)
        whole_rows = lax.dynamic_update_index_in_dim(whole_rows, part, grid.rank, 1)
        return whole_rows.reshape(devices, -1)

    return jnp.concatenate(
        [
            gain.reshape(devices, -1),
            shift.reshape(devices, -1),
            laid(jnp.concatenate(sums_qkv, 0), 3),
            jnp.sum(cotangent.astype(WIDE), (0, 1)).reshape(devices, -1),
            laid(sum_up, 1),
        ],
        1,
    )


def on_device(
    tokens, block_order, ln_gain, ln_bias, w_qkv, b_qkv, w_dense, b_dense, w_fc1, b_fc1, w_fc2, b_fc2, cotangent,
):
    grid = Grid()
    seqs, span, model_width = tokens.shape
    zn, yn, ranks = grid.z_count, grid.y_count, grid.rank_count
    device_count = ranks * 4
    length = span * grid.ctx_count
    block_len = span // 2
    group_seqs = zn // 2
    head_width = model_width // ranks

    split = 3 * head_width
    dense_rows = 4 * w_dense.shape[0]
    rows = group_seqs * length // yn
    seq_rows = length // yn
    last = group_seqs - 1

    def ordered(spreads):
        return [spreads[i].parts[dy] for dy in range(yn) for i in range(group_seqs)]

    def ordered(spreads):
        return [spreads[i].parts[dy] for dy in range(yn) for i in range(group_seqs)]

    def rows_of(array, i):
        return array[i * seq_rows : (i + 1) * seq_rows]

    def across_x(ks):
        own = near[ks[0]][None] if len(ks) == 1 else grid.pile(*[near[k][None] for k in ks])
        return ks, own, grid.start(own, x=1)

    def both_columns(group):
        ks, own, moving = group
        return ks, grid.pile(own[None], grid.wait(moving)[None])

    away, own_tokens, own_cotangent = part_cores(grid, tokens, cotangent)
    moving = grid.start(away, c=1)
    down_moving = grid.start(w_fc2, x=1)
    others = grid.wait(moving)
    ring = Ring(grid, grid.pile(own_tokens, others[:span]))
    ring.begin(1)
    ahead, across = cut_columns(grid, *grid.after((w_qkv, w_fc1)))
    across = [grid.start(part, y=dy + 1) for dy, part in enumerate(across)]
    vectors = (ln_gain, ln_bias, b_qkv, b_dense, b_fc1, b_fc2, block_order.reshape(-1))
    sizes = [item.shape[0] for item in vectors]
    vectors = jnp.concatenate([item.astype(WIDE) for item in grid.after(vectors)])
    gather = VectorGather(grid, vectors)
    gather.begin()
    down_moving = grid.wait(down_moving)
    dense_moving = grid.start(w_dense, x=1)
    gather.end()
    ring.end()
    dense_moving = grid.wait(dense_moving)
    gather.begin()
    spreads = [Spread(grid, ring.pair(0))]
    ring.begin(2)
    across = grid.wait(across)
    gather.end()

    def pack(z, y, x, c, ins, outs):
        for k in range(zn):
            outs[k][0] = ins[k][...]
            for dy in range(1, yn):
                outs[k][dy] = ins[zn + dy - 1][k]

    near = grid.local(pack, [*ahead, *across], [low_shape(yn, *ahead[0].shape)] * zn)
    near = dict(enumerate(near))
    near[zn - 1] = grid.start(near[zn - 1], z=-1)
    gather.begin()
    spreads[0].end_x()
    spreads[0].begin_y()
    group_own = across_x([0])
    ring.end()
    near[zn - 1] = grid.wait(near[zn - 1])
    gather.end()
    ring.finish()
    spreads += [Spread(grid, ring.pair(i)) for i in range(1, group_seqs)]
    rest = [k for k in grid.steps() if k != zn - 1]
    moving = {k: grid.start(near[k], z=k) for k in rest}
    gather.begin()

    def stack_out(z, y, x, c, ins, outs):
        for at in range(2):
            dense = ins[2 * at].shape[0]
            outs[0][at, :dense] = ins[2 * at][...]
            outs[0][at, dense:] = ins[2 * at + 1][...]

    out_rows = grid.local(
        stack_out,
        grid.after([w_dense, w_fc2, dense_moving, down_moving]),
        [low_shape(2, w_dense.shape[0] + w_fc2.shape[0], model_width)],
    )[0]
    group_own = both_columns(group_own)
    for spread in spreads[1:]:
        spread.end_x()
    spreads[1].begin_y()
    group_far = across_x([zn - 1])
    spreads[0].end_y()
    gather.end()
    near.update(grid.wait(moving))
    met_grad = grid.pile(own_cotangent, others[span:])
    ring = Ring(grid, met_grad)
    ring.begin(1)
    group_far = both_columns(group_far)
    gather.begin()
    group_rest = across_x(rest)
    gather.end()

    def beside(z, y, x, c, ins, outs):
        for at, ref in enumerate(ins):
            outs[0][:, at : at + 1] = ref[...]

    first = group_own[0] + group_far[0]
    first_rows = grid.local(beside, [group_own[1], group_far[1]], [low_shape(2, 2, *group_own[1].shape[2:])])[0]
    first_moving = grid.start(first_rows, c=1)
    out_moving = grid.start(out_rows, c=1)
    while gather.ways:
        gather.step()
    if head_width % 128 == 0:
        unfolded = grid.hold(unfold_vectors(grid, gather, sizes, block_len, group_seqs))
    else:
        unfolded = unfold_rows(grid, gather.result(), sizes, block_len, group_seqs)
    gain_full, shift_full, bias_in, bias_out, cosine, sine, column, row = unfolded
    spreads[1].end_y()
    for spread in spreads[2:]:
        spread.begin_y()
        spread.end_y()
    normed_low, unit_low = grid.hold(normalize(ordered(spreads), gain_full, shift_full))
    first_moving = grid.wait(first_moving)
    group_rest = both_columns(group_rest)
    out_moving = grid.wait(out_moving)
    rest_moving = grid.start(group_rest[1], c=1)
    w_out = grid.hold(join_out(grid, *grid.after((out_rows, out_moving)), w_dense.shape[0]))
    ring.end()
    grads = [Spread(grid, ring.pair(0))]
    ring.begin(2)
    rest_moving = grid.wait(rest_moving)
    w_in = grid.hold(join_columns(grid, [(first, first_rows, first_moving), (*group_rest, rest_moving)]))
    grads[0].end_x()
    grads[0].begin_y()
    grid.page()
    ring.end()
    ring.finish()
    grads += [Spread(grid, ring.pair(i)) for i in range(1, group_seqs)]

    qkv, hidden_low, slope = grid.hold(project(grid.after(normed_low), w_in, bias_in, split))
    grid.pages = False
    for spread in grads[1:]:
        spread.end_x()
    grads[1].begin_y()
    attention_low, kept = grid.hold(attend(grid.after(qkv), cosine, sine, yn, group_seqs, column=column, row=row))
    out_parts = {}
    for dy in range(yn - 1, -1, -1):
        if dy == 0:
            grads[0].end_y()
        out_parts[dy] = grid.hold(out_part(grid.after(attention_low), hidden_low, w_out, dy, rows, group_seqs))
    grads[1].end_y()
    for spread in grads[2:]:
        spread.begin_y()
        spread.end_y()

    out_sums = {i: TokenSum(grid, out_parts[yn - 1][i], yn - 1) for i in range(last, -1, -1)}
    grad_out = grid.pile(*grid.after(ordered(grads)))
    grad_attention_low, grad_up_low = grid.hold(project_back(grad_out, w_out, slope, dense_rows))

    def finish_y(sums, parts, i):
        for dy in range(yn - 2, -1, -1):
            sums[i].more(parts[dy][i])

    grads_qkv = grid.hold(
        attend(grid.after(qkv), cosine, sine, yn, group_seqs, grad_attention=grad_attention_low, kept=kept)
    )
    grads_in = [*grads_qkv, grad_up_low]
    finish_y(out_sums, out_parts, last)
    out_sums[last].begin_x()
    in_parts, gain_parts, shift_parts = {}, {}, {}

    def make_in_part(dy):
        in_parts[dy], gain_parts[dy], shift_parts[dy] = grid.hold(
            in_part(grid.after(grads_in), w_in, unit_low, dy, rows, group_seqs)
        )

    make_in_part(yn - 1)
    in_sums = {last: TokenSum(grid, in_parts[yn - 1][last], yn - 1)}
    up_kept, up_away, (sum_up,) = grid.hold(halves_in(grid, grid.after(normed_low), [grad_up_low]))
    up_moving = grid.start(up_away, c=1)
    out_ring = RingSum(grid)
    out_pair = out_sums[last].end_x()
    for i in range(last - 1, 0, -1):
        finish_y(out_sums, out_parts, i)
        out_sums[i].begin_x()
        out_ring.pieces[2 * i], out_ring.pieces[2 * i + 1] = out_sums[i].end_x()
    finish_y(out_sums, out_parts, 0)
    grid.turn()
    out_ring.pieces[2 * last], out_ring.pieces[2 * last + 1] = out_pair
    out_ring.begin_far()
    out_sums[0].begin_x()
    for dy in range(yn - 2, -1, -1):
        make_in_part(dy)
    up_moving = grid.wait(up_moving)
    up_kept, up_away = grid.hold(halve_columns(grid, up_kept, up_moving))
    up_moving = grid.start(up_away, x=1)
    finish_y(in_sums, in_parts, last)
    for i in range(last - 1, -1, -1):
        in_sums[i] = TokenSum(grid, in_parts[yn - 1][i], yn - 1)
    qkv_kept, qkv_away, sums_qkv = grid.hold(halves_in(grid, grid.after(normed_low), grads_qkv))
    qkv_moving = grid.start(qkv_away, c=1)
    out_ring.pieces[0], out_ring.pieces[1] = out_sums[0].end_x()
    out_ring.end_far()
    out_ring.begin_near()
    in_sums[last].begin_x()
    up_moving = grid.wait(up_moving)
    out_ring.end_near()
    up_return = ColumnReturn(grid, up_kept, up_moving)
    in_ring = RingSum(grid)
    finish_y(in_sums, in_parts, 0)
    in_sums[0].begin_x()
    out_kept, out_away = grid.hold(halves_out(grid, *grid.after((attention_low, hidden_low)), grad_out))
    in_ring.pieces[2 * last], in_ring.pieces[2 * last + 1] = in_sums[last].end_x()
    for i in range(last - 1, 0, -1):
        finish_y(in_sums, in_parts, i)
        in_sums[i].begin_x()
        in_ring.pieces[2 * i], in_ring.pieces[2 * i + 1] = in_sums[i].end_x()
    up_return.end_z()
    in_ring.begin_far()
    up_return.begin_y()
    in_ring.pieces[0], in_ring.pieces[1] = in_sums[0].end_x()
    out_moving = grid.start(out_away, c=1)
    grid.turn()
    projected = out_ring.end()
    qkv_moving = grid.wait(qkv_moving)
    qkv_kept, qkv_away = grid.hold(halve_columns(grid, qkv_kept, qkv_moving))
    qkv_moving = grid.start(qkv_away, x=1)
    if head_width % 128 == 0:
        sums = fold_vectors(
            grid, list(gain_parts.values()), list(shift_parts.values()), sums_qkv, sum_up, cotangent, sizes
        )
    else:
        sums = fold_rows(
            grid, sum(gain_parts.values()), sum(shift_parts.values()), sums_qkv, sum_up, cotangent
        )
    sums = VectorSum(grid, grid.hold(sums))
    sums.begin()
    up_found = up_return.end()
    qkv_moving = grid.wait(qkv_moving)
    sums.end()
    sums.begin()
    out_kept, out_away = grid.hold(halve_columns(grid, out_kept, grid.wait(out_moving)))
    sums.end()
    sums.begin()
    out_moving = grid.start(out_away, x=1)
    in_ring.end_far()
    in_ring.begin_near()
    qkv_return = ColumnReturn(grid, qkv_kept, qkv_moving)
    sums.end()
    grad_w_up = grid.hold(lay_columns(grid, up_found, 1))
    in_ring.end_near()
    sums.begin()
    grad_normed = in_ring.end()
    token_grad = grid.hold(finish_grad(grid, tokens, cotangent, *grad_normed, gain_full))
    qkv_return.end_z()
    qkv_return.begin_y()
    sums.end()
    sums.begin()
    output = grid.hold(finish_output(grid, grid.after(tokens), *projected, bias_out))
    sums.end()
    qkv_found = qkv_return.end()
    out_moving = grid.wait(out_moving)
    sums = sums.result()
    grad_w_out = (out_kept.astype(WIDE) + out_moving.astype(WIDE))[0]

    grad_w_qkv = lay_columns(grid, qkv_found, 3)

    grad_gain, grad_shift = sums[: sizes[0]], sums[sizes[0] : 2 * sizes[0]]
    rest = sums[2 * sizes[0] :]
    grad_bias_qkv = rest[: sizes[2]]
    grad_bias_out = rest[sizes[2] : sizes[2] + sizes[3]]
    grad_bias_up = rest[sizes[2] + sizes[3] :]
    grad_w_dense = grad_w_out[: w_dense.shape[0]]
    grad_w_down = grad_w_out[w_dense.shape[0] :]
    return (
        output, token_grad, grad_gain, grad_shift, grad_w_qkv, grad_bias_qkv,
        grad_w_dense, grad_bias_out, grad_w_up, grad_bias_up, grad_w_down, grad_bias_out,
    )


def solution(mesh):
    rows = P(("dp", "ctx"), None)
    vector = P(("dp", "ctx"))
    spread = P("dp", "ctx", None)
    in_specs = (
        spread, P("dp", None), vector, vector, rows, vector, rows, vector, rows, vector, rows, vector, spread,
    )
    out_specs = (
        spread, spread, vector, vector, rows, vector, rows, vector, rows, vector, rows, vector,
    )
    return jax.shard_map(on_device, mesh=mesh, in_specs=in_specs, out_specs=out_specs, check_vma=False)
```

```python
from functools import partial

import jax
import jax.numpy as jnp
import numpy as np
from jax import lax
from jax.experimental import pallas as pl
from jax.experimental.pallas import tpu as pltpu
from jax.sharding import PartitionSpec as P

HEAD = 64
ROT = 32
ROPE_BASE = 10000
NORM_EPS = 1e-05
BOTH = ("dp", "ctx")
LOW = jnp.bfloat16
WIDE = jnp.float32
GELU_SCALE = 0.7978845608028654
GELU_CUBIC = 0.044715


COST_SCALE = 20_000_000


LIGHT = pl.CostEstimate(flops=1024, bytes_accessed=1024, transcendentals=1)


def cost(micros):
    return pl.CostEstimate(flops=int(micros * COST_SCALE), bytes_accessed=1024, transcendentals=1)
ROOM = pltpu.CompilerParams(vmem_limit_bytes=48 * 1024 * 1024)


def low_shape(*shape):
    return jax.ShapeDtypeStruct(shape, LOW)


def place(array, index):
    return lax.dynamic_index_in_dim(array, index, 0, keepdims=False)


def turn_page(token):
    def body(token_ref, copy_ref):
        copy_ref[...] = token_ref[...]

    return pl.pallas_call(
        body,
        out_shape=jax.ShapeDtypeStruct(token.shape, token.dtype),
        cost_estimate=pl.CostEstimate(flops=100_000_000_000, bytes_accessed=8192, transcendentals=0),
    )(token)


class Grid:
    def __init__(self):
        self.z_count = lax.axis_size("dp")
        self.ctx_count = lax.axis_size("ctx")
        self.y_count = self.ctx_count // 4
        ctx = lax.axis_index("ctx")
        self.z = lax.axis_index("dp")
        self.y = ctx // 4
        self.x = (ctx // 2) % 2
        self.c = ctx % 2
        self.where = jnp.stack([self.z, self.y, self.x, self.c]).astype(jnp.int32)
        self.rank = self.z * self.y_count + self.y
        self.rank_count = self.z_count * self.y_count
        self.parity = (self.z + self.x) % 2
        self.token = jnp.zeros((8, 128), WIDE)
        self.started, self.pages = False, True

    def steps(self):
        order = sorted(range(1, self.z_count), key=lambda k: (min(k, self.z_count - k), k))
        return order

    def after(self, value):
        self.page()
        return lax.optimization_barrier((value, self.token))[0]

    def hold(self, value):
        self.page()
        value, self.token = lax.optimization_barrier((value, self.token))
        return value

    wait = hold

    def page(self):
        if self.started and self.pages:
            self.token = turn_page(self.token)
        self.started = False

    def swap(self, value, bit):
        pairs = [(device, device ^ (1 << bit)) for device in range(self.rank_count * 4)]
        return self.send(value, pairs)

    def turn(self):
        self.token = turn_page(self.token)
        self.started = False

    def start(self, value, z=0, y=0, x=0, c=0):
        pairs = []
        for z_at in range(self.z_count):
            for y_at in range(self.y_count):
                for x_at in range(2):
                    for c_at in range(2):
                        z_to = (z_at + z) % self.z_count
                        y_to = (y_at + y) % self.y_count
                        source = ((z_at * self.y_count + y_at) * 2 + x_at) * 2 + c_at
                        target = ((z_to * self.y_count + y_to) * 2 + (x_at ^ x)) * 2 + (c_at ^ c)
                        pairs.append((source, target))
        return self.send(value, pairs)

    def send(self, value, pairs):
        value = lax.optimization_barrier((value, self.token))[0]
        self.started = True
        return lax.ppermute(value, BOTH, pairs)

    def local(self, body, inputs, outs):
        count = len(inputs)

        def whole_body(where_ref, *refs):
            body(*[where_ref[i] for i in range(4)], refs[:count], refs[count:])

        vmem = pl.BlockSpec(memory_space=pltpu.VMEM)
        return pl.pallas_call(
            whole_body,
            in_specs=[pl.BlockSpec(memory_space=pltpu.SMEM)] + [vmem] * count,
            out_specs=[vmem] * len(outs),
            out_shape=outs,
            compiler_params=ROOM,
            cost_estimate=cost(1.5),
        )(self.where, *inputs)

    def pile(self, *arrays):
        lengths = [item.shape[0] for item in arrays]
        starts = [sum(lengths[:i]) for i in range(len(lengths))]

        def body(z, y, x, c, ins, outs):
            for ref, start, length in zip(ins, starts, lengths):
                outs[0][start : start + length] = ref[...]

        shape = (sum(lengths), *arrays[0].shape[1:])
        return self.local(body, arrays, [jax.ShapeDtypeStruct(shape, arrays[0].dtype)])[0]


def mover(grid, plan, inputs, outs):
    count = len(inputs)

    def copies_of(where_ref, refs, sems):
        at = [where_ref[i] for i in range(4)]
        listed = plan(*at, refs[:count], refs[count:])
        return [pltpu.make_async_copy(source, target, sems.at[i]) for i, (source, target) in enumerate(listed)]

    def body(where_ref, *refs):
        copies = copies_of(where_ref, refs[:-1], refs[-1])
        for copy in copies:
            copy.start()
        for copy in copies:
            copy.wait()

    most = 4 * max(4, grid.rank_count)
    return pl.pallas_call(
        body,
        in_specs=[pl.BlockSpec(memory_space=pltpu.SMEM)] + [pl.BlockSpec(memory_space=pltpu.VMEM)] * count,
        out_specs=[pl.BlockSpec(memory_space=pltpu.HBM)] * len(outs),
        out_shape=outs,
        scratch_shapes=[pltpu.SemaphoreType.DMA((most,))],
        compiler_params=pltpu.CompilerParams(vmem_limit_bytes=24 * 1024 * 1024),
        cost_estimate=LIGHT,
    )(grid.where, *inputs)


def part_cores(grid, tokens, cotangent):
    span, width = tokens.shape[1:]

    def body(z, y, x, c, ins, outs):
        for at, ref in enumerate(ins):
            outs[0][at * span : (at + 1) * span] = ref[1 - c]
            outs[1 + at][...] = ref[c]

    shapes = [low_shape(2 * span, width), low_shape(span, width), low_shape(span, width)]
    return grid.local(body, [tokens, cotangent], shapes)


def pair_of(grid, even, odd):
    def body(z, y, x, c, ins, outs):
        swap = lax.rem(z + x, 2)
        for first in range(2):

            @pl.when(swap == first)
            def _(first=first):
                outs[0][...] = ins[first][...]
                outs[1][...] = ins[1 - first][...]

    return grid.local(body, [even, odd], [low_shape(*even.shape)] * 2)


class Ring:
    def __init__(self, grid, first):
        self.grid, self.pieces, self.moving = grid, {0: first}, {}

    def begin(self, r):
        zn = self.grid.z_count
        self.moving[r] = self.grid.start(self.pieces[r - 1], z=1)
        if zn - r > zn // 2:
            self.moving[zn - r] = self.grid.start(self.pieces[(zn - r + 1) % zn], z=-1)

    def end(self):
        self.pieces.update(self.grid.wait(self.moving))
        self.moving = {}

    def finish(self):
        for r in range(3, self.grid.z_count // 2 + 1):
            self.begin(r)
            self.end()

    def pair(self, i):
        return pair_of(self.grid, self.pieces[2 * i], self.pieces[2 * i + 1])


class Spread:
    def __init__(self, grid, pair):
        self.grid = grid
        self.keep, away = pair
        self.moving = grid.start(away, x=1)

    def end_x(self):
        self.parts = [self.grid.pile(self.keep, self.grid.wait(self.moving))]

    def begin_y(self):
        self.moving = self.grid.start(self.parts[-1], y=1)

    def end_y(self):
        self.parts.append(self.grid.wait(self.moving))
        for _ in range(2, self.grid.y_count):
            self.begin_y()
            self.parts.append(self.grid.wait(self.moving))


def sum_low(left, right):
    return (left.astype(WIDE) + right.astype(WIDE)).astype(LOW)


class TokenSum:
    def __init__(self, grid, part, dy):
        self.grid = grid
        self.moving = grid.start(part, y=-1)
        self.left = dy - 1

    def more(self, part):
        arrived = self.grid.wait(self.moving)
        if self.left:
            self.moving = self.grid.start(sum_low(part, arrived), y=-1)
            self.left -= 1
            return
        span = arrived.shape[0] // 2

        def body(z, y, x, c, ins, outs):
            for at in range(2):
                here = slice(at * span, (at + 1) * span)
                outs[at][...] = sum_low(ins[0][here], ins[1][here])

        self.kept, self.away = self.grid.local(body, [part, arrived], [low_shape(span, arrived.shape[1])] * 2)

    def begin_x(self):
        self.moving = self.grid.start(self.away, x=1)

    def end_x(self):
        return pair_of(self.grid, self.kept, self.grid.wait(self.moving))


class RingSum:
    def __init__(self, grid):
        self.grid, self.pieces = grid, {}

    def add(self, left, right):
        def body(z, y, x, c, ins, outs):
            outs[0][...] = sum_low(ins[0][...], ins[1][...])

        return self.grid.local(body, [left, right], [low_shape(*left.shape)])[0]

    def begin_far(self):
        grid, zn, pieces = self.grid, self.grid.z_count, self.pieces
        down, up = zn // 2, zn // 2 + 1
        while down > 2:
            arrived = grid.wait(grid.start(pieces[down], z=-1))
            down -= 1
            pieces[down] = self.add(pieces[down], arrived)
        while up < zn - 1:
            arrived = grid.wait(grid.start(pieces[up], z=1))
            up += 1
            pieces[up] = self.add(pieces[up], arrived)
        self.moving = grid.start(pieces[2], z=-1), grid.start(pieces[zn - 1], z=1)

    def end_far(self):
        self.down, self.up = self.grid.wait(self.moving)

    def begin_near(self):
        self.moving = self.grid.start(self.add(self.pieces[1], self.down), z=-1)

    def end_near(self):
        near = self.grid.wait(self.moving)
        span = near.shape[0] // 2

        def body(z, y, x, c, ins, outs):
            total = ins[0][...].astype(WIDE) + ins[1][...].astype(WIDE) + ins[2][...].astype(WIDE)
            outs[0][...] = total[:span]
            outs[1][...] = total[span:].astype(LOW)

        shapes = [jax.ShapeDtypeStruct((span, near.shape[1]), WIDE), low_shape(span, near.shape[1])]
        self.own, away = self.grid.local(body, [self.pieces[0], self.up, near], shapes)
        self.moving = self.grid.start(away, c=1)

    def end(self):
        return self.own, self.grid.wait(self.moving)


def finish_output(grid, tokens, own, other, bias_out):
    def body(z, y, x, c, ins, outs):
        for ref, at in ((ins[1], c), (ins[2], 1 - c)):
            outs[0][at] = (ins[0][at].astype(WIDE) + ref[...].astype(WIDE) + ins[3][...]).astype(LOW)

    return grid.local(body, [tokens, own, other, bias_out], [low_shape(*tokens.shape)])[0]


def finish_grad(grid, tokens, cotangent, own, other, gain_vec):
    def body(z, y, x, c, ins, outs):
        for ref, at in ((ins[2], c), (ins[3], 1 - c)):
            inputs = ins[0][at].astype(WIDE)
            centre = inputs - jnp.mean(inputs, -1, keepdims=True)
            turn = lax.rsqrt(jnp.mean(centre * centre, -1, keepdims=True) + NORM_EPS)
            unit = centre * turn
            scaled = ref[...].astype(WIDE) * ins[4][...]
            along = jnp.mean(scaled * unit, -1, keepdims=True)
            change = turn * (scaled - jnp.mean(scaled, -1, keepdims=True) - unit * along)
            outs[0][at] = (ins[1][at].astype(WIDE) + change).astype(LOW)

    return grid.local(body, [tokens, cotangent, own, other, gain_vec], [low_shape(*tokens.shape)])[0]


def cut_columns(grid, w_qkv, w_up):
    zn, yn, ranks = grid.z_count, grid.y_count, grid.rank_count
    rows, third, wide = w_qkv.shape[0], w_qkv.shape[1] // 3, w_up.shape[1]
    head, hidden = third // ranks, wide // ranks
    width = 3 * head + hidden
    outs = [low_shape(rows, width)] * zn + [low_shape(zn, rows, width)] * (yn - 1)

    def plan(z, y, x, c, ins, refs):
        copies = []
        for dy in range(yn):
            for k in range(zn):
                rank = lax.rem(z + k, zn) * yn + lax.rem(y + dy, yn)
                target = refs[k] if dy == 0 else refs[zn + dy - 1].at[k]
                for part in range(3):
                    start = pl.multiple_of(part * third + rank * head, 128)
                    copies.append((ins[0].at[:, pl.ds(start, head)], target.at[:, pl.ds(part * head, head)]))
                start = pl.multiple_of(rank * hidden, 128)
                copies.append((ins[1].at[:, pl.ds(start, hidden)], target.at[:, pl.ds(3 * head, hidden)]))
        return copies

    if head % 128 == 0:
        made = mover(grid, plan, [w_qkv, w_up], outs)
    else:
        heads = w_qkv.reshape(rows, 3, ranks, head)
        hiddens = w_up.reshape(rows, ranks, hidden)

        def block(k, dy):
            rank = (grid.z + k) % zn * yn + (grid.y + dy) % yn
            mine = lax.dynamic_index_in_dim(heads, rank, 2, keepdims=False).reshape(rows, 3 * head)
            return jnp.concatenate([mine, lax.dynamic_index_in_dim(hiddens, rank, 1, keepdims=False)], 1)

        made = [block(k, 0) for k in range(zn)] + [
            jnp.stack([block(k, dy) for k in range(zn)]) for dy in range(1, yn)
        ]
    return made[:zn], made[zn:]


def join_columns(grid, groups):
    zn, yn = grid.z_count, grid.y_count
    rows, width = groups[0][1].shape[-2:]
    flat = [item for group in groups for item in group[1:]]

    def body(where_ref, *refs):
        z, y, x, c = [where_ref[i] for i in range(4)]
        for at_group, group in enumerate(groups):
            for way in range(4):
                column, core = lax.rem(x + way % 2, 2), lax.rem(c + way // 2, 2)
                for at, k in enumerate(group[0]):
                    for dy in range(yn):
                        rank = lax.rem(z - k + zn, zn) * yn + lax.rem(y - dy + yn, yn)
                        start = pl.multiple_of(((rank * 2 + column) * 2 + core) * rows, rows)
                        refs[-1][pl.ds(start, rows)] = refs[2 * at_group + way // 2][way % 2, at, dy]

    vmem = pl.BlockSpec(memory_space=pltpu.VMEM)
    return pl.pallas_call(
        body,
        in_specs=[pl.BlockSpec(memory_space=pltpu.SMEM)] + [vmem] * len(flat),
        out_specs=vmem,
        out_shape=low_shape(zn * yn * 4 * rows, width),
        compiler_params=ROOM,
        cost_estimate=LIGHT,
    )(grid.where, *flat)


def join_out(grid, here, there, dense_rows):
    down_rows = here.shape[1] - dense_rows

    def plan(z, y, x, c, ins, outs):
        copies = []
        for way in range(4):
            source = ins[way // 2].at[way % 2]
            at = lax.rem(x + way % 2, 2) * 2 + lax.rem(c + way // 2, 2)
            first = pl.multiple_of(at * dense_rows, dense_rows)
            second = pl.multiple_of(4 * dense_rows + at * down_rows, dense_rows)
            copies.append((source.at[pl.ds(0, dense_rows)], outs[0].at[pl.ds(first, dense_rows)]))
            copies.append((source.at[pl.ds(dense_rows, down_rows)], outs[0].at[pl.ds(second, down_rows)]))
        return copies

    return mover(grid, plan, [here, there], [low_shape(4 * here.shape[1], here.shape[2])])[0]


def halves_in(grid, left, rights):
    tokens, ranks = left.shape[0], grid.rank_count
    widths = [item.shape[1] for item in rights]
    width = sum(widths)
    quad = left.shape[1] // ranks
    rows = quad // 4
    sums = [jax.ShapeDtypeStruct((1, size), WIDE) for size in widths]
    if quad % 128:
        made = contract_first(left, jnp.concatenate(rights, 1)).astype(LOW).reshape(ranks, 2, 2, rows, width)
        pick = lambda index: lax.dynamic_index_in_dim(made, index, 2, keepdims=False)
        return pick(grid.c), pick(1 - grid.c), [jnp.sum(item.astype(WIDE), 0, keepdims=True) for item in rights]
    starts = [sum(widths[:i]) for i in range(len(widths))]

    def body(where_ref, left_ref, *refs):
        core = where_ref[3]
        ins, (kept_ref, away_ref, *sum_refs), made_ref = refs[: len(rights)], refs[len(rights) : -1], refs[-1]
        for ref, start, size in zip(ins, starts, widths):
            made_ref[:, start : start + size] = contract_first(left_ref[...], ref[...]).astype(LOW)
        for column in range(2):
            for out_ref, at in ((kept_ref, core), (away_ref, 1 - core)):
                start = pl.multiple_of((2 * column + at) * rows, rows)
                out_ref[column] = made_ref[pl.ds(start, rows)]

        @pl.when(pl.program_id(0) == 0)
        def _():
            for ref, sum_ref in zip(ins, sum_refs):
                sum_ref[...] = jnp.sum(ref[...].astype(WIDE), 0, keepdims=True)

    half = pl.BlockSpec((None, 2, rows, width), lambda t: (t, 0, 0, 0))
    made = pl.pallas_call(
        body,
        grid=(ranks,),
        in_specs=[pl.BlockSpec(memory_space=pltpu.SMEM), pl.BlockSpec((tokens, quad), lambda t: (0, t))]
        + [whole(item) for item in rights],
        out_specs=[half, half] + [whole(item) for item in sums],
        out_shape=[low_shape(ranks, 2, rows, width)] * 2 + sums,
        scratch_shapes=[pltpu.VMEM((quad, width), LOW)],
        compiler_params=ROOM,
        cost_estimate=cost(8.0),
    )(grid.where, left, *rights)
    return made[0], made[1], made[2:]


def halves_out(grid, attention_low, hidden_low, grad_out):
    tokens, width = grad_out.shape
    dense, down = attention_low.shape[1], hidden_low.shape[1]
    rows = (dense // 4, down // 4)
    shape = low_shape(1, 2, sum(rows), width)
    if dense % 128 or down % 512:
        made = [
            contract_first(item, grad_out).astype(LOW).reshape(2, 2, -1, width) for item in (attention_low, hidden_low)
        ]
        pick = lambda index: jnp.concatenate(
            [lax.dynamic_index_in_dim(item, index, 1, keepdims=False) for item in made], 1
        )[None]
        return pick(grid.c), pick(1 - grid.c)

    def body(where_ref, dense_ref, down_ref, grad_ref, kept_ref, away_ref, made_ref):
        core, step = where_ref[3], pl.program_id(0)

        @pl.when(step == 0)
        def _():
            made_ref[...] = contract_first(dense_ref[...], grad_ref[...]).astype(LOW)
            for column in range(2):
                for out_ref, at in ((kept_ref, core), (away_ref, 1 - core)):
                    start = pl.multiple_of((2 * column + at) * rows[0], rows[0])
                    out_ref[0, column, : rows[0]] = made_ref[pl.ds(start, rows[0])]

        for quarter in range(4):
            for out_ref, at in ((kept_ref, core), (away_ref, 1 - core)):

                @pl.when((step == quarter + 1) & (at == quarter % 2))
                def _(out_ref=out_ref, quarter=quarter):
                    made = contract_first(down_ref[...], grad_ref[...]).astype(LOW)
                    out_ref[0, quarter // 2, rows[0] :] = made

    return pl.pallas_call(
        body,
        grid=(5,),
        in_specs=[
            pl.BlockSpec(memory_space=pltpu.SMEM),
            whole(attention_low),
            pl.BlockSpec((tokens, rows[1]), lambda t: (0, jnp.maximum(t - 1, 0))),
            whole(grad_out),
        ],
        out_specs=[whole(shape)] * 2,
        out_shape=[shape] * 2,
        scratch_shapes=[pltpu.VMEM((dense, width), LOW)],
        compiler_params=ROOM,
        cost_estimate=cost(11.0),
    )(grid.where, attention_low, hidden_low, grad_out)


def halve_columns(grid, kept, arrived):
    count, _, rows, width = kept.shape

    def body(where_ref, kept_ref, arrived_ref, here_ref, there_ref):
        column = where_ref[2]
        for ref, at in ((here_ref, column), (there_ref, 1 - column)):
            ref[...] = sum_low(kept_ref[at], arrived_ref[at])

    both = pl.BlockSpec((None, 2, rows, width), lambda t: (t, 0, 0, 0))
    one = pl.BlockSpec((None, rows, width), lambda t: (t, 0, 0))
    return pl.pallas_call(
        body,
        grid=(count,),
        in_specs=[pl.BlockSpec(memory_space=pltpu.SMEM), both, both],
        out_specs=[one, one],
        out_shape=[low_shape(count, rows, width)] * 2,
        compiler_params=ROOM,
        cost_estimate=cost(4.5),
    )(grid.where, kept, arrived)


class ColumnReturn:
    def __init__(self, grid, kept, arrived):
        zn, yn = grid.z_count, grid.y_count
        self.grid, self.shape = grid, kept.shape[1:]

        def body(z, y, x, c, ins, outs):
            for k in range(zn):
                for at in range(yn):
                    rank = lax.rem(z + k, zn) * yn + at
                    outs[k][at] = sum_low(ins[0][rank], ins[1][rank])

        self.cut = grid.local(body, [kept, arrived], [low_shape(yn, *self.shape)] * zn)

    def begin_z(self):
        self.by_z = {0: self.cut[0]}
        self.moving = {k: self.grid.start(self.cut[k], z=k) for k in self.grid.steps()}

    def end_z(self):
        grid, zn, yn = self.grid, self.grid.z_count, self.grid.y_count
        self.by_z.update(grid.wait(self.moving))

        def body(z, y, x, c, ins, outs):
            for dy in range(yn):
                for k in range(zn):
                    outs[dy][k] = ins[k][lax.rem(y + dy, yn)]

        self.cut = grid.local(body, [self.by_z[k] for k in range(zn)], [low_shape(zn, *self.shape)] * yn)

    def begin_y(self):
        self.moving = [self.grid.start(self.cut[dy], y=dy) for dy in range(1, self.grid.y_count)]

    def end(self):
        return [self.cut[0], *self.grid.wait(self.moving)]


def lay_columns(grid, found, parts):
    zn, yn, ranks = grid.z_count, grid.y_count, grid.rank_count
    rows, width = found[0].shape[1:]
    width = width // parts

    if width % 128 == 0:

        def body(z, y, x, c, ins, outs):
            for dy, ref in enumerate(ins):
                for k in range(zn):
                    rank = lax.rem(z - k + zn, zn) * yn + lax.rem(y - dy + yn, yn)
                    for part in range(parts):
                        start = pl.multiple_of((part * ranks + rank) * width, 128)
                        item = ref[k, :, part * width : (part + 1) * width]
                        outs[0][:, pl.ds(start, width)] = item.astype(WIDE)

        return grid.local(body, found, [jax.ShapeDtypeStruct((rows, parts * ranks * width), WIDE)])[0]
    laid = jnp.zeros((rows, parts, ranks, width), LOW)
    for dy, item in enumerate(found):
        for k in range(zn):
            rank = (grid.z - k) % zn * yn + (grid.y - dy) % yn
            laid = lax.dynamic_update_index_in_dim(laid, item[k].reshape(rows, parts, width), rank, 2)
    return laid.reshape(rows, -1).astype(WIDE)


class VectorGather:
    def __init__(self, grid, row):
        self.grid, self.block = grid, row[None]
        bits = (grid.rank_count * 4).bit_length() - 1
        self.bits = [0, *range(bits - (grid.z_count - 1).bit_length(), bits)]
        self.bits += [bit for bit in range(bits - 1, 0, -1) if bit not in self.bits]
        self.ways = list(self.bits)

    def begin(self):
        self.moving = self.grid.swap(self.block, self.ways.pop(0))

    def end(self):
        self.block = self.grid.pile(self.block, self.grid.wait(self.moving))

    def step(self):
        self.begin()
        self.end()

    def row_of(self, here, device):
        return sum(
            lax.rem(lax.rem(here // (1 << bit), 2) + (device >> bit) % 2, 2) * (1 << at)
            for at, bit in enumerate(self.bits)
        )

    def result(self):
        grid = self.grid
        here = (grid.rank * 2 + grid.x) * 2 + grid.c
        return self.block[jnp.stack([self.row_of(here, device) for device in range(grid.rank_count * 4)])]


def unfold_vectors(grid, gather, sizes, block_len, seqs):
    zn, yn, block = grid.z_count, grid.y_count, gather.block
    ranks, devices = grid.rank_count, grid.rank_count * 4
    cuts = [sum(sizes[:i]) for i in range(len(sizes) + 1)]
    slots = sizes[6] // 2
    head, hidden = sizes[2] * devices // (3 * ranks), sizes[4] * devices // ranks
    third = sizes[2] * devices // 3
    rows = 8 * block_len
    length = yn * rows
    half = ROT // 2
    lane = np.arange(128) % HEAD
    freqs = np.float32(ROPE_BASE) ** (-((lane % half).astype(np.float32) * np.float32(2.0 / ROT)))
    turned = (lane < ROT).astype(np.float32)
    sign = np.where(lane < half, -1.0, 1.0).astype(np.float32) * turned
    marks = jnp.asarray(np.stack([freqs.astype(np.float32), turned, sign]))

    def body(where_ref, block_ref, mark_ref, *refs):
        z, y, x, c = [where_ref[i] for i in range(4)]
        gain_ref, shift_ref, in_ref, out_ref, cos_ref, sin_ref, column_ref, row_ref = refs[:8]
        qkv_ref, up_ref = refs[8:]
        here_at = ((z * yn + y) * 2 + x) * 2 + c
        for device in range(devices):
            row = block_ref[pl.ds(gather.row_of(here_at, device), 1), :]
            item = [row[:, cuts[i] : cuts[i + 1]] for i in range(6)]
            here = [pl.ds(device * sizes[i], sizes[i]) for i in range(6)]
            gain_ref[:, here[0]] = item[0]
            shift_ref[:, here[1]] = item[1]
            qkv_ref[:, here[2]] = item[2]
            out_ref[:, here[3]] = item[3] + item[5]
            up_ref[:, here[4]] = item[4]
        rank = z * yn + y
        for part in range(3):
            start = pl.multiple_of(part * third + rank * head, 128)
            in_ref[:, part * head : (part + 1) * head] = qkv_ref[:, pl.ds(start, head)]
        in_ref[:, 3 * head :] = up_ref[:, pl.ds(pl.multiple_of(rank * hidden, 128), hidden)]

        def order_row(source):
            parts = [
                jnp.where(source == at, block_ref[pl.ds(gather.row_of(here_at, at * 4 * yn), 1), :], 0.0)
                for at in range(zn)
            ]
            return sum(parts)

        parity = lax.rem(z + x, 2)
        slot_at = lax.broadcasted_iota(jnp.int32, (1, slots), 1)
        tall = lax.broadcasted_iota(jnp.int32, (block_len, 128), 0).astype(WIDE)
        flat = lax.broadcasted_iota(jnp.int32, (1, block_len), 1).astype(WIDE)
        for i in range(seqs):
            row = order_row(lax.rem(z - 2 * i - parity + 2 * zn, zn))
            order = jnp.where(c == 0, row[:, cuts[6] : cuts[6] + slots], row[:, cuts[6] + slots : cuts[7]])
            for dy in range(yn):
                for near in range(4):
                    ctx = (lax.rem(y - dy + yn, yn) * 2 + lax.rem(x + near // 2, 2)) * 2 + lax.rem(c + near, 2)
                    for at in range(2):
                        value = jnp.sum(jnp.where(slot_at == 2 * ctx + at, order, 0.0), 1, keepdims=True) * block_len
                        place = value + tall
                        angle = place * mark_ref[0:1, :]
                        inside = (near * 2 + at) * block_len
                        here = pl.ds((dy * seqs + i) * rows + inside, block_len)
                        cos_ref[here, :] = jnp.where(mark_ref[1:2, :] > 0.0, jnp.cos(angle), 1.0)
                        sin_ref[here, :] = jnp.sin(angle) * mark_ref[2:3, :]
                        there = dy * rows + inside
                        column_ref[pl.ds(i * length + there, block_len), :] = place[:, :1]
                        row_ref[i, :, there : there + block_len] = value + flat

    wide = lambda *shape: jax.ShapeDtypeStruct(shape, WIDE)
    tokens = seqs * length
    vmem = pl.BlockSpec(memory_space=pltpu.VMEM)
    return pl.pallas_call(
        body,
        in_specs=[pl.BlockSpec(memory_space=pltpu.SMEM), vmem, vmem],
        out_specs=[vmem] * 8,
        out_shape=[
            wide(1, sizes[0] * devices), wide(1, sizes[1] * devices), wide(1, 3 * head + hidden),
            wide(1, sizes[3] * devices), wide(tokens, 128), wide(tokens, 128), wide(tokens, 1), wide(seqs, 1, length),
        ],
        scratch_shapes=[
            pltpu.VMEM((1, 3 * third), WIDE), pltpu.VMEM((1, hidden * ranks), WIDE),
        ],
        compiler_params=ROOM,
        cost_estimate=LIGHT,
    )(grid.where, block, marks)


class VectorSum:
    def __init__(self, grid, rows):
        self.grid, self.terms, self.bit = grid, [rows], 0

    def begin(self):
        grid, bit, yn = self.grid, self.bit, self.grid.y_count
        count, width = self.terms[0].shape

        def body(z, y, x, c, ins, outs):
            own = lax.rem((((z * yn + y) * 2 + x) * 2 + c) // (1 << bit), 2)
            for at in range(count // 2):
                for out, pick in zip(outs, (own, 1 - own)):
                    row = pl.ds(2 * at + pick, 1)
                    out[at : at + 1, :] = sum(ref[row, :] for ref in ins)

        kept, away = grid.local(body, self.terms, [jax.ShapeDtypeStruct((count // 2, width), WIDE)] * 2)
        self.kept, self.moving = kept, grid.swap(away, bit)
        self.bit += 1

    def end(self):
        self.terms = [self.kept, self.grid.wait(self.moving)]

    def result(self):
        while self.terms[0].shape[0] > 1:
            self.begin()
            self.end()
        return sum(self.terms)[0]


def fold_vectors(grid, gains, shifts, sums_qkv, sum_up, cotangent, sizes):
    devices, ranks, yn = grid.rank_count * 4, grid.rank_count, grid.y_count
    head, hidden = sums_qkv[0].shape[1], sum_up.shape[1]
    third = head * ranks
    chunks = (sizes[0], sizes[1], sizes[2], sizes[3], sizes[4])
    starts = [sum(chunks[:i]) for i in range(len(chunks))]
    count = len(gains)

    def body(where_ref, *refs):
        ins, out_ref, qkv_ref, up_ref = refs[:-3], refs[-3], refs[-2], refs[-1]
        rank = where_ref[0] * yn + where_ref[1]
        gain = sum(ref[...] for ref in ins[:count])
        shift = sum(ref[...] for ref in ins[count : 2 * count])
        grad = jnp.sum(ins[2 * count + 4][...].astype(WIDE), (0, 1))[None]
        qkv_ref[...] = jnp.zeros_like(qkv_ref)
        up_ref[...] = jnp.zeros_like(up_ref)
        for part in range(3):
            qkv_ref[:, pl.ds(pl.multiple_of(part * third + rank * head, 128), head)] = ins[2 * count + part][...]
        up_ref[:, pl.ds(pl.multiple_of(rank * hidden, 128), hidden)] = ins[2 * count + 3][...]
        for device in range(devices):
            for start, size, whole_row in zip(starts, chunks, (gain, shift, qkv_ref, grad, up_ref)):
                item = whole_row[:, device * size : (device + 1) * size]
                out_ref[device : device + 1, start : start + size] = item

    vmem = pl.BlockSpec(memory_space=pltpu.VMEM)
    inputs = [*gains, *shifts, *sums_qkv, sum_up, cotangent]
    return pl.pallas_call(
        body,
        in_specs=[pl.BlockSpec(memory_space=pltpu.SMEM)] + [vmem] * len(inputs),
        out_specs=vmem,
        out_shape=jax.ShapeDtypeStruct((devices, sum(chunks)), WIDE),
        scratch_shapes=[pltpu.VMEM((1, 3 * third), WIDE), pltpu.VMEM((1, hidden * ranks), WIDE)],
        compiler_params=ROOM,
        cost_estimate=cost(3.0),
    )(grid.where, *inputs)


def contract_last(left, right):
    return lax.dot_general(
        left, right, (((1,), (1,)), ((), ())), preferred_element_type=WIDE
    )


def contract_first(left, right):
    return lax.dot_general(
        left, right, (((0,), (0,)), ((), ())), preferred_element_type=WIDE
    )


def whole(array):
    return pl.BlockSpec(array.shape, lambda *at: (0,) * array.ndim)


def swap_halves(field):
    width = field.shape[-1]
    half = ROT // 2
    if width % 128 == 0:
        after = pltpu.roll(field, width - half, 1)
        before = pltpu.roll(field, half, 1)
    else:
        after = jnp.concatenate([field[:, half:], field[:, :half]], 1)
        before = jnp.concatenate([field[:, width - half :], field[:, : width - half]], 1)
    lane = lax.broadcasted_iota(jnp.int32, field.shape, 1) % HEAD
    return jnp.where(lane < half, after, before)


def turned_heads(query_ref, key_ref, value_ref, cos_ref, sin_ref):
    rows = (-1, cos_ref.shape[-1])
    cosine, sine = cos_ref[...].reshape(rows), sin_ref[...].reshape(rows)
    query = query_ref[...].reshape(rows)
    query_all = (query * cosine + swap_halves(query) * sine).astype(LOW)
    key = key_ref[...].reshape(rows)
    key_all = (key * cosine + swap_halves(key) * sine).astype(LOW)
    value_all = value_ref[...].reshape(rows).astype(LOW)
    return cosine, sine, query_all, key_all, value_all


def probability_of(query_low, key_low, allowed):
    scores = jnp.where(allowed, contract_last(query_low, key_low) * HEAD**-0.5, -1e30)
    weights = jnp.exp(scores - jnp.max(scores, -1, keepdims=True))
    return weights * (1.0 / jnp.sum(weights, -1, keepdims=True))


def forward_body(
    query_ref, key_ref, value_ref, cos_ref, sin_ref, column_ref, row_ref, mixed_ref, kept_ref
):
    _, _, query_all, key_all, value_all = turned_heads(query_ref, key_ref, value_ref, cos_ref, sin_ref)
    allowed = row_ref[...] <= column_ref[...]
    outs = []
    for at in range(query_all.shape[1] // HEAD):
        part = slice(at * HEAD, (at + 1) * HEAD)
        probability_low = probability_of(query_all[:, part], key_all[:, part], allowed).astype(LOW)
        kept_ref[at] = probability_low
        outs.append(jnp.dot(probability_low, value_all[:, part], preferred_element_type=WIDE))
    mixed_ref[...] = jnp.concatenate(outs, 1).astype(LOW).reshape(mixed_ref.shape)


def backward_body(
    query_ref, key_ref, value_ref, cos_ref, sin_ref, grad_ref, kept_ref, grad_query_ref, grad_key_ref, grad_value_ref
):
    cosine, sine, query_all, key_all, value_all = turned_heads(query_ref, key_ref, value_ref, cos_ref, sin_ref)
    grad_all = grad_ref[...].reshape(value_all.shape)
    scale = HEAD**-0.5
    outs = []
    for at in range(query_all.shape[1] // HEAD):
        part = slice(at * HEAD, (at + 1) * HEAD)
        query_low, key_low = query_all[:, part], key_all[:, part]
        value_low, grad_low = value_all[:, part], grad_all[:, part]
        probability_low = kept_ref[at]
        mixed = jnp.dot(probability_low, value_low, preferred_element_type=WIDE)
        delta = jnp.sum(grad_low.astype(WIDE) * mixed, -1, keepdims=True)
        grad_probability = contract_last(grad_low, value_low)
        grad_scores = (probability_low.astype(WIDE) * (grad_probability - delta)).astype(LOW)
        grad_value = contract_first(probability_low, grad_low)
        grad_query = jnp.dot(grad_scores, key_low, preferred_element_type=WIDE) * scale
        grad_key = contract_first(grad_scores, query_low) * scale
        outs.append((grad_query, grad_key, grad_value))
    grad_query, grad_key, grad_value = [jnp.concatenate(item, 1) for item in zip(*outs)]
    block = grad_query_ref.shape
    grad_query = grad_query * cosine - swap_halves(grad_query) * sine
    grad_key = grad_key * cosine - swap_halves(grad_key) * sine
    grad_query_ref[...] = grad_query.astype(LOW).reshape(block)
    grad_key_ref[...] = grad_key.astype(LOW).reshape(block)
    grad_value_ref[...] = grad_value.astype(LOW).reshape(block)


def attend(qkv, cosine, sine, yn, seqs, column=None, row=None, grad_attention=None, kept=None):
    backward = grad_attention is not None
    tokens, width = qkv.shape[0], qkv.shape[1] // 3
    lanes = min(128, width)
    length = tokens // seqs
    rows = length // yn
    block = (yn, None, rows, lanes)
    cut = lambda array: array.reshape(yn, seqs, rows, array.shape[-1])
    field = pl.BlockSpec(block, lambda s, h: (0, s, 0, h))
    table = pl.BlockSpec(block, lambda s, h: (0, s, 0, 0))
    square = pl.BlockSpec((None, lanes // HEAD, length, length), lambda s, h: (s, h, 0, 0))
    low = low_shape(yn, seqs, rows, width)
    if width % 128 == 0:
        thirds = [cut(qkv)] * 3
        blocks = [
            pl.BlockSpec(block, lambda s, h, part=part: (0, s, 0, part * (width // lanes) + h)) for part in range(3)
        ]
    else:
        thirds = [cut(qkv[:, part * width : (part + 1) * width]) for part in range(3)]
        blocks = [field] * 3
    inputs = [*thirds, cut(cosine[:, :lanes]), cut(sine[:, :lanes])]
    blocks = blocks + [table, table]
    if backward:
        body, inputs, blocks = backward_body, inputs + [cut(grad_attention), kept], blocks + [field, square]
        outs, out_blocks = [low] * 3, [field] * 3
    else:
        body, inputs = forward_body, inputs + [column, row]
        blocks = blocks + [
            pl.BlockSpec((length, 1), lambda s, h: (s, 0)),
            pl.BlockSpec((None, 1, length), lambda s, h: (s, 0, 0)),
        ]
        outs, out_blocks = [low, low_shape(seqs, width // HEAD, length, length)], [field, square]
    made = pl.pallas_call(
        body,
        grid=(seqs, width // lanes),
        in_specs=blocks,
        out_specs=out_blocks,
        out_shape=outs,
        compiler_params=pltpu.CompilerParams(vmem_limit_bytes=40 * 1024 * 1024),
        cost_estimate=cost(13.0),
    )(*inputs)
    return [item.reshape(tokens, width) if item.shape == low.shape else item for item in made]


def normalize(parts, gain_vec, shift_vec):
    span, width = parts[0].shape
    tile = min(span, 128)
    each = span // tile

    def body(*refs):
        step = pl.program_id(0)
        gain_ref, shift_ref, normed_ref, unit_ref = refs[len(parts) :]
        for at, ref in enumerate(refs[: len(parts)]):

            @pl.when(step // each == at)
            def _(ref=ref):
                inputs = ref[...].astype(WIDE)
                centre = inputs - jnp.mean(inputs, -1, keepdims=True)
                spread = jnp.mean(centre * centre, -1, keepdims=True)
                unit = centre * lax.rsqrt(spread + NORM_EPS)
                normed_ref[...] = (unit * gain_ref[...] + shift_ref[...]).astype(LOW)
                unit_ref[...] = unit.astype(LOW)

    block = (tile, width)
    clamp = lambda at: pl.BlockSpec(block, lambda t: (jnp.clip(t - at * each, 0, each - 1), 0))
    vector = pl.BlockSpec((1, width), lambda t: (0, 0))
    return pl.pallas_call(
        body,
        grid=(len(parts) * each,),
        in_specs=[clamp(at) for at in range(len(parts))] + [vector, vector],
        out_specs=[pl.BlockSpec(block, lambda t: (t, 0))] * 2,
        out_shape=[low_shape(len(parts) * span, width)] * 2,
        compiler_params=ROOM,
        cost_estimate=cost(8.0),
    )(*parts, gain_vec, shift_vec)


def bend(up):
    bent = jnp.tanh(GELU_SCALE * (up + GELU_CUBIC * up * up * up))
    slope = 0.5 * (1.0 + bent) + 0.5 * up * (1.0 - bent * bent) * GELU_SCALE * (1.0 + 3.0 * GELU_CUBIC * up * up)
    return (0.5 * up * (1.0 + bent)).astype(LOW), slope.astype(LOW)


def project(normed_low, w_in, bias, split):
    tokens, total = normed_low.shape[0], w_in.shape[1]
    if split % 256 or total % 256:
        made = jnp.dot(normed_low, w_in, preferred_element_type=WIDE) + bias
        return made[:, :split], *bend(made[:, split:])
    heads = split // 256

    def body(normed_ref, w_ref, bias_ref, qkv_ref, hidden_ref, slope_ref):
        step = pl.program_id(0)
        made = jnp.dot(normed_ref[...], w_ref[...], preferred_element_type=WIDE) + bias_ref[...]

        @pl.when(step < heads)
        def _():
            qkv_ref[...] = made

        @pl.when(step >= heads)
        def _():
            hidden_ref[...], slope_ref[...] = bend(made)

    late = pl.BlockSpec((tokens, 256), lambda t: (0, jnp.maximum(t - heads, 0)))
    return pl.pallas_call(
        body,
        grid=(total // 256,),
        in_specs=[
            whole(normed_low),
            pl.BlockSpec((w_in.shape[0], 256), lambda t: (0, t)),
            pl.BlockSpec((1, 256), lambda t: (0, t)),
        ],
        out_specs=[pl.BlockSpec((tokens, 256), lambda t: (0, jnp.minimum(t, heads - 1))), late, late],
        out_shape=[jax.ShapeDtypeStruct((tokens, split), WIDE)] + [low_shape(tokens, total - split)] * 2,
        compiler_params=ROOM,
        cost_estimate=cost(16.0),
    )(normed_low, w_in, bias)


def project_back(grad_out, w_out, slope, dense_rows):
    tokens, width = grad_out.shape
    if dense_rows % 256 or w_out.shape[0] % 256:
        return (
            contract_last(grad_out, w_out[:dense_rows]).astype(LOW),
            (contract_last(grad_out, w_out[dense_rows:]) * slope.astype(WIDE)).astype(LOW),
        )
    first = dense_rows // 256

    def body(grad_ref, w_ref, slope_ref, attention_ref, up_ref):
        step = pl.program_id(0)
        made = contract_last(grad_ref[...], w_ref[...])

        @pl.when(step < first)
        def _():
            attention_ref[...] = made.astype(LOW)

        @pl.when(step >= first)
        def _():
            up_ref[...] = (made * slope_ref[...].astype(WIDE)).astype(LOW)

    late = pl.BlockSpec((tokens, 256), lambda t: (0, jnp.maximum(t - first, 0)))
    return pl.pallas_call(
        body,
        grid=(w_out.shape[0] // 256,),
        in_specs=[whole(grad_out), pl.BlockSpec((256, width), lambda t: (t, 0)), late],
        out_specs=[pl.BlockSpec((tokens, 256), lambda t: (0, jnp.minimum(t, first - 1))), late],
        out_shape=[low_shape(tokens, dense_rows), low_shape(*slope.shape)],
        compiler_params=ROOM,
        cost_estimate=cost(10.0),
    )(grad_out, w_out, slope)


def out_part(attention_low, hidden_low, w_out, dy, rows, seqs):
    head, hidden, width = attention_low.shape[1], hidden_low.shape[1], w_out.shape[1]
    each = rows // seqs
    if head % 128:
        here = slice(dy * rows, (dy + 1) * rows)
        joined = jnp.concatenate([attention_low[here], hidden_low[here]], 1)
        made = jnp.dot(joined, w_out, preferred_element_type=WIDE).astype(LOW)
        return [made[i * each : (i + 1) * each] for i in range(seqs)]

    def body(attention_ref, hidden_ref, w_ref, *out_refs):
        made = jnp.dot(attention_ref[...], w_ref[:head], preferred_element_type=WIDE)
        made += jnp.dot(hidden_ref[...], w_ref[head:], preferred_element_type=WIDE)
        for i, out_ref in enumerate(out_refs):
            out_ref[...] = made[i * each : (i + 1) * each].astype(LOW)

    tile = min(width, 512)
    return pl.pallas_call(
        body,
        grid=(width // tile,),
        in_specs=[
            pl.BlockSpec((rows, head), lambda t: (dy, 0)),
            pl.BlockSpec((rows, hidden), lambda t: (dy, 0)),
            pl.BlockSpec((w_out.shape[0], tile), lambda t: (0, t)),
        ],
        out_specs=[pl.BlockSpec((each, tile), lambda t: (0, t))] * seqs,
        out_shape=[low_shape(each, width)] * seqs,
        compiler_params=ROOM,
        cost_estimate=cost(150.0),
    )(attention_low, hidden_low, w_out)


def in_part(grads, w_in, unit_low, dy, rows, seqs):
    widths = [item.shape[1] for item in grads]
    starts = [sum(widths[:i]) for i in range(len(widths))]
    width = w_in.shape[0]
    each = rows // seqs
    if widths[0] % 128:
        here = slice(dy * rows, (dy + 1) * rows)
        made = contract_last(jnp.concatenate([item[here] for item in grads], 1), w_in)
        sums = [jnp.sum(item, 0, keepdims=True) for item in (made * unit_low[here].astype(WIDE), made)]
        return [made[i * each : (i + 1) * each].astype(LOW) for i in range(seqs)], *sums

    def body(*refs):
        w_ref, unit_ref, *out_refs, gain_ref, shift_ref = refs[len(grads) :]
        made = None
        for ref, start, size in zip(refs, starts, widths):
            term = contract_last(ref[...], w_ref[:, start : start + size])
            made = term if made is None else made + term
        for i, out_ref in enumerate(out_refs):
            out_ref[...] = made[i * each : (i + 1) * each].astype(LOW)
        gain_ref[...] = jnp.sum(made * unit_ref[...].astype(WIDE), 0, keepdims=True)
        shift_ref[...] = jnp.sum(made, 0, keepdims=True)

    tile = min(width, 512)
    vector = pl.BlockSpec((1, tile), lambda t: (0, t))
    *made, gain, shift = pl.pallas_call(
        body,
        grid=(width // tile,),
        in_specs=[pl.BlockSpec((rows, size), lambda t: (dy, 0)) for size in widths]
        + [
            pl.BlockSpec((tile, w_in.shape[1]), lambda t: (t, 0)),
            pl.BlockSpec((rows, tile), lambda t: (dy, t)),
        ],
        out_specs=[pl.BlockSpec((each, tile), lambda t: (0, t))] * seqs + [vector, vector],
        out_shape=[low_shape(each, width)] * seqs + [jax.ShapeDtypeStruct((1, width), WIDE)] * 2,
        compiler_params=ROOM,
        cost_estimate=cost(7.0),
    )(*grads, w_in, unit_low)
    return made, gain, shift


def rotary_tables(places):
    lane = jnp.arange(128, dtype=jnp.int32) % HEAD
    half = ROT // 2
    freqs = jnp.asarray(ROPE_BASE, WIDE) ** (-((lane % half).astype(WIDE) * (2.0 / ROT)))
    angles = places.astype(WIDE)[:, None] * freqs
    turned = (lane < ROT)[None, :]
    sign = jnp.where(lane < half, -1.0, 1.0)
    return jnp.where(turned, jnp.cos(angles), 1.0), jnp.where(turned, jnp.sin(angles) * sign, 0.0)


def unfold_rows(grid, gathered, sizes, block_len, group_seqs):
    zn, yn, ranks = grid.z_count, grid.y_count, grid.rank_count
    cuts = [sum(sizes[:i]) for i in range(len(sizes) + 1)]
    gain_full, shift_full, bias_qkv, bias_dense, bias_up, bias_down = [
        gathered[:, cuts[i] : cuts[i + 1]].reshape(-1).astype(WIDE) for i in range(6)
    ]
    orders = gathered[:: grid.ctx_count, cuts[6] :].reshape(zn, 2, -1).astype(jnp.int32)

    ctx_from = jnp.stack(
        [
            (((grid.y - dy) % yn) * 2 + (grid.x ^ dx)) * 2 + (grid.c ^ dc)
            for dy in range(yn)
            for dx in range(2)
            for dc in range(2)
        ]
    )
    z_from = jnp.stack([(grid.z - 2 * i - grid.parity) % zn for i in range(group_seqs)])
    own_orders = lax.dynamic_index_in_dim(orders, grid.c, 1, keepdims=False)[z_from]
    slots = (ctx_from[:, None] * 2 + jnp.arange(2)).reshape(-1)
    places = own_orders[:, slots].reshape(group_seqs, yn, -1).swapaxes(0, 1)
    places = (places[..., None] * block_len + jnp.arange(block_len)).reshape(-1)
    cosine, sine = rotary_tables(places)


    bias_in = jnp.concatenate(
        [
            lax.dynamic_index_in_dim(bias_qkv.reshape(3, ranks, -1), grid.rank, 1, keepdims=False).reshape(-1),
            place(bias_up.reshape(ranks, -1), grid.rank),
        ]
    )
    column = places.reshape(yn, group_seqs, -1).swapaxes(0, 1).reshape(-1).astype(WIDE)
    return (
        gain_full[None], shift_full[None], bias_in[None], (bias_dense + bias_down)[None], cosine, sine,
        column[:, None], column.reshape(group_seqs, 1, -1),
    )


def fold_rows(grid, gain, shift, sums_qkv, sum_up, cotangent):
    ranks, devices = grid.rank_count, grid.rank_count * 4

    def laid(part, count):
        whole_rows = jnp.zeros((count, ranks, part.shape[-1]), WIDE)
        whole_rows = lax.dynamic_update_index_in_dim(whole_rows, part, grid.rank, 1)
        return whole_rows.reshape(devices, -1)

    return jnp.concatenate(
        [
            gain.reshape(devices, -1),
            shift.reshape(devices, -1),
            laid(jnp.concatenate(sums_qkv, 0), 3),
            jnp.sum(cotangent.astype(WIDE), (0, 1)).reshape(devices, -1),
            laid(sum_up, 1),
        ],
        1,
    )


def on_device(
    tokens, block_order, ln_gain, ln_bias, w_qkv, b_qkv, w_dense, b_dense, w_fc1, b_fc1, w_fc2, b_fc2, cotangent,
):
    grid = Grid()
    seqs, span, model_width = tokens.shape
    zn, yn, ranks = grid.z_count, grid.y_count, grid.rank_count
    device_count = ranks * 4
    length = span * grid.ctx_count
    block_len = span // 2
    group_seqs = zn // 2
    head_width = model_width // ranks

    split = 3 * head_width
    dense_rows = 4 * w_dense.shape[0]
    rows = group_seqs * length // yn
    seq_rows = length // yn
    last = group_seqs - 1

    def ordered(spreads):
        return [spreads[i].parts[dy] for dy in range(yn) for i in range(group_seqs)]

    def ordered(spreads):
        return [spreads[i].parts[dy] for dy in range(yn) for i in range(group_seqs)]

    def rows_of(array, i):
        return array[i * seq_rows : (i + 1) * seq_rows]

    def across_x(ks):
        own = near[ks[0]][None] if len(ks) == 1 else grid.pile(*[near[k][None] for k in ks])
        return ks, own, grid.start(own, x=1)

    def both_columns(group):
        ks, own, moving = group
        return ks, grid.pile(own[None], grid.wait(moving)[None])

    away, own_tokens, own_cotangent = part_cores(grid, tokens, cotangent)
    moving = grid.start(away, c=1)
    down_moving = grid.start(w_fc2, x=1)
    others = grid.wait(moving)
    ring = Ring(grid, grid.pile(own_tokens, others[:span]))
    ring.begin(1)
    ahead, across = cut_columns(grid, *grid.after((w_qkv, w_fc1)))
    across = [grid.start(part, y=dy + 1) for dy, part in enumerate(across)]
    vectors = (ln_gain, ln_bias, b_qkv, b_dense, b_fc1, b_fc2, block_order.reshape(-1))
    sizes = [item.shape[0] for item in vectors]
    vectors = jnp.concatenate([item.astype(WIDE) for item in grid.after(vectors)])
    gather = VectorGather(grid, vectors)
    gather.begin()
    down_moving = grid.wait(down_moving)
    dense_moving = grid.start(w_dense, x=1)
    gather.end()
    ring.end()
    ring.begin(2)
    dense_moving = grid.wait(dense_moving)
    gather.begin()
    spreads = [Spread(grid, ring.pair(0))]
    across = grid.wait(across)
    gather.end()

    def pack(z, y, x, c, ins, outs):
        for k in range(zn):
            outs[k][0] = ins[k][...]
            for dy in range(1, yn):
                outs[k][dy] = ins[zn + dy - 1][k]

    near = grid.local(pack, [*ahead, *across], [low_shape(yn, *ahead[0].shape)] * zn)
    near = dict(enumerate(near))
    near[zn - 1] = grid.start(near[zn - 1], z=-1)
    gather.begin()
    spreads[0].end_x()
    spreads[0].begin_y()
    ring.end()
    rest = [k for k in grid.steps() if k != zn - 1]
    moving = {rest[0]: grid.start(near[rest[0]], z=rest[0])}
    group_own = across_x([0])
    near[zn - 1] = grid.wait(near[zn - 1])
    gather.end()
    ring.finish()
    moving.update({k: grid.start(near[k], z=k) for k in rest[1:]})
    spreads += [Spread(grid, ring.pair(i)) for i in range(1, group_seqs)]
    gather.begin()

    def stack_out(z, y, x, c, ins, outs):
        for at in range(2):
            dense = ins[2 * at].shape[0]
            outs[0][at, :dense] = ins[2 * at][...]
            outs[0][at, dense:] = ins[2 * at + 1][...]

    out_rows = grid.local(
        stack_out,
        grid.after([w_dense, w_fc2, dense_moving, down_moving]),
        [low_shape(2, w_dense.shape[0] + w_fc2.shape[0], model_width)],
    )[0]
    group_own = both_columns(group_own)
    for spread in spreads[1:]:
        spread.end_x()
    spreads[1].begin_y()
    group_far = across_x([zn - 1])
    spreads[0].end_y()
    gather.end()
    near.update(grid.wait(moving))
    group_rest = across_x(rest)
    met_grad = grid.pile(own_cotangent, others[span:])
    ring = Ring(grid, met_grad)
    ring.begin(1)
    group_far = both_columns(group_far)
    gather.begin()

    def beside(z, y, x, c, ins, outs):
        for at, ref in enumerate(ins):
            outs[0][:, at : at + 1] = ref[...]

    first = group_own[0] + group_far[0]
    first_rows = grid.local(beside, [group_own[1], group_far[1]], [low_shape(2, 2, *group_own[1].shape[2:])])[0]
    gather.end()
    while gather.ways:
        gather.step()
    if head_width % 128 == 0:
        unfolded = grid.hold(unfold_vectors(grid, gather, sizes, block_len, group_seqs))
    else:
        unfolded = unfold_rows(grid, gather.result(), sizes, block_len, group_seqs)
    gain_full, shift_full, bias_in, bias_out, cosine, sine, column, row = unfolded
    first_moving = grid.start(first_rows, c=1)
    spreads[1].end_y()
    for spread in spreads[2:]:
        spread.begin_y()
        spread.end_y()
    out_moving = grid.start(out_rows, c=1)
    normed_low, unit_low = grid.hold(normalize(ordered(spreads), gain_full, shift_full))
    first_moving = grid.wait(first_moving)
    group_rest = both_columns(group_rest)
    rest_moving = grid.start(group_rest[1], c=1)
    out_moving = grid.wait(out_moving)
    w_out = grid.hold(join_out(grid, *grid.after((out_rows, out_moving)), w_dense.shape[0]))
    ring.end()
    grads = [Spread(grid, ring.pair(0))]
    ring.begin(2)
    rest_moving = grid.wait(rest_moving)
    w_in = grid.hold(join_columns(grid, [(first, first_rows, first_moving), (*group_rest, rest_moving)]))
    grads[0].end_x()
    grads[0].begin_y()
    grid.page()
    ring.end()
    ring.finish()
    grads += [Spread(grid, ring.pair(i)) for i in range(1, group_seqs)]

    qkv, hidden_low, slope = grid.hold(project(grid.after(normed_low), w_in, bias_in, split))
    grid.pages = False
    for spread in grads[1:]:
        spread.end_x()
    grads[1].begin_y()
    attention_low, kept = grid.hold(attend(grid.after(qkv), cosine, sine, yn, group_seqs, column=column, row=row))
    out_parts = {}
    for dy in range(yn - 1, -1, -1):
        if dy == 0:
            grads[0].end_y()
        out_parts[dy] = grid.hold(out_part(grid.after(attention_low), hidden_low, w_out, dy, rows, group_seqs))
    grads[1].end_y()
    for spread in grads[2:]:
        spread.begin_y()
        spread.end_y()

    out_sums = {i: TokenSum(grid, out_parts[yn - 1][i], yn - 1) for i in range(last, -1, -1)}
    grad_out = grid.pile(*grid.after(ordered(grads)))
    grad_attention_low, grad_up_low = grid.hold(project_back(grad_out, w_out, slope, dense_rows))

    def finish_y(sums, parts, i):
        for dy in range(yn - 2, -1, -1):
            sums[i].more(parts[dy][i])

    grads_qkv = grid.hold(
        attend(grid.after(qkv), cosine, sine, yn, group_seqs, grad_attention=grad_attention_low, kept=kept)
    )
    grads_in = [*grads_qkv, grad_up_low]
    finish_y(out_sums, out_parts, last)
    out_sums[last].begin_x()
    in_parts, gain_parts, shift_parts = {}, {}, {}

    def make_in_part(dy):
        in_parts[dy], gain_parts[dy], shift_parts[dy] = grid.hold(
            in_part(grid.after(grads_in), w_in, unit_low, dy, rows, group_seqs)
        )

    make_in_part(yn - 1)
    in_sums = {last: TokenSum(grid, in_parts[yn - 1][last], yn - 1)}
    out_ring = RingSum(grid)
    out_ring.pieces[2 * last], out_ring.pieces[2 * last + 1] = out_sums[last].end_x()
    for i in range(last - 1, 0, -1):
        finish_y(out_sums, out_parts, i)
        out_sums[i].begin_x()
        out_ring.pieces[2 * i], out_ring.pieces[2 * i + 1] = out_sums[i].end_x()
    out_ring.begin_far()
    finish_y(out_sums, out_parts, 0)
    out_sums[0].begin_x()
    for dy in range(yn - 2, -1, -1):
        make_in_part(dy)
    up_kept, up_away, (sum_up,) = grid.hold(halves_in(grid, grid.after(normed_low), [grad_up_low]))
    up_moving = grid.start(up_away, c=1)
    out_ring.pieces[0], out_ring.pieces[1] = out_sums[0].end_x()
    out_ring.end_far()
    out_ring.begin_near()
    finish_y(in_sums, in_parts, last)
    for i in range(last - 1, -1, -1):
        in_sums[i] = TokenSum(grid, in_parts[yn - 1][i], yn - 1)
    in_sums[last].begin_x()
    grid.turn()
    up_kept, up_away = grid.hold(halve_columns(grid, up_kept, grid.wait(up_moving)))
    up_moving = grid.start(up_away, x=1)
    qkv_kept, qkv_away, sums_qkv = grid.hold(halves_in(grid, grid.after(normed_low), grads_qkv))
    qkv_moving = grid.start(qkv_away, c=1)
    out_ring.end_near()
    if head_width % 128 == 0:
        sums = fold_vectors(
            grid, list(gain_parts.values()), list(shift_parts.values()), sums_qkv, sum_up, cotangent, sizes
        )
    else:
        sums = fold_rows(
            grid, sum(gain_parts.values()), sum(shift_parts.values()), sums_qkv, sum_up, cotangent
        )
    sums = VectorSum(grid, grid.hold(sums))
    sums.begin()
    in_ring = RingSum(grid)
    in_ring.pieces[2 * last], in_ring.pieces[2 * last + 1] = in_sums[last].end_x()
    for i in range(last - 1, 0, -1):
        finish_y(in_sums, in_parts, i)
        in_sums[i].begin_x()
        in_ring.pieces[2 * i], in_ring.pieces[2 * i + 1] = in_sums[i].end_x()
    sums.end()
    in_ring.begin_far()
    sums.begin()
    out_kept, out_away = grid.hold(halves_out(grid, *grid.after((attention_low, hidden_low)), grad_out))
    finish_y(in_sums, in_parts, 0)
    in_sums[0].begin_x()
    sums.end()
    up_return = ColumnReturn(grid, up_kept, grid.wait(up_moving))
    up_return.begin_z()
    in_ring.end_far()
    sums.begin()
    out_moving = grid.start(out_away, c=1)
    grid.turn()
    projected = out_ring.end()
    qkv_moving = grid.wait(qkv_moving)
    sums.end()
    qkv_kept, qkv_away = grid.hold(halve_columns(grid, qkv_kept, qkv_moving))
    qkv_moving = grid.start(qkv_away, x=1)
    out_kept, out_away = grid.hold(halve_columns(grid, out_kept, grid.wait(out_moving)))
    out_moving = grid.start(out_away, x=1)
    in_ring.pieces[0], in_ring.pieces[1] = in_sums[0].end_x()
    up_return.end_z()
    in_ring.begin_near()
    qkv_return = ColumnReturn(grid, qkv_kept, grid.wait(qkv_moving))
    sums.begin()
    qkv_return.begin_z()
    up_return.begin_y()
    sums.end()
    sums.begin()
    in_ring.end_near()
    grad_normed = in_ring.end()
    token_grad = grid.hold(finish_grad(grid, tokens, cotangent, *grad_normed, gain_full))
    up_found = up_return.end()
    grad_w_up = grid.hold(lay_columns(grid, up_found, 1))
    sums.end()
    qkv_return.end_z()
    qkv_return.begin_y()
    output = grid.hold(finish_output(grid, grid.after(tokens), *projected, bias_out))
    qkv_found = qkv_return.end()
    out_moving = grid.wait(out_moving)
    sums = sums.result()
    grad_w_out = (out_kept.astype(WIDE) + out_moving.astype(WIDE))[0]

    grad_w_qkv = lay_columns(grid, qkv_found, 3)

    grad_gain, grad_shift = sums[: sizes[0]], sums[sizes[0] : 2 * sizes[0]]
    rest = sums[2 * sizes[0] :]
    grad_bias_qkv = rest[: sizes[2]]
    grad_bias_out = rest[sizes[2] : sizes[2] + sizes[3]]
    grad_bias_up = rest[sizes[2] + sizes[3] :]
    grad_w_dense = grad_w_out[: w_dense.shape[0]]
    grad_w_down = grad_w_out[w_dense.shape[0] :]
    return (
        output, token_grad, grad_gain, grad_shift, grad_w_qkv, grad_bias_qkv,
        grad_w_dense, grad_bias_out, grad_w_up, grad_bias_up, grad_w_down, grad_bias_out,
    )


def solution(mesh):
    rows = P(("dp", "ctx"), None)
    vector = P(("dp", "ctx"))
    spread = P("dp", "ctx", None)
    in_specs = (
        spread, P("dp", None), vector, vector, rows, vector, rows, vector, rows, vector, rows, vector, spread,
    )
    out_specs = (
        spread, spread, vector, vector, rows, vector, rows, vector, rows, vector, rows, vector,
    )
    return jax.shard_map(on_device, mesh=mesh, in_specs=in_specs, out_specs=out_specs, check_vma=False)
```

```python
from functools import partial

import jax
import jax.numpy as jnp
import numpy as np
from jax import lax
from jax.experimental import pallas as pl
from jax.experimental.pallas import tpu as pltpu
from jax.sharding import PartitionSpec as P

HEAD = 64
ROT = 32
ROPE_BASE = 10000
NORM_EPS = 1e-05
BOTH = ("dp", "ctx")
LOW = jnp.bfloat16
WIDE = jnp.float32
GELU_SCALE = 0.7978845608028654
GELU_CUBIC = 0.044715


COST_SCALE = 20_000_000


LIGHT = pl.CostEstimate(flops=1024, bytes_accessed=1024, transcendentals=1)


def cost(micros):
    return pl.CostEstimate(flops=int(micros * COST_SCALE), bytes_accessed=1024, transcendentals=1)
ROOM = pltpu.CompilerParams(vmem_limit_bytes=20 * 1024 * 1024)


def low_shape(*shape):
    return jax.ShapeDtypeStruct(shape, LOW)


def place(array, index):
    return lax.dynamic_index_in_dim(array, index, 0, keepdims=False)


def turn_page(token):
    def body(token_ref, copy_ref):
        copy_ref[...] = token_ref[...]

    return pl.pallas_call(
        body,
        out_shape=jax.ShapeDtypeStruct(token.shape, token.dtype),
        cost_estimate=pl.CostEstimate(flops=100_000_000_000, bytes_accessed=8192, transcendentals=0),
    )(token)


class Grid:
    def __init__(self):
        self.z_count = lax.axis_size("dp")
        self.ctx_count = lax.axis_size("ctx")
        self.y_count = self.ctx_count // 4
        ctx = lax.axis_index("ctx")
        self.z = lax.axis_index("dp")
        self.y = ctx // 4
        self.x = (ctx // 2) % 2
        self.c = ctx % 2
        self.where = jnp.stack([self.z, self.y, self.x, self.c]).astype(jnp.int32)
        self.rank = self.z * self.y_count + self.y
        self.rank_count = self.z_count * self.y_count
        self.parity = (self.z + self.x) % 2
        self.token = jnp.zeros((8, 128), WIDE)
        self.started, self.pages = False, True

    def steps(self):
        order = sorted(range(1, self.z_count), key=lambda k: (min(k, self.z_count - k), k))
        return order

    def after(self, value):
        self.page()
        return lax.optimization_barrier((value, self.token))[0]

    def hold(self, value):
        self.page()
        value, self.token = lax.optimization_barrier((value, self.token))
        return value

    wait = hold

    def page(self):
        if self.started and self.pages:
            self.token = turn_page(self.token)
        self.started = False

    def swap(self, value, bit):
        pairs = [(device, device ^ (1 << bit)) for device in range(self.rank_count * 4)]
        return self.send(value, pairs)

    def turn(self):
        self.token = turn_page(self.token)
        self.started = False

    def start(self, value, z=0, y=0, x=0, c=0):
        pairs = []
        for z_at in range(self.z_count):
            for y_at in range(self.y_count):
                for x_at in range(2):
                    for c_at in range(2):
                        z_to = (z_at + z) % self.z_count
                        y_to = (y_at + y) % self.y_count
                        source = ((z_at * self.y_count + y_at) * 2 + x_at) * 2 + c_at
                        target = ((z_to * self.y_count + y_to) * 2 + (x_at ^ x)) * 2 + (c_at ^ c)
                        pairs.append((source, target))
        return self.send(value, pairs)

    def send(self, value, pairs):
        value = lax.optimization_barrier((value, self.token))[0]
        self.started = True
        return lax.ppermute(value, BOTH, pairs)

    def local(self, body, inputs, outs):
        count = len(inputs)

        def whole_body(where_ref, *refs):
            body(*[where_ref[i] for i in range(4)], refs[:count], refs[count:])

        vmem = pl.BlockSpec(memory_space=pltpu.VMEM)
        return pl.pallas_call(
            whole_body,
            in_specs=[pl.BlockSpec(memory_space=pltpu.SMEM)] + [vmem] * count,
            out_specs=[vmem] * len(outs),
            out_shape=outs,
            compiler_params=ROOM,
            cost_estimate=cost(1.5),
        )(self.where, *inputs)

    def pile(self, *arrays):
        lengths = [item.shape[0] for item in arrays]
        starts = [sum(lengths[:i]) for i in range(len(lengths))]

        def body(z, y, x, c, ins, outs):
            for ref, start, length in zip(ins, starts, lengths):
                outs[0][start : start + length] = ref[...]

        shape = (sum(lengths), *arrays[0].shape[1:])
        return self.local(body, arrays, [jax.ShapeDtypeStruct(shape, arrays[0].dtype)])[0]


def mover(grid, plan, inputs, outs):
    count = len(inputs)

    def copies_of(where_ref, refs, sems):
        at = [where_ref[i] for i in range(4)]
        listed = plan(*at, refs[:count], refs[count:])
        return [pltpu.make_async_copy(source, target, sems.at[i]) for i, (source, target) in enumerate(listed)]

    def body(where_ref, *refs):
        copies = copies_of(where_ref, refs[:-1], refs[-1])
        for copy in copies:
            copy.start()
        for copy in copies:
            copy.wait()

    most = 4 * max(4, grid.rank_count)
    return pl.pallas_call(
        body,
        in_specs=[pl.BlockSpec(memory_space=pltpu.SMEM)] + [pl.BlockSpec(memory_space=pltpu.VMEM)] * count,
        out_specs=[pl.BlockSpec(memory_space=pltpu.HBM)] * len(outs),
        out_shape=outs,
        scratch_shapes=[pltpu.SemaphoreType.DMA((most,))],
        compiler_params=pltpu.CompilerParams(vmem_limit_bytes=24 * 1024 * 1024),
        cost_estimate=LIGHT,
    )(grid.where, *inputs)


def part_cores(grid, tokens, cotangent):
    span, width = tokens.shape[1:]

    def body(z, y, x, c, ins, outs):
        for at, ref in enumerate(ins):
            outs[0][at * span : (at + 1) * span] = ref[1 - c]
            outs[1 + at][...] = ref[c]

    shapes = [low_shape(2 * span, width), low_shape(span, width), low_shape(span, width)]
    return grid.local(body, [tokens, cotangent], shapes)


def pair_of(grid, even, odd):
    def body(z, y, x, c, ins, outs):
        swap = lax.rem(z + x, 2)
        for first in range(2):

            @pl.when(swap == first)
            def _(first=first):
                outs[0][...] = ins[first][...]
                outs[1][...] = ins[1 - first][...]

    return grid.local(body, [even, odd], [low_shape(*even.shape)] * 2)


class Ring:
    def __init__(self, grid, first):
        self.grid, self.pieces, self.moving = grid, {0: first}, {}

    def begin(self, r):
        zn = self.grid.z_count
        self.moving[r] = self.grid.start(self.pieces[r - 1], z=1)
        if zn - r > zn // 2:
            self.moving[zn - r] = self.grid.start(self.pieces[(zn - r + 1) % zn], z=-1)

    def end(self):
        self.pieces.update(self.grid.wait(self.moving))
        self.moving = {}

    def finish(self):
        for r in range(3, self.grid.z_count // 2 + 1):
            self.begin(r)
            self.end()

    def pair(self, i):
        return pair_of(self.grid, self.pieces[2 * i], self.pieces[2 * i + 1])


class Spread:
    def __init__(self, grid, pair):
        self.grid = grid
        self.keep, away = pair
        self.moving = grid.start(away, x=1)

    def end_x(self):
        self.parts = [self.grid.pile(self.keep, self.grid.wait(self.moving))]

    def begin_y(self):
        self.moving = self.grid.start(self.parts[-1], y=1)

    def end_y(self):
        self.parts.append(self.grid.wait(self.moving))
        for _ in range(2, self.grid.y_count):
            self.begin_y()
            self.parts.append(self.grid.wait(self.moving))


def sum_low(left, right):
    return (left.astype(WIDE) + right.astype(WIDE)).astype(LOW)


class TokenSum:
    def __init__(self, grid, part, dy):
        self.grid = grid
        self.moving = grid.start(part, y=-1)
        self.left = dy - 1

    def more(self, part):
        arrived = self.grid.wait(self.moving)
        if self.left:
            self.moving = self.grid.start(sum_low(part, arrived), y=-1)
            self.left -= 1
            return
        span = arrived.shape[0] // 2

        def body(z, y, x, c, ins, outs):
            for at in range(2):
                here = slice(at * span, (at + 1) * span)
                outs[at][...] = sum_low(ins[0][here], ins[1][here])

        self.kept, self.away = self.grid.local(body, [part, arrived], [low_shape(span, arrived.shape[1])] * 2)

    def begin_x(self):
        self.moving = self.grid.start(self.away, x=1)

    def end_x(self):
        return pair_of(self.grid, self.kept, self.grid.wait(self.moving))


class RingSum:
    def __init__(self, grid):
        self.grid, self.pieces = grid, {}

    def add(self, left, right):
        def body(z, y, x, c, ins, outs):
            outs[0][...] = sum_low(ins[0][...], ins[1][...])

        return self.grid.local(body, [left, right], [low_shape(*left.shape)])[0]

    def begin_far(self):
        grid, zn, pieces = self.grid, self.grid.z_count, self.pieces
        down, up = zn // 2, zn // 2 + 1
        while down > 2:
            arrived = grid.wait(grid.start(pieces[down], z=-1))
            down -= 1
            pieces[down] = self.add(pieces[down], arrived)
        while up < zn - 1:
            arrived = grid.wait(grid.start(pieces[up], z=1))
            up += 1
            pieces[up] = self.add(pieces[up], arrived)
        self.moving = grid.start(pieces[2], z=-1), grid.start(pieces[zn - 1], z=1)

    def end_far(self):
        self.down, self.up = self.grid.wait(self.moving)

    def begin_near(self):
        self.moving = self.grid.start(self.add(self.pieces[1], self.down), z=-1)

    def end_near(self):
        near = self.grid.wait(self.moving)
        span = near.shape[0] // 2

        def body(z, y, x, c, ins, outs):
            total = ins[0][...].astype(WIDE) + ins[1][...].astype(WIDE) + ins[2][...].astype(WIDE)
            outs[0][...] = total[:span]
            outs[1][...] = total[span:].astype(LOW)

        shapes = [jax.ShapeDtypeStruct((span, near.shape[1]), WIDE), low_shape(span, near.shape[1])]
        self.own, away = self.grid.local(body, [self.pieces[0], self.up, near], shapes)
        self.moving = self.grid.start(away, c=1)

    def end(self):
        return self.own, self.grid.wait(self.moving)


def finish_output(grid, tokens, own, other, bias_out):
    def body(z, y, x, c, ins, outs):
        for ref, at in ((ins[1], c), (ins[2], 1 - c)):
            outs[0][at] = (ins[0][at].astype(WIDE) + ref[...].astype(WIDE) + ins[3][...]).astype(LOW)

    return grid.local(body, [tokens, own, other, bias_out], [low_shape(*tokens.shape)])[0]


def finish_grad(grid, tokens, cotangent, own, other, gain_vec):
    def body(z, y, x, c, ins, outs):
        for ref, at in ((ins[2], c), (ins[3], 1 - c)):
            inputs = ins[0][at].astype(WIDE)
            centre = inputs - jnp.mean(inputs, -1, keepdims=True)
            turn = lax.rsqrt(jnp.mean(centre * centre, -1, keepdims=True) + NORM_EPS)
            unit = centre * turn
            scaled = ref[...].astype(WIDE) * ins[4][...]
            along = jnp.mean(scaled * unit, -1, keepdims=True)
            change = turn * (scaled - jnp.mean(scaled, -1, keepdims=True) - unit * along)
            outs[0][at] = (ins[1][at].astype(WIDE) + change).astype(LOW)

    return grid.local(body, [tokens, cotangent, own, other, gain_vec], [low_shape(*tokens.shape)])[0]


def cut_columns(grid, w_qkv, w_up):
    zn, yn, ranks = grid.z_count, grid.y_count, grid.rank_count
    rows, third, wide = w_qkv.shape[0], w_qkv.shape[1] // 3, w_up.shape[1]
    head, hidden = third // ranks, wide // ranks
    width = 3 * head + hidden
    outs = [low_shape(rows, width)] * zn + [low_shape(zn, rows, width)] * (yn - 1)

    def plan(z, y, x, c, ins, refs):
        copies = []
        for dy in range(yn):
            for k in range(zn):
                rank = lax.rem(z + k, zn) * yn + lax.rem(y + dy, yn)
                target = refs[k] if dy == 0 else refs[zn + dy - 1].at[k]
                for part in range(3):
                    start = pl.multiple_of(part * third + rank * head, 128)
                    copies.append((ins[0].at[:, pl.ds(start, head)], target.at[:, pl.ds(part * head, head)]))
                start = pl.multiple_of(rank * hidden, 128)
                copies.append((ins[1].at[:, pl.ds(start, hidden)], target.at[:, pl.ds(3 * head, hidden)]))
        return copies

    if head % 128 == 0:
        made = mover(grid, plan, [w_qkv, w_up], outs)
    else:
        heads = w_qkv.reshape(rows, 3, ranks, head)
        hiddens = w_up.reshape(rows, ranks, hidden)

        def block(k, dy):
            rank = (grid.z + k) % zn * yn + (grid.y + dy) % yn
            mine = lax.dynamic_index_in_dim(heads, rank, 2, keepdims=False).reshape(rows, 3 * head)
            return jnp.concatenate([mine, lax.dynamic_index_in_dim(hiddens, rank, 1, keepdims=False)], 1)

        made = [block(k, 0) for k in range(zn)] + [
            jnp.stack([block(k, dy) for k in range(zn)]) for dy in range(1, yn)
        ]
    return made[:zn], made[zn:]


def join_columns(grid, groups):
    zn, yn = grid.z_count, grid.y_count
    rows, width = groups[0][1].shape[-2:]
    flat = [item for group in groups for item in group[1:]]

    def body(where_ref, *refs):
        z, y, x, c = [where_ref[i] for i in range(4)]
        for at_group, group in enumerate(groups):
            for way in range(4):
                column, core = lax.rem(x + way % 2, 2), lax.rem(c + way // 2, 2)
                for at, k in enumerate(group[0]):
                    for dy in range(yn):
                        rank = lax.rem(z - k + zn, zn) * yn + lax.rem(y - dy + yn, yn)
                        start = pl.multiple_of(((rank * 2 + column) * 2 + core) * rows, rows)
                        refs[-1][pl.ds(start, rows)] = refs[2 * at_group + way // 2][way % 2, at, dy]

    vmem = pl.BlockSpec(memory_space=pltpu.VMEM)
    return pl.pallas_call(
        body,
        in_specs=[pl.BlockSpec(memory_space=pltpu.SMEM)] + [vmem] * len(flat),
        out_specs=vmem,
        out_shape=low_shape(zn * yn * 4 * rows, width),
        compiler_params=ROOM,
        cost_estimate=LIGHT,
    )(grid.where, *flat)


def join_out(grid, here, there, dense_rows):
    down_rows = here.shape[1] - dense_rows

    def plan(z, y, x, c, ins, outs):
        copies = []
        for way in range(4):
            source = ins[way // 2].at[way % 2]
            at = lax.rem(x + way % 2, 2) * 2 + lax.rem(c + way // 2, 2)
            first = pl.multiple_of(at * dense_rows, dense_rows)
            second = pl.multiple_of(4 * dense_rows + at * down_rows, dense_rows)
            copies.append((source.at[pl.ds(0, dense_rows)], outs[0].at[pl.ds(first, dense_rows)]))
            copies.append((source.at[pl.ds(dense_rows, down_rows)], outs[0].at[pl.ds(second, down_rows)]))
        return copies

    return mover(grid, plan, [here, there], [low_shape(4 * here.shape[1], here.shape[2])])[0]


def halves_in(grid, left, rights):
    tokens, ranks = left.shape[0], grid.rank_count
    widths = [item.shape[1] for item in rights]
    width = sum(widths)
    quad = left.shape[1] // ranks
    rows = quad // 4
    sums = [jax.ShapeDtypeStruct((1, size), WIDE) for size in widths]
    if quad % 128:
        made = contract_first(left, jnp.concatenate(rights, 1)).astype(LOW).reshape(ranks, 2, 2, rows, width)
        pick = lambda index: lax.dynamic_index_in_dim(made, index, 2, keepdims=False)
        return pick(grid.c), pick(1 - grid.c), [jnp.sum(item.astype(WIDE), 0, keepdims=True) for item in rights]
    starts = [sum(widths[:i]) for i in range(len(widths))]

    def body(where_ref, left_ref, *refs):
        core = where_ref[3]
        ins, (kept_ref, away_ref, *sum_refs), made_ref = refs[: len(rights)], refs[len(rights) : -1], refs[-1]
        for ref, start, size in zip(ins, starts, widths):
            made_ref[:, start : start + size] = contract_first(left_ref[...], ref[...]).astype(LOW)
        for column in range(2):
            for out_ref, at in ((kept_ref, core), (away_ref, 1 - core)):
                start = pl.multiple_of((2 * column + at) * rows, rows)
                out_ref[column] = made_ref[pl.ds(start, rows)]

        @pl.when(pl.program_id(0) == 0)
        def _():
            for ref, sum_ref in zip(ins, sum_refs):
                sum_ref[...] = jnp.sum(ref[...].astype(WIDE), 0, keepdims=True)

    half = pl.BlockSpec((None, 2, rows, width), lambda t: (t, 0, 0, 0))
    made = pl.pallas_call(
        body,
        grid=(ranks,),
        in_specs=[pl.BlockSpec(memory_space=pltpu.SMEM), pl.BlockSpec((tokens, quad), lambda t: (0, t))]
        + [whole(item) for item in rights],
        out_specs=[half, half] + [whole(item) for item in sums],
        out_shape=[low_shape(ranks, 2, rows, width)] * 2 + sums,
        scratch_shapes=[pltpu.VMEM((quad, width), LOW)],
        compiler_params=ROOM,
        cost_estimate=cost(8.0),
    )(grid.where, left, *rights)
    return made[0], made[1], made[2:]


def halves_out(grid, attention_low, hidden_low, grad_out):
    tokens, width = grad_out.shape
    dense, down = attention_low.shape[1], hidden_low.shape[1]
    rows = (dense // 4, down // 4)
    shape = low_shape(1, 2, sum(rows), width)
    if dense % 128 or down % 512:
        made = [
            contract_first(item, grad_out).astype(LOW).reshape(2, 2, -1, width) for item in (attention_low, hidden_low)
        ]
        pick = lambda index: jnp.concatenate(
            [lax.dynamic_index_in_dim(item, index, 1, keepdims=False) for item in made], 1
        )[None]
        return pick(grid.c), pick(1 - grid.c)

    def body(where_ref, dense_ref, down_ref, grad_ref, kept_ref, away_ref, made_ref):
        core, step = where_ref[3], pl.program_id(0)

        @pl.when(step == 0)
        def _():
            made_ref[...] = contract_first(dense_ref[...], grad_ref[...]).astype(LOW)
            for column in range(2):
                for out_ref, at in ((kept_ref, core), (away_ref, 1 - core)):
                    start = pl.multiple_of((2 * column + at) * rows[0], rows[0])
                    out_ref[0, column, : rows[0]] = made_ref[pl.ds(start, rows[0])]

        for quarter in range(4):
            for out_ref, at in ((kept_ref, core), (away_ref, 1 - core)):

                @pl.when((step == quarter + 1) & (at == quarter % 2))
                def _(out_ref=out_ref, quarter=quarter):
                    made = contract_first(down_ref[...], grad_ref[...]).astype(LOW)
                    out_ref[0, quarter // 2, rows[0] :] = made

    return pl.pallas_call(
        body,
        grid=(5,),
        in_specs=[
            pl.BlockSpec(memory_space=pltpu.SMEM),
            whole(attention_low),
            pl.BlockSpec((tokens, rows[1]), lambda t: (0, jnp.maximum(t - 1, 0))),
            whole(grad_out),
        ],
        out_specs=[whole(shape)] * 2,
        out_shape=[shape] * 2,
        scratch_shapes=[pltpu.VMEM((dense, width), LOW)],
        compiler_params=ROOM,
        cost_estimate=cost(11.0),
    )(grid.where, attention_low, hidden_low, grad_out)


def halve_columns(grid, kept, arrived):
    count, _, rows, width = kept.shape

    def body(where_ref, kept_ref, arrived_ref, here_ref, there_ref):
        column = where_ref[2]
        for ref, at in ((here_ref, column), (there_ref, 1 - column)):
            ref[...] = sum_low(kept_ref[at], arrived_ref[at])

    both = pl.BlockSpec((None, 2, rows, width), lambda t: (t, 0, 0, 0))
    one = pl.BlockSpec((None, rows, width), lambda t: (t, 0, 0))
    return pl.pallas_call(
        body,
        grid=(count,),
        in_specs=[pl.BlockSpec(memory_space=pltpu.SMEM), both, both],
        out_specs=[one, one],
        out_shape=[low_shape(count, rows, width)] * 2,
        compiler_params=ROOM,
        cost_estimate=cost(4.5),
    )(grid.where, kept, arrived)


class ColumnReturn:
    def __init__(self, grid, kept, arrived):
        zn, yn = grid.z_count, grid.y_count
        self.grid, self.shape = grid, kept.shape[1:]

        def body(z, y, x, c, ins, outs):
            for k in range(zn):
                for at in range(yn):
                    rank = lax.rem(z + k, zn) * yn + at
                    outs[k][at] = sum_low(ins[0][rank], ins[1][rank])

        self.cut = grid.local(body, [kept, arrived], [low_shape(yn, *self.shape)] * zn)

    def begin_z(self):
        self.by_z = {0: self.cut[0]}
        self.moving = {k: self.grid.start(self.cut[k], z=k) for k in self.grid.steps()}

    def end_z(self):
        grid, zn, yn = self.grid, self.grid.z_count, self.grid.y_count
        self.by_z.update(grid.wait(self.moving))

        def body(z, y, x, c, ins, outs):
            for dy in range(yn):
                for k in range(zn):
                    outs[dy][k] = ins[k][lax.rem(y + dy, yn)]

        self.cut = grid.local(body, [self.by_z[k] for k in range(zn)], [low_shape(zn, *self.shape)] * yn)

    def begin_y(self):
        self.moving = [self.grid.start(self.cut[dy], y=dy) for dy in range(1, self.grid.y_count)]

    def end(self):
        return [self.cut[0], *self.grid.wait(self.moving)]


def lay_columns(grid, found, parts):
    zn, yn, ranks = grid.z_count, grid.y_count, grid.rank_count
    rows, width = found[0].shape[1:]
    width = width // parts

    if width % 128 == 0:

        def body(z, y, x, c, ins, outs):
            for dy, ref in enumerate(ins):
                for k in range(zn):
                    rank = lax.rem(z - k + zn, zn) * yn + lax.rem(y - dy + yn, yn)
                    for part in range(parts):
                        start = pl.multiple_of((part * ranks + rank) * width, 128)
                        item = ref[k, :, part * width : (part + 1) * width]
                        outs[0][:, pl.ds(start, width)] = item.astype(WIDE)

        return grid.local(body, found, [jax.ShapeDtypeStruct((rows, parts * ranks * width), WIDE)])[0]
    laid = jnp.zeros((rows, parts, ranks, width), LOW)
    for dy, item in enumerate(found):
        for k in range(zn):
            rank = (grid.z - k) % zn * yn + (grid.y - dy) % yn
            laid = lax.dynamic_update_index_in_dim(laid, item[k].reshape(rows, parts, width), rank, 2)
    return laid.reshape(rows, -1).astype(WIDE)


class VectorGather:
    def __init__(self, grid, row):
        self.grid, self.block = grid, row[None]
        bits = (grid.rank_count * 4).bit_length() - 1
        self.bits = [0, *range(bits - (grid.z_count - 1).bit_length(), bits)]
        self.bits += [bit for bit in range(bits - 1, 0, -1) if bit not in self.bits]
        self.ways = list(self.bits)

    def begin(self):
        self.moving = self.grid.swap(self.block, self.ways.pop(0))

    def end(self):
        self.block = self.grid.pile(self.block, self.grid.wait(self.moving))

    def step(self):
        self.begin()
        self.end()

    def row_of(self, here, device):
        return sum(
            lax.rem(lax.rem(here // (1 << bit), 2) + (device >> bit) % 2, 2) * (1 << at)
            for at, bit in enumerate(self.bits)
        )

    def result(self):
        grid = self.grid
        here = (grid.rank * 2 + grid.x) * 2 + grid.c
        return self.block[jnp.stack([self.row_of(here, device) for device in range(grid.rank_count * 4)])]


def unfold_vectors(grid, gather, sizes, block_len, seqs):
    zn, yn, block = grid.z_count, grid.y_count, gather.block
    ranks, devices = grid.rank_count, grid.rank_count * 4
    cuts = [sum(sizes[:i]) for i in range(len(sizes) + 1)]
    slots = sizes[6] // 2
    head, hidden = sizes[2] * devices // (3 * ranks), sizes[4] * devices // ranks
    third = sizes[2] * devices // 3
    rows = 8 * block_len
    length = yn * rows
    half = ROT // 2
    lane = np.arange(128) % HEAD
    freqs = np.float32(ROPE_BASE) ** (-((lane % half).astype(np.float32) * np.float32(2.0 / ROT)))
    turned = (lane < ROT).astype(np.float32)
    sign = np.where(lane < half, -1.0, 1.0).astype(np.float32) * turned
    marks = jnp.asarray(np.stack([freqs.astype(np.float32), turned, sign]))

    def body(where_ref, block_ref, mark_ref, *refs):
        z, y, x, c = [where_ref[i] for i in range(4)]
        gain_ref, shift_ref, in_ref, out_ref, cos_ref, sin_ref, column_ref, row_ref = refs[:8]
        qkv_ref, up_ref = refs[8:]
        here_at = ((z * yn + y) * 2 + x) * 2 + c
        for device in range(devices):
            row = block_ref[pl.ds(gather.row_of(here_at, device), 1), :]
            item = [row[:, cuts[i] : cuts[i + 1]] for i in range(6)]
            here = [pl.ds(device * sizes[i], sizes[i]) for i in range(6)]
            gain_ref[:, here[0]] = item[0]
            shift_ref[:, here[1]] = item[1]
            qkv_ref[:, here[2]] = item[2]
            out_ref[:, here[3]] = item[3] + item[5]
            up_ref[:, here[4]] = item[4]
        rank = z * yn + y
        for part in range(3):
            start = pl.multiple_of(part * third + rank * head, 128)
            in_ref[:, part * head : (part + 1) * head] = qkv_ref[:, pl.ds(start, head)]
        in_ref[:, 3 * head :] = up_ref[:, pl.ds(pl.multiple_of(rank * hidden, 128), hidden)]

        def order_row(source):
            parts = [
                jnp.where(source == at, block_ref[pl.ds(gather.row_of(here_at, at * 4 * yn), 1), :], 0.0)
                for at in range(zn)
            ]
            return sum(parts)

        parity = lax.rem(z + x, 2)
        slot_at = lax.broadcasted_iota(jnp.int32, (1, slots), 1)
        tall = lax.broadcasted_iota(jnp.int32, (block_len, 128), 0).astype(WIDE)
        flat = lax.broadcasted_iota(jnp.int32, (1, block_len), 1).astype(WIDE)
        for i in range(seqs):
            row = order_row(lax.rem(z - 2 * i - parity + 2 * zn, zn))
            order = jnp.where(c == 0, row[:, cuts[6] : cuts[6] + slots], row[:, cuts[6] + slots : cuts[7]])
            for dy in range(yn):
                for near in range(4):
                    ctx = (lax.rem(y - dy + yn, yn) * 2 + lax.rem(x + near // 2, 2)) * 2 + lax.rem(c + near, 2)
                    for at in range(2):
                        value = jnp.sum(jnp.where(slot_at == 2 * ctx + at, order, 0.0), 1, keepdims=True) * block_len
                        place = value + tall
                        angle = place * mark_ref[0:1, :]
                        inside = (near * 2 + at) * block_len
                        here = pl.ds((dy * seqs + i) * rows + inside, block_len)
                        cos_ref[here, :] = jnp.where(mark_ref[1:2, :] > 0.0, jnp.cos(angle), 1.0)
                        sin_ref[here, :] = jnp.sin(angle) * mark_ref[2:3, :]
                        there = dy * rows + inside
                        column_ref[pl.ds(i * length + there, block_len), :] = place[:, :1]
                        row_ref[i, :, there : there + block_len] = value + flat

    wide = lambda *shape: jax.ShapeDtypeStruct(shape, WIDE)
    tokens = seqs * length
    vmem = pl.BlockSpec(memory_space=pltpu.VMEM)
    return pl.pallas_call(
        body,
        in_specs=[pl.BlockSpec(memory_space=pltpu.SMEM), vmem, vmem],
        out_specs=[vmem] * 8,
        out_shape=[
            wide(1, sizes[0] * devices), wide(1, sizes[1] * devices), wide(1, 3 * head + hidden),
            wide(1, sizes[3] * devices), wide(tokens, 128), wide(tokens, 128), wide(tokens, 1), wide(seqs, 1, length),
        ],
        scratch_shapes=[
            pltpu.VMEM((1, 3 * third), WIDE), pltpu.VMEM((1, hidden * ranks), WIDE),
        ],
        compiler_params=ROOM,
        cost_estimate=LIGHT,
    )(grid.where, block, marks)


class VectorSum:
    def __init__(self, grid, rows):
        self.grid, self.terms, self.bit = grid, [rows], 0

    def begin(self):
        grid, bit, yn = self.grid, self.bit, self.grid.y_count
        count, width = self.terms[0].shape

        def body(z, y, x, c, ins, outs):
            own = lax.rem((((z * yn + y) * 2 + x) * 2 + c) // (1 << bit), 2)
            for at in range(count // 2):
                for out, pick in zip(outs, (own, 1 - own)):
                    row = pl.ds(2 * at + pick, 1)
                    out[at : at + 1, :] = sum(ref[row, :] for ref in ins)

        kept, away = grid.local(body, self.terms, [jax.ShapeDtypeStruct((count // 2, width), WIDE)] * 2)
        self.kept, self.moving = kept, grid.swap(away, bit)
        self.bit += 1

    def end(self):
        self.terms = [self.kept, self.grid.wait(self.moving)]

    def result(self):
        while self.terms[0].shape[0] > 1:
            self.begin()
            self.end()
        return sum(self.terms)[0]


def fold_vectors(grid, gains, shifts, sums_qkv, sum_up, cotangent, sizes):
    devices, ranks, yn = grid.rank_count * 4, grid.rank_count, grid.y_count
    head, hidden = sums_qkv[0].shape[1], sum_up.shape[1]
    third = head * ranks
    chunks = (sizes[0], sizes[1], sizes[2], sizes[3], sizes[4])
    starts = [sum(chunks[:i]) for i in range(len(chunks))]
    count = len(gains)

    def body(where_ref, *refs):
        ins, out_ref, qkv_ref, up_ref = refs[:-3], refs[-3], refs[-2], refs[-1]
        rank = where_ref[0] * yn + where_ref[1]
        gain = sum(ref[...] for ref in ins[:count])
        shift = sum(ref[...] for ref in ins[count : 2 * count])
        grad = jnp.sum(ins[2 * count + 4][...].astype(WIDE), (0, 1))[None]
        qkv_ref[...] = jnp.zeros_like(qkv_ref)
        up_ref[...] = jnp.zeros_like(up_ref)
        for part in range(3):
            qkv_ref[:, pl.ds(pl.multiple_of(part * third + rank * head, 128), head)] = ins[2 * count + part][...]
        up_ref[:, pl.ds(pl.multiple_of(rank * hidden, 128), hidden)] = ins[2 * count + 3][...]
        for device in range(devices):
            for start, size, whole_row in zip(starts, chunks, (gain, shift, qkv_ref, grad, up_ref)):
                item = whole_row[:, device * size : (device + 1) * size]
                out_ref[device : device + 1, start : start + size] = item

    vmem = pl.BlockSpec(memory_space=pltpu.VMEM)
    inputs = [*gains, *shifts, *sums_qkv, sum_up, cotangent]
    return pl.pallas_call(
        body,
        in_specs=[pl.BlockSpec(memory_space=pltpu.SMEM)] + [vmem] * len(inputs),
        out_specs=vmem,
        out_shape=jax.ShapeDtypeStruct((devices, sum(chunks)), WIDE),
        scratch_shapes=[pltpu.VMEM((1, 3 * third), WIDE), pltpu.VMEM((1, hidden * ranks), WIDE)],
        compiler_params=ROOM,
        cost_estimate=cost(3.0),
    )(grid.where, *inputs)


def contract_last(left, right):
    return lax.dot_general(
        left, right, (((1,), (1,)), ((), ())), preferred_element_type=WIDE
    )


def contract_first(left, right):
    return lax.dot_general(
        left, right, (((0,), (0,)), ((), ())), preferred_element_type=WIDE
    )


def whole(array):
    return pl.BlockSpec(array.shape, lambda *at: (0,) * array.ndim)


def swap_halves(field):
    width = field.shape[-1]
    half = ROT // 2
    if width % 128 == 0:
        after = pltpu.roll(field, width - half, 1)
        before = pltpu.roll(field, half, 1)
    else:
        after = jnp.concatenate([field[:, half:], field[:, :half]], 1)
        before = jnp.concatenate([field[:, width - half :], field[:, : width - half]], 1)
    lane = lax.broadcasted_iota(jnp.int32, field.shape, 1) % HEAD
    return jnp.where(lane < half, after, before)


def turned_heads(query_ref, key_ref, value_ref, cos_ref, sin_ref):
    rows = (-1, cos_ref.shape[-1])
    cosine, sine = cos_ref[...].reshape(rows), sin_ref[...].reshape(rows)
    query = query_ref[...].reshape(rows)
    query_all = (query * cosine + swap_halves(query) * sine).astype(LOW)
    key = key_ref[...].reshape(rows)
    key_all = (key * cosine + swap_halves(key) * sine).astype(LOW)
    value_all = value_ref[...].reshape(rows).astype(LOW)
    return cosine, sine, query_all, key_all, value_all


def probability_of(query_low, key_low, allowed):
    scores = jnp.where(allowed, contract_last(query_low, key_low) * HEAD**-0.5, -1e30)
    weights = jnp.exp(scores - jnp.max(scores, -1, keepdims=True))
    return weights * (1.0 / jnp.sum(weights, -1, keepdims=True))


def forward_body(
    query_ref, key_ref, value_ref, cos_ref, sin_ref, column_ref, row_ref, mixed_ref, kept_ref
):
    _, _, query_all, key_all, value_all = turned_heads(query_ref, key_ref, value_ref, cos_ref, sin_ref)
    allowed = row_ref[...] <= column_ref[...]
    outs = []
    for at in range(query_all.shape[1] // HEAD):
        part = slice(at * HEAD, (at + 1) * HEAD)
        probability_low = probability_of(query_all[:, part], key_all[:, part], allowed).astype(LOW)
        kept_ref[at] = probability_low
        outs.append(jnp.dot(probability_low, value_all[:, part], preferred_element_type=WIDE))
    mixed_ref[...] = jnp.concatenate(outs, 1).astype(LOW).reshape(mixed_ref.shape)


def backward_body(
    query_ref, key_ref, value_ref, cos_ref, sin_ref, grad_ref, kept_ref, grad_query_ref, grad_key_ref, grad_value_ref
):
    cosine, sine, query_all, key_all, value_all = turned_heads(query_ref, key_ref, value_ref, cos_ref, sin_ref)
    grad_all = grad_ref[...].reshape(value_all.shape)
    scale = HEAD**-0.5
    outs = []
    for at in range(query_all.shape[1] // HEAD):
        part = slice(at * HEAD, (at + 1) * HEAD)
        query_low, key_low = query_all[:, part], key_all[:, part]
        value_low, grad_low = value_all[:, part], grad_all[:, part]
        probability_low = kept_ref[at]
        mixed = jnp.dot(probability_low, value_low, preferred_element_type=WIDE)
        delta = jnp.sum(grad_low.astype(WIDE) * mixed, -1, keepdims=True)
        grad_probability = contract_last(grad_low, value_low)
        grad_scores = (probability_low.astype(WIDE) * (grad_probability - delta)).astype(LOW)
        grad_value = contract_first(probability_low, grad_low)
        grad_query = jnp.dot(grad_scores, key_low, preferred_element_type=WIDE) * scale
        grad_key = contract_first(grad_scores, query_low) * scale
        outs.append((grad_query, grad_key, grad_value))
    grad_query, grad_key, grad_value = [jnp.concatenate(item, 1) for item in zip(*outs)]
    block = grad_query_ref.shape
    grad_query = grad_query * cosine - swap_halves(grad_query) * sine
    grad_key = grad_key * cosine - swap_halves(grad_key) * sine
    grad_query_ref[...] = grad_query.astype(LOW).reshape(block)
    grad_key_ref[...] = grad_key.astype(LOW).reshape(block)
    grad_value_ref[...] = grad_value.astype(LOW).reshape(block)


def attend(qkv, cosine, sine, yn, seqs, column=None, row=None, grad_attention=None, kept=None):
    backward = grad_attention is not None
    tokens, width = qkv.shape[0], qkv.shape[1] // 3
    lanes = min(128, width)
    length = tokens // seqs
    rows = length // yn
    block = (yn, None, rows, lanes)
    cut = lambda array: array.reshape(yn, seqs, rows, array.shape[-1])
    field = pl.BlockSpec(block, lambda s, h: (0, s, 0, h))
    table = pl.BlockSpec(block, lambda s, h: (0, s, 0, 0))
    square = pl.BlockSpec((None, lanes // HEAD, length, length), lambda s, h: (s, h, 0, 0))
    low = low_shape(yn, seqs, rows, width)
    if width % 128 == 0:
        thirds = [cut(qkv)] * 3
        blocks = [
            pl.BlockSpec(block, lambda s, h, part=part: (0, s, 0, part * (width // lanes) + h)) for part in range(3)
        ]
    else:
        thirds = [cut(qkv[:, part * width : (part + 1) * width]) for part in range(3)]
        blocks = [field] * 3
    inputs = [*thirds, cut(cosine[:, :lanes]), cut(sine[:, :lanes])]
    blocks = blocks + [table, table]
    if backward:
        body, inputs, blocks = backward_body, inputs + [cut(grad_attention), kept], blocks + [field, square]
        outs, out_blocks = [low] * 3, [field] * 3
    else:
        body, inputs = forward_body, inputs + [column, row]
        blocks = blocks + [
            pl.BlockSpec((length, 1), lambda s, h: (s, 0)),
            pl.BlockSpec((None, 1, length), lambda s, h: (s, 0, 0)),
        ]
        outs, out_blocks = [low, low_shape(seqs, width // HEAD, length, length)], [field, square]
    made = pl.pallas_call(
        body,
        grid=(seqs, width // lanes),
        in_specs=blocks,
        out_specs=out_blocks,
        out_shape=outs,
        compiler_params=pltpu.CompilerParams(vmem_limit_bytes=20 * 1024 * 1024),
        cost_estimate=cost(13.0),
    )(*inputs)
    return [item.reshape(tokens, width) if item.shape == low.shape else item for item in made]


def normalize(parts, gain_vec, shift_vec):
    span, width = parts[0].shape
    tile = min(span, 128)
    each = span // tile

    def body(*refs):
        step = pl.program_id(0)
        gain_ref, shift_ref, normed_ref, unit_ref = refs[len(parts) :]
        for at, ref in enumerate(refs[: len(parts)]):

            @pl.when(step // each == at)
            def _(ref=ref):
                inputs = ref[...].astype(WIDE)
                centre = inputs - jnp.mean(inputs, -1, keepdims=True)
                spread = jnp.mean(centre * centre, -1, keepdims=True)
                unit = centre * lax.rsqrt(spread + NORM_EPS)
                normed_ref[...] = (unit * gain_ref[...] + shift_ref[...]).astype(LOW)
                unit_ref[...] = unit.astype(LOW)

    block = (tile, width)
    clamp = lambda at: pl.BlockSpec(block, lambda t: (jnp.clip(t - at * each, 0, each - 1), 0))
    vector = pl.BlockSpec((1, width), lambda t: (0, 0))
    return pl.pallas_call(
        body,
        grid=(len(parts) * each,),
        in_specs=[clamp(at) for at in range(len(parts))] + [vector, vector],
        out_specs=[pl.BlockSpec(block, lambda t: (t, 0))] * 2,
        out_shape=[low_shape(len(parts) * span, width)] * 2,
        compiler_params=ROOM,
        cost_estimate=cost(8.0),
    )(*parts, gain_vec, shift_vec)


def bend(up):
    bent = jnp.tanh(GELU_SCALE * (up + GELU_CUBIC * up * up * up))
    slope = 0.5 * (1.0 + bent) + 0.5 * up * (1.0 - bent * bent) * GELU_SCALE * (1.0 + 3.0 * GELU_CUBIC * up * up)
    return (0.5 * up * (1.0 + bent)).astype(LOW), slope.astype(LOW)


def project(normed_low, w_in, bias, split):
    tokens, total = normed_low.shape[0], w_in.shape[1]
    if split % 256 or total % 256:
        made = jnp.dot(normed_low, w_in, preferred_element_type=WIDE) + bias
        return made[:, :split], *bend(made[:, split:])
    heads = split // 256

    def body(normed_ref, w_ref, bias_ref, qkv_ref, hidden_ref, slope_ref):
        step = pl.program_id(0)
        made = jnp.dot(normed_ref[...], w_ref[...], preferred_element_type=WIDE) + bias_ref[...]

        @pl.when(step < heads)
        def _():
            qkv_ref[...] = made

        @pl.when(step >= heads)
        def _():
            hidden_ref[...], slope_ref[...] = bend(made)

    late = pl.BlockSpec((tokens, 256), lambda t: (0, jnp.maximum(t - heads, 0)))
    return pl.pallas_call(
        body,
        grid=(total // 256,),
        in_specs=[
            whole(normed_low),
            pl.BlockSpec((w_in.shape[0], 256), lambda t: (0, t)),
            pl.BlockSpec((1, 256), lambda t: (0, t)),
        ],
        out_specs=[pl.BlockSpec((tokens, 256), lambda t: (0, jnp.minimum(t, heads - 1))), late, late],
        out_shape=[jax.ShapeDtypeStruct((tokens, split), WIDE)] + [low_shape(tokens, total - split)] * 2,
        compiler_params=ROOM,
        cost_estimate=cost(16.0),
    )(normed_low, w_in, bias)


def project_back(grad_out, w_out, slope, dense_rows):
    tokens, width = grad_out.shape
    if dense_rows % 256 or w_out.shape[0] % 256:
        return (
            contract_last(grad_out, w_out[:dense_rows]).astype(LOW),
            (contract_last(grad_out, w_out[dense_rows:]) * slope.astype(WIDE)).astype(LOW),
        )
    first = dense_rows // 256

    def body(grad_ref, w_ref, slope_ref, attention_ref, up_ref):
        step = pl.program_id(0)
        made = contract_last(grad_ref[...], w_ref[...])

        @pl.when(step < first)
        def _():
            attention_ref[...] = made.astype(LOW)

        @pl.when(step >= first)
        def _():
            up_ref[...] = (made * slope_ref[...].astype(WIDE)).astype(LOW)

    late = pl.BlockSpec((tokens, 256), lambda t: (0, jnp.maximum(t - first, 0)))
    return pl.pallas_call(
        body,
        grid=(w_out.shape[0] // 256,),
        in_specs=[whole(grad_out), pl.BlockSpec((256, width), lambda t: (t, 0)), late],
        out_specs=[pl.BlockSpec((tokens, 256), lambda t: (0, jnp.minimum(t, first - 1))), late],
        out_shape=[low_shape(tokens, dense_rows), low_shape(*slope.shape)],
        compiler_params=ROOM,
        cost_estimate=cost(10.0),
    )(grad_out, w_out, slope)


def out_part(attention_low, hidden_low, w_out, dy, rows, seqs):
    head, hidden, width = attention_low.shape[1], hidden_low.shape[1], w_out.shape[1]
    each = rows // seqs
    if head % 128:
        here = slice(dy * rows, (dy + 1) * rows)
        joined = jnp.concatenate([attention_low[here], hidden_low[here]], 1)
        made = jnp.dot(joined, w_out, preferred_element_type=WIDE).astype(LOW)
        return [made[i * each : (i + 1) * each] for i in range(seqs)]

    def body(attention_ref, hidden_ref, w_ref, *out_refs):
        made = jnp.dot(attention_ref[...], w_ref[:head], preferred_element_type=WIDE)
        made += jnp.dot(hidden_ref[...], w_ref[head:], preferred_element_type=WIDE)
        for i, out_ref in enumerate(out_refs):
            out_ref[...] = made[i * each : (i + 1) * each].astype(LOW)

    tile = min(width, 512)
    return pl.pallas_call(
        body,
        grid=(width // tile,),
        in_specs=[
            pl.BlockSpec((rows, head), lambda t: (dy, 0)),
            pl.BlockSpec((rows, hidden), lambda t: (dy, 0)),
            pl.BlockSpec((w_out.shape[0], tile), lambda t: (0, t)),
        ],
        out_specs=[pl.BlockSpec((each, tile), lambda t: (0, t))] * seqs,
        out_shape=[low_shape(each, width)] * seqs,
        compiler_params=ROOM,
        cost_estimate=cost(150.0),
    )(attention_low, hidden_low, w_out)


def in_part(grads, w_in, unit_low, dy, rows, seqs):
    widths = [item.shape[1] for item in grads]
    starts = [sum(widths[:i]) for i in range(len(widths))]
    width = w_in.shape[0]
    each = rows // seqs
    if widths[0] % 128:
        here = slice(dy * rows, (dy + 1) * rows)
        made = contract_last(jnp.concatenate([item[here] for item in grads], 1), w_in)
        sums = [jnp.sum(item, 0, keepdims=True) for item in (made * unit_low[here].astype(WIDE), made)]
        return [made[i * each : (i + 1) * each].astype(LOW) for i in range(seqs)], *sums

    def body(*refs):
        w_ref, unit_ref, *out_refs, gain_ref, shift_ref = refs[len(grads) :]
        made = None
        for ref, start, size in zip(refs, starts, widths):
            term = contract_last(ref[...], w_ref[:, start : start + size])
            made = term if made is None else made + term
        for i, out_ref in enumerate(out_refs):
            out_ref[...] = made[i * each : (i + 1) * each].astype(LOW)
        gain_ref[...] = jnp.sum(made * unit_ref[...].astype(WIDE), 0, keepdims=True)
        shift_ref[...] = jnp.sum(made, 0, keepdims=True)

    tile = min(width, 512)
    vector = pl.BlockSpec((1, tile), lambda t: (0, t))
    *made, gain, shift = pl.pallas_call(
        body,
        grid=(width // tile,),
        in_specs=[pl.BlockSpec((rows, size), lambda t: (dy, 0)) for size in widths]
        + [
            pl.BlockSpec((tile, w_in.shape[1]), lambda t: (t, 0)),
            pl.BlockSpec((rows, tile), lambda t: (dy, t)),
        ],
        out_specs=[pl.BlockSpec((each, tile), lambda t: (0, t))] * seqs + [vector, vector],
        out_shape=[low_shape(each, width)] * seqs + [jax.ShapeDtypeStruct((1, width), WIDE)] * 2,
        compiler_params=ROOM,
        cost_estimate=cost(7.0),
    )(*grads, w_in, unit_low)
    return made, gain, shift


def rotary_tables(places):
    lane = jnp.arange(128, dtype=jnp.int32) % HEAD
    half = ROT // 2
    freqs = jnp.asarray(ROPE_BASE, WIDE) ** (-((lane % half).astype(WIDE) * (2.0 / ROT)))
    angles = places.astype(WIDE)[:, None] * freqs
    turned = (lane < ROT)[None, :]
    sign = jnp.where(lane < half, -1.0, 1.0)
    return jnp.where(turned, jnp.cos(angles), 1.0), jnp.where(turned, jnp.sin(angles) * sign, 0.0)


def unfold_rows(grid, gathered, sizes, block_len, group_seqs):
    zn, yn, ranks = grid.z_count, grid.y_count, grid.rank_count
    cuts = [sum(sizes[:i]) for i in range(len(sizes) + 1)]
    gain_full, shift_full, bias_qkv, bias_dense, bias_up, bias_down = [
        gathered[:, cuts[i] : cuts[i + 1]].reshape(-1).astype(WIDE) for i in range(6)
    ]
    orders = gathered[:: grid.ctx_count, cuts[6] :].reshape(zn, 2, -1).astype(jnp.int32)

    ctx_from = jnp.stack(
        [
            (((grid.y - dy) % yn) * 2 + (grid.x ^ dx)) * 2 + (grid.c ^ dc)
            for dy in range(yn)
            for dx in range(2)
            for dc in range(2)
        ]
    )
    z_from = jnp.stack([(grid.z - 2 * i - grid.parity) % zn for i in range(group_seqs)])
    own_orders = lax.dynamic_index_in_dim(orders, grid.c, 1, keepdims=False)[z_from]
    slots = (ctx_from[:, None] * 2 + jnp.arange(2)).reshape(-1)
    places = own_orders[:, slots].reshape(group_seqs, yn, -1).swapaxes(0, 1)
    places = (places[..., None] * block_len + jnp.arange(block_len)).reshape(-1)
    cosine, sine = rotary_tables(places)


    bias_in = jnp.concatenate(
        [
            lax.dynamic_index_in_dim(bias_qkv.reshape(3, ranks, -1), grid.rank, 1, keepdims=False).reshape(-1),
            place(bias_up.reshape(ranks, -1), grid.rank),
        ]
    )
    column = places.reshape(yn, group_seqs, -1).swapaxes(0, 1).reshape(-1).astype(WIDE)
    return (
        gain_full[None], shift_full[None], bias_in[None], (bias_dense + bias_down)[None], cosine, sine,
        column[:, None], column.reshape(group_seqs, 1, -1),
    )


def fold_rows(grid, gain, shift, sums_qkv, sum_up, cotangent):
    ranks, devices = grid.rank_count, grid.rank_count * 4

    def laid(part, count):
        whole_rows = jnp.zeros((count, ranks, part.shape[-1]), WIDE)
        whole_rows = lax.dynamic_update_index_in_dim(whole_rows, part, grid.rank, 1)
        return whole_rows.reshape(devices, -1)

    return jnp.concatenate(
        [
            gain.reshape(devices, -1),
            shift.reshape(devices, -1),
            laid(jnp.concatenate(sums_qkv, 0), 3),
            jnp.sum(cotangent.astype(WIDE), (0, 1)).reshape(devices, -1),
            laid(sum_up, 1),
        ],
        1,
    )


def on_device(
    tokens, block_order, ln_gain, ln_bias, w_qkv, b_qkv, w_dense, b_dense, w_fc1, b_fc1, w_fc2, b_fc2, cotangent,
):
    grid = Grid()
    seqs, span, model_width = tokens.shape
    zn, yn, ranks = grid.z_count, grid.y_count, grid.rank_count
    device_count = ranks * 4
    length = span * grid.ctx_count
    block_len = span // 2
    group_seqs = zn // 2
    head_width = model_width // ranks

    split = 3 * head_width
    dense_rows = 4 * w_dense.shape[0]
    rows = group_seqs * length // yn
    seq_rows = length // yn
    last = group_seqs - 1

    def ordered(spreads):
        return [spreads[i].parts[dy] for dy in range(yn) for i in range(group_seqs)]

    def ordered(spreads):
        return [spreads[i].parts[dy] for dy in range(yn) for i in range(group_seqs)]

    def rows_of(array, i):
        return array[i * seq_rows : (i + 1) * seq_rows]

    def across_x(ks):
        own = near[ks[0]][None] if len(ks) == 1 else grid.pile(*[near[k][None] for k in ks])
        return ks, own, grid.start(own, x=1)

    def both_columns(group):
        ks, own, moving = group
        return ks, grid.pile(own[None], grid.wait(moving)[None])

    away, own_tokens, own_cotangent = part_cores(grid, tokens, cotangent)
    moving = grid.start(away, c=1)
    down_moving = grid.start(w_fc2, x=1)
    others = grid.wait(moving)
    ring = Ring(grid, grid.pile(own_tokens, others[:span]))
    ring.begin(1)
    ahead, across = cut_columns(grid, *grid.after((w_qkv, w_fc1)))
    across = [grid.start(part, y=dy + 1) for dy, part in enumerate(across)]
    vectors = (ln_gain, ln_bias, b_qkv, b_dense, b_fc1, b_fc2, block_order.reshape(-1))
    sizes = [item.shape[0] for item in vectors]
    vectors = jnp.concatenate([item.astype(WIDE) for item in grid.after(vectors)])
    gather = VectorGather(grid, vectors)
    gather.begin()
    down_moving = grid.wait(down_moving)
    dense_moving = grid.start(w_dense, x=1)
    gather.end()
    ring.end()
    ring.begin(2)
    dense_moving = grid.wait(dense_moving)
    gather.begin()
    spreads = [Spread(grid, ring.pair(0))]
    across = grid.wait(across)
    gather.end()

    def pack(z, y, x, c, ins, outs):
        for k in range(zn):
            outs[k][0] = ins[k][...]
            for dy in range(1, yn):
                outs[k][dy] = ins[zn + dy - 1][k]

    near = grid.local(pack, [*ahead, *across], [low_shape(yn, *ahead[0].shape)] * zn)
    near = dict(enumerate(near))
    near[zn - 1] = grid.start(near[zn - 1], z=-1)
    gather.begin()
    spreads[0].end_x()
    spreads[0].begin_y()
    ring.end()
    rest = [k for k in grid.steps() if k != zn - 1]
    moving = {rest[0]: grid.start(near[rest[0]], z=rest[0])}
    group_own = across_x([0])
    near[zn - 1] = grid.wait(near[zn - 1])
    gather.end()
    ring.finish()
    moving.update({k: grid.start(near[k], z=k) for k in rest[1:]})
    spreads += [Spread(grid, ring.pair(i)) for i in range(1, group_seqs)]
    gather.begin()

    def stack_out(z, y, x, c, ins, outs):
        for at in range(2):
            dense = ins[2 * at].shape[0]
            outs[0][at, :dense] = ins[2 * at][...]
            outs[0][at, dense:] = ins[2 * at + 1][...]

    out_rows = grid.local(
        stack_out,
        grid.after([w_dense, w_fc2, dense_moving, down_moving]),
        [low_shape(2, w_dense.shape[0] + w_fc2.shape[0], model_width)],
    )[0]
    group_own = both_columns(group_own)
    for spread in spreads[1:]:
        spread.end_x()
    spreads[1].begin_y()
    group_far = across_x([zn - 1])
    spreads[0].end_y()
    gather.end()
    near.update(grid.wait(moving))
    group_rest = across_x(rest)
    met_grad = grid.pile(own_cotangent, others[span:])
    ring = Ring(grid, met_grad)
    ring.begin(1)
    group_far = both_columns(group_far)
    gather.begin()

    def beside(z, y, x, c, ins, outs):
        for at, ref in enumerate(ins):
            outs[0][:, at : at + 1] = ref[...]

    first = group_own[0] + group_far[0]
    first_rows = grid.local(beside, [group_own[1], group_far[1]], [low_shape(2, 2, *group_own[1].shape[2:])])[0]
    gather.end()
    while gather.ways:
        gather.step()
    if head_width % 128 == 0:
        unfolded = grid.hold(unfold_vectors(grid, gather, sizes, block_len, group_seqs))
    else:
        unfolded = unfold_rows(grid, gather.result(), sizes, block_len, group_seqs)
    gain_full, shift_full, bias_in, bias_out, cosine, sine, column, row = unfolded
    first_moving = grid.start(first_rows, c=1)
    spreads[1].end_y()
    for spread in spreads[2:]:
        spread.begin_y()
        spread.end_y()
    out_moving = grid.start(out_rows, c=1)
    normed_low, unit_low = grid.hold(normalize(ordered(spreads), gain_full, shift_full))
    first_moving = grid.wait(first_moving)
    group_rest = both_columns(group_rest)
    rest_moving = grid.start(group_rest[1], c=1)
    out_moving = grid.wait(out_moving)
    w_out = grid.hold(join_out(grid, *grid.after((out_rows, out_moving)), w_dense.shape[0]))
    ring.end()
    grads = [Spread(grid, ring.pair(0))]
    ring.begin(2)
    rest_moving = grid.wait(rest_moving)
    w_in = grid.hold(join_columns(grid, [(first, first_rows, first_moving), (*group_rest, rest_moving)]))
    grads[0].end_x()
    grads[0].begin_y()
    grid.page()
    ring.end()
    ring.finish()
    grads += [Spread(grid, ring.pair(i)) for i in range(1, group_seqs)]

    qkv, hidden_low, slope = grid.hold(project(grid.after(normed_low), w_in, bias_in, split))
    grid.pages = False
    for spread in grads[1:]:
        spread.end_x()
    grads[1].begin_y()
    attention_low, kept = grid.hold(attend(grid.after(qkv), cosine, sine, yn, group_seqs, column=column, row=row))
    out_parts = {}
    for dy in range(yn - 1, -1, -1):
        if dy == 0:
            grads[0].end_y()
        out_parts[dy] = grid.hold(out_part(grid.after(attention_low), hidden_low, w_out, dy, rows, group_seqs))
    grads[1].end_y()
    for spread in grads[2:]:
        spread.begin_y()
        spread.end_y()

    out_sums = {i: TokenSum(grid, out_parts[yn - 1][i], yn - 1) for i in range(last, -1, -1)}
    grad_out = grid.pile(*grid.after(ordered(grads)))
    grad_attention_low, grad_up_low = grid.hold(project_back(grad_out, w_out, slope, dense_rows))

    def finish_y(sums, parts, i):
        for dy in range(yn - 2, -1, -1):
            sums[i].more(parts[dy][i])

    grads_qkv = grid.hold(
        attend(grid.after(qkv), cosine, sine, yn, group_seqs, grad_attention=grad_attention_low, kept=kept)
    )
    grads_in = [*grads_qkv, grad_up_low]
    finish_y(out_sums, out_parts, last)
    out_sums[last].begin_x()
    in_parts, gain_parts, shift_parts = {}, {}, {}

    def make_in_part(dy):
        in_parts[dy], gain_parts[dy], shift_parts[dy] = grid.hold(
            in_part(grid.after(grads_in), w_in, unit_low, dy, rows, group_seqs)
        )

    make_in_part(yn - 1)
    in_sums = {last: TokenSum(grid, in_parts[yn - 1][last], yn - 1)}
    out_ring = RingSum(grid)
    out_ring.pieces[2 * last], out_ring.pieces[2 * last + 1] = out_sums[last].end_x()
    for i in range(last - 1, 0, -1):
        finish_y(out_sums, out_parts, i)
        out_sums[i].begin_x()
        out_ring.pieces[2 * i], out_ring.pieces[2 * i + 1] = out_sums[i].end_x()
    out_ring.begin_far()
    finish_y(out_sums, out_parts, 0)
    out_sums[0].begin_x()
    for dy in range(yn - 2, -1, -1):
        make_in_part(dy)
    up_kept, up_away, (sum_up,) = grid.hold(halves_in(grid, grid.after(normed_low), [grad_up_low]))
    up_moving = grid.start(up_away, c=1)
    out_ring.pieces[0], out_ring.pieces[1] = out_sums[0].end_x()
    out_ring.end_far()
    out_ring.begin_near()
    finish_y(in_sums, in_parts, last)
    for i in range(last - 1, -1, -1):
        in_sums[i] = TokenSum(grid, in_parts[yn - 1][i], yn - 1)
    in_sums[last].begin_x()
    grid.turn()
    up_kept, up_away = grid.hold(halve_columns(grid, up_kept, grid.wait(up_moving)))
    up_moving = grid.start(up_away, x=1)
    qkv_kept, qkv_away, sums_qkv = grid.hold(halves_in(grid, grid.after(normed_low), grads_qkv))
    qkv_moving = grid.start(qkv_away, c=1)
    out_ring.end_near()
    if head_width % 128 == 0:
        sums = fold_vectors(
            grid, list(gain_parts.values()), list(shift_parts.values()), sums_qkv, sum_up, cotangent, sizes
        )
    else:
        sums = fold_rows(
            grid, sum(gain_parts.values()), sum(shift_parts.values()), sums_qkv, sum_up, cotangent
        )
    sums = VectorSum(grid, grid.hold(sums))
    sums.begin()
    in_ring = RingSum(grid)
    in_ring.pieces[2 * last], in_ring.pieces[2 * last + 1] = in_sums[last].end_x()
    for i in range(last - 1, 0, -1):
        finish_y(in_sums, in_parts, i)
        in_sums[i].begin_x()
        in_ring.pieces[2 * i], in_ring.pieces[2 * i + 1] = in_sums[i].end_x()
    sums.end()
    in_ring.begin_far()
    sums.begin()
    out_kept, out_away = grid.hold(halves_out(grid, *grid.after((attention_low, hidden_low)), grad_out))
    finish_y(in_sums, in_parts, 0)
    in_sums[0].begin_x()
    sums.end()
    up_return = ColumnReturn(grid, up_kept, grid.wait(up_moving))
    up_return.begin_z()
    in_ring.end_far()
    sums.begin()
    out_moving = grid.start(out_away, c=1)
    grid.turn()
    projected = out_ring.end()
    qkv_moving = grid.wait(qkv_moving)
    sums.end()
    qkv_kept, qkv_away = grid.hold(halve_columns(grid, qkv_kept, qkv_moving))
    qkv_moving = grid.start(qkv_away, x=1)
    out_kept, out_away = grid.hold(halve_columns(grid, out_kept, grid.wait(out_moving)))
    out_moving = grid.start(out_away, x=1)
    in_ring.pieces[0], in_ring.pieces[1] = in_sums[0].end_x()
    up_return.end_z()
    in_ring.begin_near()
    qkv_return = ColumnReturn(grid, qkv_kept, grid.wait(qkv_moving))
    sums.begin()
    qkv_return.begin_z()
    up_return.begin_y()
    sums.end()
    sums.begin()
    in_ring.end_near()
    grad_normed = in_ring.end()
    token_grad = grid.hold(finish_grad(grid, tokens, cotangent, *grad_normed, gain_full))
    up_found = up_return.end()
    grad_w_up = grid.hold(lay_columns(grid, up_found, 1))
    sums.end()
    qkv_return.end_z()
    qkv_return.begin_y()
    output = grid.hold(finish_output(grid, grid.after(tokens), *projected, bias_out))
    qkv_found = qkv_return.end()
    out_moving = grid.wait(out_moving)
    sums = sums.result()
    grad_w_out = (out_kept.astype(WIDE) + out_moving.astype(WIDE))[0]

    grad_w_qkv = lay_columns(grid, qkv_found, 3)

    grad_gain, grad_shift = sums[: sizes[0]], sums[sizes[0] : 2 * sizes[0]]
    rest = sums[2 * sizes[0] :]
    grad_bias_qkv = rest[: sizes[2]]
    grad_bias_out = rest[sizes[2] : sizes[2] + sizes[3]]
    grad_bias_up = rest[sizes[2] + sizes[3] :]
    grad_w_dense = grad_w_out[: w_dense.shape[0]]
    grad_w_down = grad_w_out[w_dense.shape[0] :]
    return (
        output, token_grad, grad_gain, grad_shift, grad_w_qkv, grad_bias_qkv,
        grad_w_dense, grad_bias_out, grad_w_up, grad_bias_up, grad_w_down, grad_bias_out,
    )


def solution(mesh):
    rows = P(("dp", "ctx"), None)
    vector = P(("dp", "ctx"))
    spread = P("dp", "ctx", None)
    in_specs = (
        spread, P("dp", None), vector, vector, rows, vector, rows, vector, rows, vector, rows, vector, spread,
    )
    out_specs = (
        spread, spread, vector, vector, rows, vector, rows, vector, rows, vector, rows, vector,
    )
    return jax.shard_map(on_device, mesh=mesh, in_specs=in_specs, out_specs=out_specs, check_vma=False)
```

```python
from functools import partial

import jax
import jax.numpy as jnp
import numpy as np
from jax import lax
from jax.experimental import pallas as pl
from jax.experimental.pallas import tpu as pltpu
from jax.sharding import PartitionSpec as P

HEAD = 64
ROT = 32
ROPE_BASE = 10000
NORM_EPS = 1e-05
BOTH = ("dp", "ctx")
LOW = jnp.bfloat16
WIDE = jnp.float32
GELU_SCALE = 0.7978845608028654
GELU_CUBIC = 0.044715


COST_SCALE = 20_000_000


LIGHT = pl.CostEstimate(flops=1024, bytes_accessed=1024, transcendentals=1)


def cost(micros):
    return pl.CostEstimate(flops=int(micros * COST_SCALE), bytes_accessed=1024, transcendentals=1)
ROOM = pltpu.CompilerParams(vmem_limit_bytes=20 * 1024 * 1024)


def low_shape(*shape):
    return jax.ShapeDtypeStruct(shape, LOW)


def place(array, index):
    return lax.dynamic_index_in_dim(array, index, 0, keepdims=False)


def turn_page(token):
    def body(token_ref, copy_ref):
        copy_ref[...] = token_ref[...]

    return pl.pallas_call(
        body,
        out_shape=jax.ShapeDtypeStruct(token.shape, token.dtype),
        cost_estimate=pl.CostEstimate(flops=100_000_000_000, bytes_accessed=8192, transcendentals=0),
    )(token)


class Grid:
    def __init__(self):
        self.z_count = lax.axis_size("dp")
        self.ctx_count = lax.axis_size("ctx")
        self.y_count = self.ctx_count // 4
        ctx = lax.axis_index("ctx")
        self.z = lax.axis_index("dp")
        self.y = ctx // 4
        self.x = (ctx // 2) % 2
        self.c = ctx % 2
        self.where = jnp.stack([self.z, self.y, self.x, self.c]).astype(jnp.int32)
        self.rank = self.z * self.y_count + self.y
        self.rank_count = self.z_count * self.y_count
        self.parity = (self.z + self.x) % 2
        self.token = jnp.zeros((8, 128), WIDE)
        self.started, self.pages = False, True

    def steps(self):
        order = sorted(range(1, self.z_count), key=lambda k: (min(k, self.z_count - k), k))
        return order

    def after(self, value):
        self.page()
        return lax.optimization_barrier((value, self.token))[0]

    def hold(self, value):
        self.page()
        value, self.token = lax.optimization_barrier((value, self.token))
        return value

    wait = hold

    def page(self):
        if self.started and self.pages:
            self.token = turn_page(self.token)
        self.started = False

    def swap(self, value, bit):
        pairs = [(device, device ^ (1 << bit)) for device in range(self.rank_count * 4)]
        return self.send(value, pairs)

    def turn(self):
        self.token = turn_page(self.token)
        self.started = False

    def start(self, value, z=0, y=0, x=0, c=0):
        pairs = []
        for z_at in range(self.z_count):
            for y_at in range(self.y_count):
                for x_at in range(2):
                    for c_at in range(2):
                        z_to = (z_at + z) % self.z_count
                        y_to = (y_at + y) % self.y_count
                        source = ((z_at * self.y_count + y_at) * 2 + x_at) * 2 + c_at
                        target = ((z_to * self.y_count + y_to) * 2 + (x_at ^ x)) * 2 + (c_at ^ c)
                        pairs.append((source, target))
        return self.send(value, pairs)

    def send(self, value, pairs):
        value = lax.optimization_barrier((value, self.token))[0]
        self.started = True
        return lax.ppermute(value, BOTH, pairs)

    def local(self, body, inputs, outs):
        count = len(inputs)

        def whole_body(where_ref, *refs):
            body(*[where_ref[i] for i in range(4)], refs[:count], refs[count:])

        vmem = pl.BlockSpec(memory_space=pltpu.VMEM)
        return pl.pallas_call(
            whole_body,
            in_specs=[pl.BlockSpec(memory_space=pltpu.SMEM)] + [vmem] * count,
            out_specs=[vmem] * len(outs),
            out_shape=outs,
            compiler_params=ROOM,
            cost_estimate=cost(1.5),
        )(self.where, *inputs)

    def pile(self, *arrays):
        lengths = [item.shape[0] for item in arrays]
        starts = [sum(lengths[:i]) for i in range(len(lengths))]

        def body(z, y, x, c, ins, outs):
            for ref, start, length in zip(ins, starts, lengths):
                outs[0][start : start + length] = ref[...]

        shape = (sum(lengths), *arrays[0].shape[1:])
        return self.local(body, arrays, [jax.ShapeDtypeStruct(shape, arrays[0].dtype)])[0]


def mover(grid, plan, inputs, outs):
    count = len(inputs)

    def copies_of(where_ref, refs, sems):
        at = [where_ref[i] for i in range(4)]
        listed = plan(*at, refs[:count], refs[count:])
        return [pltpu.make_async_copy(source, target, sems.at[i]) for i, (source, target) in enumerate(listed)]

    def body(where_ref, *refs):
        copies = copies_of(where_ref, refs[:-1], refs[-1])
        for copy in copies:
            copy.start()
        for copy in copies:
            copy.wait()

    most = 4 * max(4, grid.rank_count)
    return pl.pallas_call(
        body,
        in_specs=[pl.BlockSpec(memory_space=pltpu.SMEM)] + [pl.BlockSpec(memory_space=pltpu.VMEM)] * count,
        out_specs=[pl.BlockSpec(memory_space=pltpu.HBM)] * len(outs),
        out_shape=outs,
        scratch_shapes=[pltpu.SemaphoreType.DMA((most,))],
        compiler_params=pltpu.CompilerParams(vmem_limit_bytes=24 * 1024 * 1024),
        cost_estimate=LIGHT,
    )(grid.where, *inputs)


def part_cores(grid, tokens, cotangent):
    span, width = tokens.shape[1:]

    def body(z, y, x, c, ins, outs):
        for at, ref in enumerate(ins):
            outs[0][at * span : (at + 1) * span] = ref[1 - c]
            outs[1 + at][...] = ref[c]

    shapes = [low_shape(2 * span, width), low_shape(span, width), low_shape(span, width)]
    return grid.local(body, [tokens, cotangent], shapes)


def pair_of(grid, even, odd):
    def body(z, y, x, c, ins, outs):
        swap = lax.rem(z + x, 2)
        for first in range(2):

            @pl.when(swap == first)
            def _(first=first):
                outs[0][...] = ins[first][...]
                outs[1][...] = ins[1 - first][...]

    return grid.local(body, [even, odd], [low_shape(*even.shape)] * 2)


class Ring:
    def __init__(self, grid, first):
        self.grid, self.pieces, self.moving = grid, {0: first}, {}

    def begin(self, r):
        zn = self.grid.z_count
        self.moving[r] = self.grid.start(self.pieces[r - 1], z=1)
        if zn - r > zn // 2:
            self.moving[zn - r] = self.grid.start(self.pieces[(zn - r + 1) % zn], z=-1)

    def end(self):
        self.pieces.update(self.grid.wait(self.moving))
        self.moving = {}

    def finish(self):
        for r in range(3, self.grid.z_count // 2 + 1):
            self.begin(r)
            self.end()

    def pair(self, i):
        return pair_of(self.grid, self.pieces[2 * i], self.pieces[2 * i + 1])


class Spread:
    def __init__(self, grid, pair):
        self.grid = grid
        self.keep, away = pair
        self.moving = grid.start(away, x=1)

    def end_x(self):
        self.parts = [self.grid.pile(self.keep, self.grid.wait(self.moving))]

    def begin_y(self):
        self.moving = self.grid.start(self.parts[-1], y=1)

    def end_y(self):
        self.parts.append(self.grid.wait(self.moving))
        for _ in range(2, self.grid.y_count):
            self.begin_y()
            self.parts.append(self.grid.wait(self.moving))


def sum_low(left, right):
    return (left.astype(WIDE) + right.astype(WIDE)).astype(LOW)


class TokenSum:
    def __init__(self, grid, part, dy):
        self.grid = grid
        self.moving = grid.start(part, y=-1)
        self.left = dy - 1

    def more(self, part):
        arrived = self.grid.wait(self.moving)
        if self.left:
            self.moving = self.grid.start(sum_low(part, arrived), y=-1)
            self.left -= 1
            return
        span = arrived.shape[0] // 2

        def body(z, y, x, c, ins, outs):
            for at in range(2):
                here = slice(at * span, (at + 1) * span)
                outs[at][...] = sum_low(ins[0][here], ins[1][here])

        self.kept, self.away = self.grid.local(body, [part, arrived], [low_shape(span, arrived.shape[1])] * 2)

    def begin_x(self):
        self.moving = self.grid.start(self.away, x=1)

    def end_x(self):
        return pair_of(self.grid, self.kept, self.grid.wait(self.moving))


class RingSum:
    def __init__(self, grid):
        self.grid, self.pieces = grid, {}

    def add(self, left, right):
        def body(z, y, x, c, ins, outs):
            outs[0][...] = sum_low(ins[0][...], ins[1][...])

        return self.grid.local(body, [left, right], [low_shape(*left.shape)])[0]

    def begin_far(self):
        grid, zn, pieces = self.grid, self.grid.z_count, self.pieces
        down, up = zn // 2, zn // 2 + 1
        while down > 2:
            arrived = grid.wait(grid.start(pieces[down], z=-1))
            down -= 1
            pieces[down] = self.add(pieces[down], arrived)
        while up < zn - 1:
            arrived = grid.wait(grid.start(pieces[up], z=1))
            up += 1
            pieces[up] = self.add(pieces[up], arrived)
        self.moving = grid.start(pieces[2], z=-1), grid.start(pieces[zn - 1], z=1)

    def end_far(self):
        self.down, self.up = self.grid.wait(self.moving)

    def begin_near(self):
        self.moving = self.grid.start(self.add(self.pieces[1], self.down), z=-1)

    def end_near(self):
        near = self.grid.wait(self.moving)
        span = near.shape[0] // 2

        def body(z, y, x, c, ins, outs):
            total = ins[0][...].astype(WIDE) + ins[1][...].astype(WIDE) + ins[2][...].astype(WIDE)
            outs[0][...] = total[:span]
            outs[1][...] = total[span:].astype(LOW)

        shapes = [jax.ShapeDtypeStruct((span, near.shape[1]), WIDE), low_shape(span, near.shape[1])]
        self.own, away = self.grid.local(body, [self.pieces[0], self.up, near], shapes)
        self.moving = self.grid.start(away, c=1)

    def end(self):
        return self.own, self.grid.wait(self.moving)


def finish_output(grid, tokens, own, other, bias_out):
    def body(z, y, x, c, ins, outs):
        for ref, at in ((ins[1], c), (ins[2], 1 - c)):
            outs[0][at] = (ins[0][at].astype(WIDE) + ref[...].astype(WIDE) + ins[3][...]).astype(LOW)

    return grid.local(body, [tokens, own, other, bias_out], [low_shape(*tokens.shape)])[0]


def finish_grad(grid, tokens, cotangent, own, other, gain_vec):
    def body(z, y, x, c, ins, outs):
        for ref, at in ((ins[2], c), (ins[3], 1 - c)):
            inputs = ins[0][at].astype(WIDE)
            centre = inputs - jnp.mean(inputs, -1, keepdims=True)
            turn = lax.rsqrt(jnp.mean(centre * centre, -1, keepdims=True) + NORM_EPS)
            unit = centre * turn
            scaled = ref[...].astype(WIDE) * ins[4][...]
            along = jnp.mean(scaled * unit, -1, keepdims=True)
            change = turn * (scaled - jnp.mean(scaled, -1, keepdims=True) - unit * along)
            outs[0][at] = (ins[1][at].astype(WIDE) + change).astype(LOW)

    return grid.local(body, [tokens, cotangent, own, other, gain_vec], [low_shape(*tokens.shape)])[0]


def cut_columns(grid, w_qkv, w_up):
    zn, yn, ranks = grid.z_count, grid.y_count, grid.rank_count
    rows, third, wide = w_qkv.shape[0], w_qkv.shape[1] // 3, w_up.shape[1]
    head, hidden = third // ranks, wide // ranks
    width = 3 * head + hidden
    outs = [low_shape(rows, width)] * zn + [low_shape(zn, rows, width)] * (yn - 1)

    def plan(z, y, x, c, ins, refs):
        copies = []
        for dy in range(yn):
            for k in range(zn):
                rank = lax.rem(z + k, zn) * yn + lax.rem(y + dy, yn)
                target = refs[k] if dy == 0 else refs[zn + dy - 1].at[k]
                for part in range(3):
                    start = pl.multiple_of(part * third + rank * head, 128)
                    copies.append((ins[0].at[:, pl.ds(start, head)], target.at[:, pl.ds(part * head, head)]))
                start = pl.multiple_of(rank * hidden, 128)
                copies.append((ins[1].at[:, pl.ds(start, hidden)], target.at[:, pl.ds(3 * head, hidden)]))
        return copies

    if head % 128 == 0:
        made = mover(grid, plan, [w_qkv, w_up], outs)
    else:
        heads = w_qkv.reshape(rows, 3, ranks, head)
        hiddens = w_up.reshape(rows, ranks, hidden)

        def block(k, dy):
            rank = (grid.z + k) % zn * yn + (grid.y + dy) % yn
            mine = lax.dynamic_index_in_dim(heads, rank, 2, keepdims=False).reshape(rows, 3 * head)
            return jnp.concatenate([mine, lax.dynamic_index_in_dim(hiddens, rank, 1, keepdims=False)], 1)

        made = [block(k, 0) for k in range(zn)] + [
            jnp.stack([block(k, dy) for k in range(zn)]) for dy in range(1, yn)
        ]
    return made[:zn], made[zn:]


def join_columns(grid, groups):
    zn, yn = grid.z_count, grid.y_count
    rows, width = groups[0][1].shape[-2:]
    flat = [item for group in groups for item in group[1:]]

    def body(where_ref, *refs):
        z, y, x, c = [where_ref[i] for i in range(4)]
        for at_group, group in enumerate(groups):
            for way in range(4):
                column, core = lax.rem(x + way % 2, 2), lax.rem(c + way // 2, 2)
                for at, k in enumerate(group[0]):
                    for dy in range(yn):
                        rank = lax.rem(z - k + zn, zn) * yn + lax.rem(y - dy + yn, yn)
                        start = pl.multiple_of(((rank * 2 + column) * 2 + core) * rows, rows)
                        refs[-1][pl.ds(start, rows)] = refs[2 * at_group + way // 2][way % 2, at, dy]

    vmem = pl.BlockSpec(memory_space=pltpu.VMEM)
    return pl.pallas_call(
        body,
        in_specs=[pl.BlockSpec(memory_space=pltpu.SMEM)] + [vmem] * len(flat),
        out_specs=vmem,
        out_shape=low_shape(zn * yn * 4 * rows, width),
        compiler_params=ROOM,
        cost_estimate=LIGHT,
    )(grid.where, *flat)


def join_out(grid, here, there, dense_rows):
    down_rows = here.shape[1] - dense_rows

    def plan(z, y, x, c, ins, outs):
        copies = []
        for way in range(4):
            source = ins[way // 2].at[way % 2]
            at = lax.rem(x + way % 2, 2) * 2 + lax.rem(c + way // 2, 2)
            first = pl.multiple_of(at * dense_rows, dense_rows)
            second = pl.multiple_of(4 * dense_rows + at * down_rows, dense_rows)
            copies.append((source.at[pl.ds(0, dense_rows)], outs[0].at[pl.ds(first, dense_rows)]))
            copies.append((source.at[pl.ds(dense_rows, down_rows)], outs[0].at[pl.ds(second, down_rows)]))
        return copies

    return mover(grid, plan, [here, there], [low_shape(4 * here.shape[1], here.shape[2])])[0]


def halves_in(grid, left, rights):
    tokens, ranks = left.shape[0], grid.rank_count
    widths = [item.shape[1] for item in rights]
    width = sum(widths)
    quad = left.shape[1] // ranks
    rows = quad // 4
    sums = [jax.ShapeDtypeStruct((1, size), WIDE) for size in widths]
    if quad % 128:
        made = contract_first(left, jnp.concatenate(rights, 1)).astype(LOW).reshape(ranks, 2, 2, rows, width)
        pick = lambda index: lax.dynamic_index_in_dim(made, index, 2, keepdims=False)
        return pick(grid.c), pick(1 - grid.c), [jnp.sum(item.astype(WIDE), 0, keepdims=True) for item in rights]
    starts = [sum(widths[:i]) for i in range(len(widths))]

    def body(where_ref, left_ref, *refs):
        core = where_ref[3]
        ins, (kept_ref, away_ref, *sum_refs), made_ref = refs[: len(rights)], refs[len(rights) : -1], refs[-1]
        for ref, start, size in zip(ins, starts, widths):
            made_ref[:, start : start + size] = contract_first(left_ref[...], ref[...]).astype(LOW)
        for column in range(2):
            for out_ref, at in ((kept_ref, core), (away_ref, 1 - core)):
                start = pl.multiple_of((2 * column + at) * rows, rows)
                out_ref[column] = made_ref[pl.ds(start, rows)]

        @pl.when(pl.program_id(0) == 0)
        def _():
            for ref, sum_ref in zip(ins, sum_refs):
                sum_ref[...] = jnp.sum(ref[...].astype(WIDE), 0, keepdims=True)

    half = pl.BlockSpec((None, 2, rows, width), lambda t: (t, 0, 0, 0))
    made = pl.pallas_call(
        body,
        grid=(ranks,),
        in_specs=[pl.BlockSpec(memory_space=pltpu.SMEM), pl.BlockSpec((tokens, quad), lambda t: (0, t))]
        + [whole(item) for item in rights],
        out_specs=[half, half] + [whole(item) for item in sums],
        out_shape=[low_shape(ranks, 2, rows, width)] * 2 + sums,
        scratch_shapes=[pltpu.VMEM((quad, width), LOW)],
        compiler_params=ROOM,
        cost_estimate=cost(8.0),
    )(grid.where, left, *rights)
    return made[0], made[1], made[2:]


def halves_out(grid, attention_low, hidden_low, grad_out):
    tokens, width = grad_out.shape
    dense, down = attention_low.shape[1], hidden_low.shape[1]
    rows = (dense // 4, down // 4)
    shape = low_shape(1, 2, sum(rows), width)
    if dense % 128 or down % 512:
        made = [
            contract_first(item, grad_out).astype(LOW).reshape(2, 2, -1, width) for item in (attention_low, hidden_low)
        ]
        pick = lambda index: jnp.concatenate(
            [lax.dynamic_index_in_dim(item, index, 1, keepdims=False) for item in made], 1
        )[None]
        return pick(grid.c), pick(1 - grid.c)

    def body(where_ref, dense_ref, down_ref, grad_ref, kept_ref, away_ref, made_ref):
        core, step = where_ref[3], pl.program_id(0)

        @pl.when(step == 0)
        def _():
            made_ref[...] = contract_first(dense_ref[...], grad_ref[...]).astype(LOW)
            for column in range(2):
                for out_ref, at in ((kept_ref, core), (away_ref, 1 - core)):
                    start = pl.multiple_of((2 * column + at) * rows[0], rows[0])
                    out_ref[0, column, : rows[0]] = made_ref[pl.ds(start, rows[0])]

        for quarter in range(4):
            for out_ref, at in ((kept_ref, core), (away_ref, 1 - core)):

                @pl.when((step == quarter + 1) & (at == quarter % 2))
                def _(out_ref=out_ref, quarter=quarter):
                    made = contract_first(down_ref[...], grad_ref[...]).astype(LOW)
                    out_ref[0, quarter // 2, rows[0] :] = made

    return pl.pallas_call(
        body,
        grid=(5,),
        in_specs=[
            pl.BlockSpec(memory_space=pltpu.SMEM),
            whole(attention_low),
            pl.BlockSpec((tokens, rows[1]), lambda t: (0, jnp.maximum(t - 1, 0))),
            whole(grad_out),
        ],
        out_specs=[whole(shape)] * 2,
        out_shape=[shape] * 2,
        scratch_shapes=[pltpu.VMEM((dense, width), LOW)],
        compiler_params=ROOM,
        cost_estimate=cost(11.0),
    )(grid.where, attention_low, hidden_low, grad_out)


def halve_columns(grid, kept, arrived):
    count, _, rows, width = kept.shape

    def body(where_ref, kept_ref, arrived_ref, here_ref, there_ref):
        column = where_ref[2]
        for ref, at in ((here_ref, column), (there_ref, 1 - column)):
            ref[...] = sum_low(kept_ref[at], arrived_ref[at])

    both = pl.BlockSpec((None, 2, rows, width), lambda t: (t, 0, 0, 0))
    one = pl.BlockSpec((None, rows, width), lambda t: (t, 0, 0))
    return pl.pallas_call(
        body,
        grid=(count,),
        in_specs=[pl.BlockSpec(memory_space=pltpu.SMEM), both, both],
        out_specs=[one, one],
        out_shape=[low_shape(count, rows, width)] * 2,
        compiler_params=ROOM,
        cost_estimate=cost(4.5),
    )(grid.where, kept, arrived)


class ColumnReturn:
    def __init__(self, grid, kept, arrived):
        zn, yn = grid.z_count, grid.y_count
        self.grid, self.shape = grid, kept.shape[1:]

        def body(z, y, x, c, ins, outs):
            for k in range(zn):
                for at in range(yn):
                    rank = lax.rem(z + k, zn) * yn + at
                    outs[k][at] = sum_low(ins[0][rank], ins[1][rank])

        self.cut = grid.local(body, [kept, arrived], [low_shape(yn, *self.shape)] * zn)

    def begin_z(self):
        self.by_z = {0: self.cut[0]}
        self.moving = {k: self.grid.start(self.cut[k], z=k) for k in self.grid.steps()}

    def end_z(self):
        grid, zn, yn = self.grid, self.grid.z_count, self.grid.y_count
        self.by_z.update(grid.wait(self.moving))

        def body(z, y, x, c, ins, outs):
            for dy in range(yn):
                for k in range(zn):
                    outs[dy][k] = ins[k][lax.rem(y + dy, yn)]

        self.cut = grid.local(body, [self.by_z[k] for k in range(zn)], [low_shape(zn, *self.shape)] * yn)

    def begin_y(self):
        self.moving = [self.grid.start(self.cut[dy], y=dy) for dy in range(1, self.grid.y_count)]

    def end(self):
        return [self.cut[0], *self.grid.wait(self.moving)]


def lay_columns(grid, found, parts):
    zn, yn, ranks = grid.z_count, grid.y_count, grid.rank_count
    rows, width = found[0].shape[1:]
    width = width // parts

    if width % 128 == 0:

        def body(z, y, x, c, ins, outs):
            for dy, ref in enumerate(ins):
                for k in range(zn):
                    rank = lax.rem(z - k + zn, zn) * yn + lax.rem(y - dy + yn, yn)
                    for part in range(parts):
                        start = pl.multiple_of((part * ranks + rank) * width, 128)
                        item = ref[k, :, part * width : (part + 1) * width]
                        outs[0][:, pl.ds(start, width)] = item.astype(WIDE)

        return grid.local(body, found, [jax.ShapeDtypeStruct((rows, parts * ranks * width), WIDE)])[0]
    laid = jnp.zeros((rows, parts, ranks, width), LOW)
    for dy, item in enumerate(found):
        for k in range(zn):
            rank = (grid.z - k) % zn * yn + (grid.y - dy) % yn
            laid = lax.dynamic_update_index_in_dim(laid, item[k].reshape(rows, parts, width), rank, 2)
    return laid.reshape(rows, -1).astype(WIDE)


class VectorGather:
    def __init__(self, grid, row):
        self.grid, self.block = grid, row[None]
        bits = (grid.rank_count * 4).bit_length() - 1
        self.bits = [0, *range(bits - (grid.z_count - 1).bit_length(), bits)]
        self.bits += [bit for bit in range(bits - 1, 0, -1) if bit not in self.bits]
        self.ways = list(self.bits)

    def begin(self):
        self.moving = self.grid.swap(self.block, self.ways.pop(0))

    def end(self):
        self.block = self.grid.pile(self.block, self.grid.wait(self.moving))

    def step(self):
        self.begin()
        self.end()

    def row_of(self, here, device):
        return sum(
            lax.rem(lax.rem(here // (1 << bit), 2) + (device >> bit) % 2, 2) * (1 << at)
            for at, bit in enumerate(self.bits)
        )

    def result(self):
        grid = self.grid
        here = (grid.rank * 2 + grid.x) * 2 + grid.c
        return self.block[jnp.stack([self.row_of(here, device) for device in range(grid.rank_count * 4)])]


def unfold_vectors(grid, gather, sizes, block_len, seqs):
    zn, yn, block = grid.z_count, grid.y_count, gather.block
    ranks, devices = grid.rank_count, grid.rank_count * 4
    cuts = [sum(sizes[:i]) for i in range(len(sizes) + 1)]
    slots = sizes[6] // 2
    head, hidden = sizes[2] * devices // (3 * ranks), sizes[4] * devices // ranks
    third = sizes[2] * devices // 3
    rows = 8 * block_len
    length = yn * rows
    half = ROT // 2
    lane = np.arange(128) % HEAD
    freqs = np.float32(ROPE_BASE) ** (-((lane % half).astype(np.float32) * np.float32(2.0 / ROT)))
    turned = (lane < ROT).astype(np.float32)
    sign = np.where(lane < half, -1.0, 1.0).astype(np.float32) * turned
    marks = jnp.asarray(np.stack([freqs.astype(np.float32), turned, sign]))

    def body(where_ref, block_ref, mark_ref, *refs):
        z, y, x, c = [where_ref[i] for i in range(4)]
        gain_ref, shift_ref, in_ref, out_ref, cos_ref, sin_ref, column_ref, row_ref = refs[:8]
        qkv_ref, up_ref = refs[8:]
        here_at = ((z * yn + y) * 2 + x) * 2 + c
        for device in range(devices):
            row = block_ref[pl.ds(gather.row_of(here_at, device), 1), :]
            item = [row[:, cuts[i] : cuts[i + 1]] for i in range(6)]
            here = [pl.ds(device * sizes[i], sizes[i]) for i in range(6)]
            gain_ref[:, here[0]] = item[0]
            shift_ref[:, here[1]] = item[1]
            qkv_ref[:, here[2]] = item[2]
            out_ref[:, here[3]] = item[3] + item[5]
            up_ref[:, here[4]] = item[4]
        rank = z * yn + y
        for part in range(3):
            start = pl.multiple_of(part * third + rank * head, 128)
            in_ref[:, part * head : (part + 1) * head] = qkv_ref[:, pl.ds(start, head)]
        in_ref[:, 3 * head :] = up_ref[:, pl.ds(pl.multiple_of(rank * hidden, 128), hidden)]

        def order_row(source):
            parts = [
                jnp.where(source == at, block_ref[pl.ds(gather.row_of(here_at, at * 4 * yn), 1), :], 0.0)
                for at in range(zn)
            ]
            return sum(parts)

        parity = lax.rem(z + x, 2)
        slot_at = lax.broadcasted_iota(jnp.int32, (1, slots), 1)
        tall = lax.broadcasted_iota(jnp.int32, (block_len, 128), 0).astype(WIDE)
        flat = lax.broadcasted_iota(jnp.int32, (1, block_len), 1).astype(WIDE)
        for i in range(seqs):
            row = order_row(lax.rem(z - 2 * i - parity + 2 * zn, zn))
            order = jnp.where(c == 0, row[:, cuts[6] : cuts[6] + slots], row[:, cuts[6] + slots : cuts[7]])
            for dy in range(yn):
                for near in range(4):
                    ctx = (lax.rem(y - dy + yn, yn) * 2 + lax.rem(x + near // 2, 2)) * 2 + lax.rem(c + near, 2)
                    for at in range(2):
                        value = jnp.sum(jnp.where(slot_at == 2 * ctx + at, order, 0.0), 1, keepdims=True) * block_len
                        place = value + tall
                        angle = place * mark_ref[0:1, :]
                        inside = (near * 2 + at) * block_len
                        here = pl.ds((dy * seqs + i) * rows + inside, block_len)
                        cos_ref[here, :] = jnp.where(mark_ref[1:2, :] > 0.0, jnp.cos(angle), 1.0)
                        sin_ref[here, :] = jnp.sin(angle) * mark_ref[2:3, :]
                        there = dy * rows + inside
                        column_ref[pl.ds(i * length + there, block_len), :] = place[:, :1]
                        row_ref[i, :, there : there + block_len] = value + flat

    wide = lambda *shape: jax.ShapeDtypeStruct(shape, WIDE)
    tokens = seqs * length
    vmem = pl.BlockSpec(memory_space=pltpu.VMEM)
    return pl.pallas_call(
        body,
        in_specs=[pl.BlockSpec(memory_space=pltpu.SMEM), vmem, vmem],
        out_specs=[vmem] * 8,
        out_shape=[
            wide(1, sizes[0] * devices), wide(1, sizes[1] * devices), wide(1, 3 * head + hidden),
            wide(1, sizes[3] * devices), wide(tokens, 128), wide(tokens, 128), wide(tokens, 1), wide(seqs, 1, length),
        ],
        scratch_shapes=[
            pltpu.VMEM((1, 3 * third), WIDE), pltpu.VMEM((1, hidden * ranks), WIDE),
        ],
        compiler_params=ROOM,
        cost_estimate=LIGHT,
    )(grid.where, block, marks)


class VectorSum:
    def __init__(self, grid, rows):
        self.grid, self.terms, self.bit = grid, [rows], 0

    def begin(self):
        grid, bit, yn = self.grid, self.bit, self.grid.y_count
        count, width = self.terms[0].shape

        def body(z, y, x, c, ins, outs):
            own = lax.rem((((z * yn + y) * 2 + x) * 2 + c) // (1 << bit), 2)
            for at in range(count // 2):
                for out, pick in zip(outs, (own, 1 - own)):
                    row = pl.ds(2 * at + pick, 1)
                    out[at : at + 1, :] = sum(ref[row, :] for ref in ins)

        kept, away = grid.local(body, self.terms, [jax.ShapeDtypeStruct((count // 2, width), WIDE)] * 2)
        self.kept, self.moving = kept, grid.swap(away, bit)
        self.bit += 1

    def end(self):
        self.terms = [self.kept, self.grid.wait(self.moving)]

    def result(self):
        while self.terms[0].shape[0] > 1:
            self.begin()
            self.end()
        return sum(self.terms)[0]


def fold_vectors(grid, gains, shifts, sums_qkv, sum_up, cotangent, sizes):
    devices, ranks, yn = grid.rank_count * 4, grid.rank_count, grid.y_count
    head, hidden = sums_qkv[0].shape[1], sum_up.shape[1]
    third = head * ranks
    chunks = (sizes[0], sizes[1], sizes[2], sizes[3], sizes[4])
    starts = [sum(chunks[:i]) for i in range(len(chunks))]
    count = len(gains)

    def body(where_ref, *refs):
        ins, out_ref, qkv_ref, up_ref = refs[:-3], refs[-3], refs[-2], refs[-1]
        rank = where_ref[0] * yn + where_ref[1]
        gain = sum(ref[...] for ref in ins[:count])
        shift = sum(ref[...] for ref in ins[count : 2 * count])
        grad = jnp.sum(ins[2 * count + 4][...].astype(WIDE), (0, 1))[None]
        qkv_ref[...] = jnp.zeros_like(qkv_ref)
        up_ref[...] = jnp.zeros_like(up_ref)
        for part in range(3):
            qkv_ref[:, pl.ds(pl.multiple_of(part * third + rank * head, 128), head)] = ins[2 * count + part][...]
        up_ref[:, pl.ds(pl.multiple_of(rank * hidden, 128), hidden)] = ins[2 * count + 3][...]
        for device in range(devices):
            for start, size, whole_row in zip(starts, chunks, (gain, shift, qkv_ref, grad, up_ref)):
                item = whole_row[:, device * size : (device + 1) * size]
                out_ref[device : device + 1, start : start + size] = item

    vmem = pl.BlockSpec(memory_space=pltpu.VMEM)
    inputs = [*gains, *shifts, *sums_qkv, sum_up, cotangent]
    return pl.pallas_call(
        body,
        in_specs=[pl.BlockSpec(memory_space=pltpu.SMEM)] + [vmem] * len(inputs),
        out_specs=vmem,
        out_shape=jax.ShapeDtypeStruct((devices, sum(chunks)), WIDE),
        scratch_shapes=[pltpu.VMEM((1, 3 * third), WIDE), pltpu.VMEM((1, hidden * ranks), WIDE)],
        compiler_params=ROOM,
        cost_estimate=cost(3.0),
    )(grid.where, *inputs)


def contract_last(left, right):
    return lax.dot_general(
        left, right, (((1,), (1,)), ((), ())), preferred_element_type=WIDE
    )


def contract_first(left, right):
    return lax.dot_general(
        left, right, (((0,), (0,)), ((), ())), preferred_element_type=WIDE
    )


def whole(array):
    return pl.BlockSpec(array.shape, lambda *at: (0,) * array.ndim)


def swap_halves(field):
    width = field.shape[-1]
    half = ROT // 2
    if width % 128 == 0:
        after = pltpu.roll(field, width - half, 1)
        before = pltpu.roll(field, half, 1)
    else:
        after = jnp.concatenate([field[:, half:], field[:, :half]], 1)
        before = jnp.concatenate([field[:, width - half :], field[:, : width - half]], 1)
    lane = lax.broadcasted_iota(jnp.int32, field.shape, 1) % HEAD
    return jnp.where(lane < half, after, before)


def turned_heads(query_ref, key_ref, value_ref, cos_ref, sin_ref):
    rows = (-1, cos_ref.shape[-1])
    cosine, sine = cos_ref[...].reshape(rows), sin_ref[...].reshape(rows)
    query = query_ref[...].reshape(rows)
    query_all = (query * cosine + swap_halves(query) * sine).astype(LOW)
    key = key_ref[...].reshape(rows)
    key_all = (key * cosine + swap_halves(key) * sine).astype(LOW)
    value_all = value_ref[...].reshape(rows).astype(LOW)
    return cosine, sine, query_all, key_all, value_all


def probability_of(query_low, key_low, allowed):
    scores = jnp.where(allowed, contract_last(query_low, key_low) * HEAD**-0.5, -1e30)
    weights = jnp.exp(scores - jnp.max(scores, -1, keepdims=True))
    return weights * (1.0 / jnp.sum(weights, -1, keepdims=True))


def forward_body(
    query_ref, key_ref, value_ref, cos_ref, sin_ref, column_ref, row_ref, mixed_ref, kept_ref
):
    _, _, query_all, key_all, value_all = turned_heads(query_ref, key_ref, value_ref, cos_ref, sin_ref)
    allowed = row_ref[...] <= column_ref[...]
    outs = []
    for at in range(query_all.shape[1] // HEAD):
        part = slice(at * HEAD, (at + 1) * HEAD)
        probability_low = probability_of(query_all[:, part], key_all[:, part], allowed).astype(LOW)
        kept_ref[at] = probability_low
        outs.append(jnp.dot(probability_low, value_all[:, part], preferred_element_type=WIDE))
    mixed_ref[...] = jnp.concatenate(outs, 1).astype(LOW).reshape(mixed_ref.shape)


def backward_body(
    query_ref, key_ref, value_ref, cos_ref, sin_ref, grad_ref, kept_ref, grad_query_ref, grad_key_ref, grad_value_ref
):
    cosine, sine, query_all, key_all, value_all = turned_heads(query_ref, key_ref, value_ref, cos_ref, sin_ref)
    grad_all = grad_ref[...].reshape(value_all.shape)
    scale = HEAD**-0.5
    outs = []
    for at in range(query_all.shape[1] // HEAD):
        part = slice(at * HEAD, (at + 1) * HEAD)
        query_low, key_low = query_all[:, part], key_all[:, part]
        value_low, grad_low = value_all[:, part], grad_all[:, part]
        probability_low = kept_ref[at]
        mixed = jnp.dot(probability_low, value_low, preferred_element_type=WIDE)
        delta = jnp.sum(grad_low.astype(WIDE) * mixed, -1, keepdims=True)
        grad_probability = contract_last(grad_low, value_low)
        grad_scores = (probability_low.astype(WIDE) * (grad_probability - delta)).astype(LOW)
        grad_value = contract_first(probability_low, grad_low)
        grad_query = jnp.dot(grad_scores, key_low, preferred_element_type=WIDE) * scale
        grad_key = contract_first(grad_scores, query_low) * scale
        outs.append((grad_query, grad_key, grad_value))
    grad_query, grad_key, grad_value = [jnp.concatenate(item, 1) for item in zip(*outs)]
    block = grad_query_ref.shape
    grad_query = grad_query * cosine - swap_halves(grad_query) * sine
    grad_key = grad_key * cosine - swap_halves(grad_key) * sine
    grad_query_ref[...] = grad_query.astype(LOW).reshape(block)
    grad_key_ref[...] = grad_key.astype(LOW).reshape(block)
    grad_value_ref[...] = grad_value.astype(LOW).reshape(block)


def attend(qkv, cosine, sine, yn, seqs, column=None, row=None, grad_attention=None, kept=None):
    backward = grad_attention is not None
    tokens, width = qkv.shape[0], qkv.shape[1] // 3
    lanes = min(128, width)
    length = tokens // seqs
    rows = length // yn
    block = (yn, None, rows, lanes)
    cut = lambda array: array.reshape(yn, seqs, rows, array.shape[-1])
    field = pl.BlockSpec(block, lambda s, h: (0, s, 0, h))
    table = pl.BlockSpec(block, lambda s, h: (0, s, 0, 0))
    square = pl.BlockSpec((None, lanes // HEAD, length, length), lambda s, h: (s, h, 0, 0))
    low = low_shape(yn, seqs, rows, width)
    if width % 128 == 0:
        thirds = [cut(qkv)] * 3
        blocks = [
            pl.BlockSpec(block, lambda s, h, part=part: (0, s, 0, part * (width // lanes) + h)) for part in range(3)
        ]
    else:
        thirds = [cut(qkv[:, part * width : (part + 1) * width]) for part in range(3)]
        blocks = [field] * 3
    inputs = [*thirds, cut(cosine[:, :lanes]), cut(sine[:, :lanes])]
    blocks = blocks + [table, table]
    if backward:
        body, inputs, blocks = backward_body, inputs + [cut(grad_attention), kept], blocks + [field, square]
        outs, out_blocks = [low] * 3, [field] * 3
    else:
        body, inputs = forward_body, inputs + [column, row]
        blocks = blocks + [
            pl.BlockSpec((length, 1), lambda s, h: (s, 0)),
            pl.BlockSpec((None, 1, length), lambda s, h: (s, 0, 0)),
        ]
        outs, out_blocks = [low, low_shape(seqs, width // HEAD, length, length)], [field, square]
    made = pl.pallas_call(
        body,
        grid=(seqs, width // lanes),
        in_specs=blocks,
        out_specs=out_blocks,
        out_shape=outs,
        compiler_params=pltpu.CompilerParams(vmem_limit_bytes=20 * 1024 * 1024),
        cost_estimate=cost(13.0),
    )(*inputs)
    return [item.reshape(tokens, width) if item.shape == low.shape else item for item in made]


def normalize(parts, gain_vec, shift_vec):
    span, width = parts[0].shape
    tile = min(span, 128)
    each = span // tile

    def body(*refs):
        step = pl.program_id(0)
        gain_ref, shift_ref, normed_ref, unit_ref = refs[len(parts) :]
        for at, ref in enumerate(refs[: len(parts)]):

            @pl.when(step // each == at)
            def _(ref=ref):
                inputs = ref[...].astype(WIDE)
                centre = inputs - jnp.mean(inputs, -1, keepdims=True)
                spread = jnp.mean(centre * centre, -1, keepdims=True)
                unit = centre * lax.rsqrt(spread + NORM_EPS)
                normed_ref[...] = (unit * gain_ref[...] + shift_ref[...]).astype(LOW)
                unit_ref[...] = unit.astype(LOW)

    block = (tile, width)
    clamp = lambda at: pl.BlockSpec(block, lambda t: (jnp.clip(t - at * each, 0, each - 1), 0))
    vector = pl.BlockSpec((1, width), lambda t: (0, 0))
    return pl.pallas_call(
        body,
        grid=(len(parts) * each,),
        in_specs=[clamp(at) for at in range(len(parts))] + [vector, vector],
        out_specs=[pl.BlockSpec(block, lambda t: (t, 0))] * 2,
        out_shape=[low_shape(len(parts) * span, width)] * 2,
        compiler_params=ROOM,
        cost_estimate=cost(8.0),
    )(*parts, gain_vec, shift_vec)


def bend(up):
    bent = jnp.tanh(GELU_SCALE * (up + GELU_CUBIC * up * up * up))
    slope = 0.5 * (1.0 + bent) + 0.5 * up * (1.0 - bent * bent) * GELU_SCALE * (1.0 + 3.0 * GELU_CUBIC * up * up)
    return (0.5 * up * (1.0 + bent)).astype(LOW), slope.astype(LOW)


def project(normed_low, w_in, bias, split):
    tokens, total = normed_low.shape[0], w_in.shape[1]
    if split % 256 or total % 256:
        made = jnp.dot(normed_low, w_in, preferred_element_type=WIDE) + bias
        return made[:, :split], *bend(made[:, split:])
    heads = split // 256

    def body(normed_ref, w_ref, bias_ref, qkv_ref, hidden_ref, slope_ref):
        step = pl.program_id(0)
        made = jnp.dot(normed_ref[...], w_ref[...], preferred_element_type=WIDE) + bias_ref[...]

        @pl.when(step < heads)
        def _():
            qkv_ref[...] = made

        @pl.when(step >= heads)
        def _():
            hidden_ref[...], slope_ref[...] = bend(made)

    late = pl.BlockSpec((tokens, 256), lambda t: (0, jnp.maximum(t - heads, 0)))
    return pl.pallas_call(
        body,
        grid=(total // 256,),
        in_specs=[
            whole(normed_low),
            pl.BlockSpec((w_in.shape[0], 256), lambda t: (0, t)),
            pl.BlockSpec((1, 256), lambda t: (0, t)),
        ],
        out_specs=[pl.BlockSpec((tokens, 256), lambda t: (0, jnp.minimum(t, heads - 1))), late, late],
        out_shape=[jax.ShapeDtypeStruct((tokens, split), WIDE)] + [low_shape(tokens, total - split)] * 2,
        compiler_params=ROOM,
        cost_estimate=cost(16.0),
    )(normed_low, w_in, bias)


def project_back(grad_out, w_out, slope, dense_rows):
    tokens, width = grad_out.shape
    if dense_rows % 256 or w_out.shape[0] % 256:
        return (
            contract_last(grad_out, w_out[:dense_rows]).astype(LOW),
            (contract_last(grad_out, w_out[dense_rows:]) * slope.astype(WIDE)).astype(LOW),
        )
    first = dense_rows // 256

    def body(grad_ref, w_ref, slope_ref, attention_ref, up_ref):
        step = pl.program_id(0)
        made = contract_last(grad_ref[...], w_ref[...])

        @pl.when(step < first)
        def _():
            attention_ref[...] = made.astype(LOW)

        @pl.when(step >= first)
        def _():
            up_ref[...] = (made * slope_ref[...].astype(WIDE)).astype(LOW)

    late = pl.BlockSpec((tokens, 256), lambda t: (0, jnp.maximum(t - first, 0)))
    return pl.pallas_call(
        body,
        grid=(w_out.shape[0] // 256,),
        in_specs=[whole(grad_out), pl.BlockSpec((256, width), lambda t: (t, 0)), late],
        out_specs=[pl.BlockSpec((tokens, 256), lambda t: (0, jnp.minimum(t, first - 1))), late],
        out_shape=[low_shape(tokens, dense_rows), low_shape(*slope.shape)],
        compiler_params=ROOM,
        cost_estimate=cost(10.0),
    )(grad_out, w_out, slope)


def out_part(attention_low, hidden_low, w_out, dy, rows, seqs):
    head, hidden, width = attention_low.shape[1], hidden_low.shape[1], w_out.shape[1]
    each = rows // seqs
    if head % 128:
        here = slice(dy * rows, (dy + 1) * rows)
        joined = jnp.concatenate([attention_low[here], hidden_low[here]], 1)
        made = jnp.dot(joined, w_out, preferred_element_type=WIDE).astype(LOW)
        return [made[i * each : (i + 1) * each] for i in range(seqs)]

    def body(attention_ref, hidden_ref, w_ref, *out_refs):
        made = jnp.dot(attention_ref[...], w_ref[:head], preferred_element_type=WIDE)
        made += jnp.dot(hidden_ref[...], w_ref[head:], preferred_element_type=WIDE)
        for i, out_ref in enumerate(out_refs):
            out_ref[...] = made[i * each : (i + 1) * each].astype(LOW)

    tile = min(width, 512)
    return pl.pallas_call(
        body,
        grid=(width // tile,),
        in_specs=[
            pl.BlockSpec((rows, head), lambda t: (dy, 0)),
            pl.BlockSpec((rows, hidden), lambda t: (dy, 0)),
            pl.BlockSpec((w_out.shape[0], tile), lambda t: (0, t)),
        ],
        out_specs=[pl.BlockSpec((each, tile), lambda t: (0, t))] * seqs,
        out_shape=[low_shape(each, width)] * seqs,
        compiler_params=ROOM,
        cost_estimate=cost(150.0),
    )(attention_low, hidden_low, w_out)


def in_part(grads, w_in, unit_low, dy, rows, seqs):
    widths = [item.shape[1] for item in grads]
    starts = [sum(widths[:i]) for i in range(len(widths))]
    width = w_in.shape[0]
    each = rows // seqs
    if widths[0] % 128:
        here = slice(dy * rows, (dy + 1) * rows)
        made = contract_last(jnp.concatenate([item[here] for item in grads], 1), w_in)
        sums = [jnp.sum(item, 0, keepdims=True) for item in (made * unit_low[here].astype(WIDE), made)]
        return [made[i * each : (i + 1) * each].astype(LOW) for i in range(seqs)], *sums

    def body(*refs):
        w_ref, unit_ref, *out_refs, gain_ref, shift_ref = refs[len(grads) :]
        made = None
        for ref, start, size in zip(refs, starts, widths):
            term = contract_last(ref[...], w_ref[:, start : start + size])
            made = term if made is None else made + term
        for i, out_ref in enumerate(out_refs):
            out_ref[...] = made[i * each : (i + 1) * each].astype(LOW)
        gain_ref[...] = jnp.sum(made * unit_ref[...].astype(WIDE), 0, keepdims=True)
        shift_ref[...] = jnp.sum(made, 0, keepdims=True)

    tile = min(width, 512)
    vector = pl.BlockSpec((1, tile), lambda t: (0, t))
    *made, gain, shift = pl.pallas_call(
        body,
        grid=(width // tile,),
        in_specs=[pl.BlockSpec((rows, size), lambda t: (dy, 0)) for size in widths]
        + [
            pl.BlockSpec((tile, w_in.shape[1]), lambda t: (t, 0)),
            pl.BlockSpec((rows, tile), lambda t: (dy, t)),
        ],
        out_specs=[pl.BlockSpec((each, tile), lambda t: (0, t))] * seqs + [vector, vector],
        out_shape=[low_shape(each, width)] * seqs + [jax.ShapeDtypeStruct((1, width), WIDE)] * 2,
        compiler_params=ROOM,
        cost_estimate=cost(7.0),
    )(*grads, w_in, unit_low)
    return made, gain, shift


def rotary_tables(places):
    lane = jnp.arange(128, dtype=jnp.int32) % HEAD
    half = ROT // 2
    freqs = jnp.asarray(ROPE_BASE, WIDE) ** (-((lane % half).astype(WIDE) * (2.0 / ROT)))
    angles = places.astype(WIDE)[:, None] * freqs
    turned = (lane < ROT)[None, :]
    sign = jnp.where(lane < half, -1.0, 1.0)
    return jnp.where(turned, jnp.cos(angles), 1.0), jnp.where(turned, jnp.sin(angles) * sign, 0.0)


def unfold_rows(grid, gathered, sizes, block_len, group_seqs):
    zn, yn, ranks = grid.z_count, grid.y_count, grid.rank_count
    cuts = [sum(sizes[:i]) for i in range(len(sizes) + 1)]
    gain_full, shift_full, bias_qkv, bias_dense, bias_up, bias_down = [
        gathered[:, cuts[i] : cuts[i + 1]].reshape(-1).astype(WIDE) for i in range(6)
    ]
    orders = gathered[:: grid.ctx_count, cuts[6] :].reshape(zn, 2, -1).astype(jnp.int32)

    ctx_from = jnp.stack(
        [
            (((grid.y - dy) % yn) * 2 + (grid.x ^ dx)) * 2 + (grid.c ^ dc)
            for dy in range(yn)
            for dx in range(2)
            for dc in range(2)
        ]
    )
    z_from = jnp.stack([(grid.z - 2 * i - grid.parity) % zn for i in range(group_seqs)])
    own_orders = lax.dynamic_index_in_dim(orders, grid.c, 1, keepdims=False)[z_from]
    slots = (ctx_from[:, None] * 2 + jnp.arange(2)).reshape(-1)
    places = own_orders[:, slots].reshape(group_seqs, yn, -1).swapaxes(0, 1)
    places = (places[..., None] * block_len + jnp.arange(block_len)).reshape(-1)
    cosine, sine = rotary_tables(places)


    bias_in = jnp.concatenate(
        [
            lax.dynamic_index_in_dim(bias_qkv.reshape(3, ranks, -1), grid.rank, 1, keepdims=False).reshape(-1),
            place(bias_up.reshape(ranks, -1), grid.rank),
        ]
    )
    column = places.reshape(yn, group_seqs, -1).swapaxes(0, 1).reshape(-1).astype(WIDE)
    return (
        gain_full[None], shift_full[None], bias_in[None], (bias_dense + bias_down)[None], cosine, sine,
        column[:, None], column.reshape(group_seqs, 1, -1),
    )


def fold_rows(grid, gain, shift, sums_qkv, sum_up, cotangent):
    ranks, devices = grid.rank_count, grid.rank_count * 4

    def laid(part, count):
        whole_rows = jnp.zeros((count, ranks, part.shape[-1]), WIDE)
        whole_rows = lax.dynamic_update_index_in_dim(whole_rows, part, grid.rank, 1)
        return whole_rows.reshape(devices, -1)

    return jnp.concatenate(
        [
            gain.reshape(devices, -1),
            shift.reshape(devices, -1),
            laid(jnp.concatenate(sums_qkv, 0), 3),
            jnp.sum(cotangent.astype(WIDE), (0, 1)).reshape(devices, -1),
            laid(sum_up, 1),
        ],
        1,
    )


def on_device(
    tokens, block_order, ln_gain, ln_bias, w_qkv, b_qkv, w_dense, b_dense, w_fc1, b_fc1, w_fc2, b_fc2, cotangent,
):
    grid = Grid()
    seqs, span, model_width = tokens.shape
    zn, yn, ranks = grid.z_count, grid.y_count, grid.rank_count
    device_count = ranks * 4
    length = span * grid.ctx_count
    block_len = span // 2
    group_seqs = zn // 2
    head_width = model_width // ranks

    split = 3 * head_width
    dense_rows = 4 * w_dense.shape[0]
    rows = group_seqs * length // yn
    seq_rows = length // yn
    last = group_seqs - 1

    def ordered(spreads):
        return [spreads[i].parts[dy] for dy in range(yn) for i in range(group_seqs)]

    def ordered(spreads):
        return [spreads[i].parts[dy] for dy in range(yn) for i in range(group_seqs)]

    def rows_of(array, i):
        return array[i * seq_rows : (i + 1) * seq_rows]

    def across_x(ks):
        own = near[ks[0]][None] if len(ks) == 1 else grid.pile(*[near[k][None] for k in ks])
        return ks, own, grid.start(own, x=1)

    def both_columns(group):
        ks, own, moving = group
        return ks, grid.pile(own[None], grid.wait(moving)[None])

    away, own_tokens, own_cotangent = part_cores(grid, tokens, cotangent)
    moving = grid.start(away, c=1)
    down_moving = grid.start(w_fc2, x=1)
    others = grid.wait(moving)
    ring = Ring(grid, grid.pile(own_tokens, others[:span]))
    ring.begin(1)
    ahead, across = cut_columns(grid, *grid.after((w_qkv, w_fc1)))
    across = [grid.start(part, y=dy + 1) for dy, part in enumerate(across)]
    vectors = (ln_gain, ln_bias, b_qkv, b_dense, b_fc1, b_fc2, block_order.reshape(-1))
    sizes = [item.shape[0] for item in vectors]
    vectors = jnp.concatenate([item.astype(WIDE) for item in grid.after(vectors)])
    gather = VectorGather(grid, vectors)
    gather.begin()
    down_moving = grid.wait(down_moving)
    dense_moving = grid.start(w_dense, x=1)
    gather.end()
    ring.end()
    ring.begin(2)
    dense_moving = grid.wait(dense_moving)
    gather.begin()
    spreads = [Spread(grid, ring.pair(0))]
    across = grid.wait(across)
    gather.end()

    def pack(z, y, x, c, ins, outs):
        for k in range(zn):
            outs[k][0] = ins[k][...]
            for dy in range(1, yn):
                outs[k][dy] = ins[zn + dy - 1][k]

    near = grid.local(pack, [*ahead, *across], [low_shape(yn, *ahead[0].shape)] * zn)
    near = dict(enumerate(near))
    near[zn - 1] = grid.start(near[zn - 1], z=-1)
    gather.begin()
    spreads[0].end_x()
    spreads[0].begin_y()
    ring.end()
    rest = [k for k in grid.steps() if k != zn - 1]
    moving = {rest[0]: grid.start(near[rest[0]], z=rest[0])}
    group_own = across_x([0])
    near[zn - 1] = grid.wait(near[zn - 1])
    gather.end()
    ring.finish()
    moving.update({k: grid.start(near[k], z=k) for k in rest[1:]})
    spreads += [Spread(grid, ring.pair(i)) for i in range(1, group_seqs)]
    gather.begin()

    def stack_out(z, y, x, c, ins, outs):
        for at in range(2):
            dense = ins[2 * at].shape[0]
            outs[0][at, :dense] = ins[2 * at][...]
            outs[0][at, dense:] = ins[2 * at + 1][...]

    out_rows = grid.local(
        stack_out,
        grid.after([w_dense, w_fc2, dense_moving, down_moving]),
        [low_shape(2, w_dense.shape[0] + w_fc2.shape[0], model_width)],
    )[0]
    group_own = both_columns(group_own)
    for spread in spreads[1:]:
        spread.end_x()
    spreads[1].begin_y()
    group_far = across_x([zn - 1])
    spreads[0].end_y()
    gather.end()
    near.update(grid.wait(moving))
    group_rest = across_x(rest)
    met_grad = grid.pile(own_cotangent, others[span:])
    ring = Ring(grid, met_grad)
    ring.begin(1)
    group_far = both_columns(group_far)
    gather.begin()

    def beside(z, y, x, c, ins, outs):
        for at, ref in enumerate(ins):
            outs[0][:, at : at + 1] = ref[...]

    first = group_own[0] + group_far[0]
    first_rows = grid.local(beside, [group_own[1], group_far[1]], [low_shape(2, 2, *group_own[1].shape[2:])])[0]
    gather.end()
    while gather.ways:
        gather.step()
    if head_width % 128 == 0:
        unfolded = grid.hold(unfold_vectors(grid, gather, sizes, block_len, group_seqs))
    else:
        unfolded = unfold_rows(grid, gather.result(), sizes, block_len, group_seqs)
    gain_full, shift_full, bias_in, bias_out, cosine, sine, column, row = unfolded
    first_moving = grid.start(first_rows, c=1)
    spreads[1].end_y()
    for spread in spreads[2:]:
        spread.begin_y()
        spread.end_y()
    out_moving = grid.start(out_rows, c=1)
    normed_low, unit_low = grid.hold(normalize(ordered(spreads), gain_full, shift_full))
    first_moving = grid.wait(first_moving)
    group_rest = both_columns(group_rest)
    rest_moving = grid.start(group_rest[1], c=1)
    out_moving = grid.wait(out_moving)
    w_out = grid.hold(join_out(grid, *grid.after((out_rows, out_moving)), w_dense.shape[0]))
    ring.end()
    grads = [Spread(grid, ring.pair(0))]
    ring.begin(2)
    rest_moving = grid.wait(rest_moving)
    w_in = grid.hold(join_columns(grid, [(first, first_rows, first_moving), (*group_rest, rest_moving)]))
    grads[0].end_x()
    grads[0].begin_y()
    grid.page()
    ring.end()
    ring.finish()
    grads += [Spread(grid, ring.pair(i)) for i in range(1, group_seqs)]

    qkv, hidden_low, slope = grid.hold(project(grid.after(normed_low), w_in, bias_in, split))
    grid.pages = False
    for spread in grads[1:]:
        spread.end_x()
    grads[1].begin_y()
    attention_low, kept = grid.hold(attend(grid.after(qkv), cosine, sine, yn, group_seqs, column=column, row=row))
    out_parts = {}
    for dy in range(yn - 1, -1, -1):
        if dy == 0:
            grads[0].end_y()
        out_parts[dy] = grid.hold(out_part(grid.after(attention_low), hidden_low, w_out, dy, rows, group_seqs))
    grads[1].end_y()
    for spread in grads[2:]:
        spread.begin_y()
        spread.end_y()

    out_sums = {i: TokenSum(grid, out_parts[yn - 1][i], yn - 1) for i in range(last, -1, -1)}
    grad_out = grid.pile(*grid.after(ordered(grads)))
    grad_attention_low, grad_up_low = grid.hold(project_back(grad_out, w_out, slope, dense_rows))

    def finish_y(sums, parts, i):
        for dy in range(yn - 2, -1, -1):
            sums[i].more(parts[dy][i])

    grads_qkv = grid.hold(
        attend(grid.after(qkv), cosine, sine, yn, group_seqs, grad_attention=grad_attention_low, kept=kept)
    )
    grads_in = [*grads_qkv, grad_up_low]
    finish_y(out_sums, out_parts, last)
    out_sums[last].begin_x()
    in_parts, gain_parts, shift_parts = {}, {}, {}

    def make_in_part(dy):
        in_parts[dy], gain_parts[dy], shift_parts[dy] = grid.hold(
            in_part(grid.after(grads_in), w_in, unit_low, dy, rows, group_seqs)
        )

    make_in_part(yn - 1)
    in_sums = {last: TokenSum(grid, in_parts[yn - 1][last], yn - 1)}
    out_ring = RingSum(grid)
    out_ring.pieces[2 * last], out_ring.pieces[2 * last + 1] = out_sums[last].end_x()
    for i in range(last - 1, 0, -1):
        finish_y(out_sums, out_parts, i)
        out_sums[i].begin_x()
        out_ring.pieces[2 * i], out_ring.pieces[2 * i + 1] = out_sums[i].end_x()
    out_ring.begin_far()
    finish_y(out_sums, out_parts, 0)
    out_sums[0].begin_x()
    for dy in range(yn - 2, -1, -1):
        make_in_part(dy)
    up_kept, up_away, (sum_up,) = grid.hold(halves_in(grid, grid.after(normed_low), [grad_up_low]))
    up_moving = grid.start(up_away, c=1)
    out_ring.pieces[0], out_ring.pieces[1] = out_sums[0].end_x()
    out_ring.end_far()
    out_ring.begin_near()
    finish_y(in_sums, in_parts, last)
    for i in range(last - 1, -1, -1):
        in_sums[i] = TokenSum(grid, in_parts[yn - 1][i], yn - 1)
    in_sums[last].begin_x()
    grid.turn()
    up_kept, up_away = grid.hold(halve_columns(grid, up_kept, grid.wait(up_moving)))
    up_moving = grid.start(up_away, x=1)
    qkv_kept, qkv_away, sums_qkv = grid.hold(halves_in(grid, grid.after(normed_low), grads_qkv))
    qkv_moving = grid.start(qkv_away, c=1)
    out_ring.end_near()
    if head_width % 128 == 0:
        sums = fold_vectors(
            grid, list(gain_parts.values()), list(shift_parts.values()), sums_qkv, sum_up, cotangent, sizes
        )
    else:
        sums = fold_rows(
            grid, sum(gain_parts.values()), sum(shift_parts.values()), sums_qkv, sum_up, cotangent
        )
    sums = VectorSum(grid, grid.hold(sums))
    sums.begin()
    in_ring = RingSum(grid)
    in_ring.pieces[2 * last], in_ring.pieces[2 * last + 1] = in_sums[last].end_x()
    for i in range(last - 1, 0, -1):
        finish_y(in_sums, in_parts, i)
        in_sums[i].begin_x()
        in_ring.pieces[2 * i], in_ring.pieces[2 * i + 1] = in_sums[i].end_x()
    sums.end()
    in_ring.begin_far()
    sums.begin()
    out_kept, out_away = grid.hold(halves_out(grid, *grid.after((attention_low, hidden_low)), grad_out))
    finish_y(in_sums, in_parts, 0)
    in_sums[0].begin_x()
    sums.end()
    up_return = ColumnReturn(grid, up_kept, grid.wait(up_moving))
    up_return.begin_z()
    in_ring.end_far()
    sums.begin()
    out_moving = grid.start(out_away, c=1)
    grid.turn()
    projected = out_ring.end()
    qkv_moving = grid.wait(qkv_moving)
    sums.end()
    qkv_kept, qkv_away = grid.hold(halve_columns(grid, qkv_kept, qkv_moving))
    qkv_moving = grid.start(qkv_away, x=1)
    in_ring.pieces[0], in_ring.pieces[1] = in_sums[0].end_x()
    up_return.end_z()
    in_ring.begin_near()
    qkv_return = ColumnReturn(grid, qkv_kept, grid.wait(qkv_moving))
    qkv_return.begin_z()
    out_kept, out_away = grid.hold(halve_columns(grid, out_kept, grid.wait(out_moving)))
    out_moving = grid.start(out_away, x=1)
    in_ring.end_near()
    qkv_return.end_z()
    qkv_return.begin_y()
    up_return.begin_y()
    grad_normed = in_ring.end()
    sums.begin()
    token_grad = grid.hold(finish_grad(grid, tokens, cotangent, *grad_normed, gain_full))
    output = grid.hold(finish_output(grid, grid.after(tokens), *projected, bias_out))
    sums.end()
    sums.begin()
    out_moving = grid.wait(out_moving)
    qkv_found = qkv_return.end()
    up_found = up_return.end()
    grad_w_up = grid.hold(lay_columns(grid, up_found, 1))
    sums.end()
    sums = sums.result()
    grad_w_out = (out_kept.astype(WIDE) + out_moving.astype(WIDE))[0]

    grad_w_qkv = lay_columns(grid, qkv_found, 3)

    grad_gain, grad_shift = sums[: sizes[0]], sums[sizes[0] : 2 * sizes[0]]
    rest = sums[2 * sizes[0] :]
    grad_bias_qkv = rest[: sizes[2]]
    grad_bias_out = rest[sizes[2] : sizes[2] + sizes[3]]
    grad_bias_up = rest[sizes[2] + sizes[3] :]
    grad_w_dense = grad_w_out[: w_dense.shape[0]]
    grad_w_down = grad_w_out[w_dense.shape[0] :]
    return (
        output, token_grad, grad_gain, grad_shift, grad_w_qkv, grad_bias_qkv,
        grad_w_dense, grad_bias_out, grad_w_up, grad_bias_up, grad_w_down, grad_bias_out,
    )


def solution(mesh):
    rows = P(("dp", "ctx"), None)
    vector = P(("dp", "ctx"))
    spread = P("dp", "ctx", None)
    in_specs = (
        spread, P("dp", None), vector, vector, rows, vector, rows, vector, rows, vector, rows, vector, spread,
    )
    out_specs = (
        spread, spread, vector, vector, rows, vector, rows, vector, rows, vector, rows, vector,
    )
    return jax.shard_map(on_device, mesh=mesh, in_specs=in_specs, out_specs=out_specs, check_vma=False)
```
